32 devices in a mesh: seq: 8 (over z, x), fsdp: 4 (over y, core).
Axes of the slice: x: 2, y: 2, z: 4, core: 2. Of those that a mesh axis runs over, the one named last changes fastest.
Arguments:
- hidden: bfloat16 [4, 1024, 1024], P('fsdp', 'seq'), may hold values from -6 to 6
- cluster_lengths: int32 [4, 8], P('fsdp'), may hold values from 1 to 1024, as said below
- norm_gain: bfloat16 [1024], P('fsdp'), may hold values from 0.5 to 1.5
- in_weight: bfloat16 [1024, 4096], P('fsdp'), may hold values from -0.1875 to 0.1875
- conv_weight: bfloat16 [2048, 4], P('fsdp'), may hold values from -3 to 3
- conv_bias: bfloat16 [2048], P('fsdp'), may hold values from -0.5 to 0.5
- xproj_weight: bfloat16 [2048, 96], P('fsdp'), may hold values from -0.125 to 0.125
- dt_weight: bfloat16 [2048, 64], P('fsdp'), may hold values from -0.75 to 0.75
- dt_bias: bfloat16 [2048], P('fsdp'), may hold values from -1 to 0.5
- a_log: bfloat16 [2048, 16], P('fsdp'), may hold values from -3.5 to 0.5
- skip: bfloat16 [2048], P('fsdp'), may hold values from 0.5 to 1.5
- out_weight: bfloat16 [2048, 1024], P('fsdp'), may hold values from -0.125 to 0.125
- cotangent: bfloat16 [4, 1024, 1024], P('fsdp', 'seq'), may hold values from -6 to 6
Outputs:
- output: bfloat16 [4, 1024, 1024], P('fsdp', 'seq')
- grad_hidden: float32 [4, 1024, 1024], P('fsdp', 'seq')
- grad_norm_gain: float32 [1024], P(('seq', 'fsdp'))
- grad_in_weight: float32 [1024, 4096], P(('seq', 'fsdp'))
- grad_conv_weight: float32 [2048, 4], P(('seq', 'fsdp'))
- grad_conv_bias: float32 [2048], P(('seq', 'fsdp'))
- grad_xproj_weight: float32 [2048, 96], P(('seq', 'fsdp'))
- grad_dt_weight: float32 [2048, 64], P(('seq', 'fsdp'))
- grad_dt_bias: float32 [2048], P(('seq', 'fsdp'))
- grad_a_log: float32 [2048, 16], P(('seq', 'fsdp'))
- grad_skip: float32 [2048], P(('seq', 'fsdp'))
- grad_out_weight: float32 [2048, 1024], P(('seq', 'fsdp'))
The draws below stay inside these ranges and needn't reach their ends.
Inputs may be any that keep to these rules, and one draw needn't show every extreme that they name: `cluster_lengths`: each row gives the 8 cluster lengths of one stream in order, summing to 1024; in every row one cluster, neither the first nor the last, starts within the first 128 tokens and ends within the last 128 tokens.
All inputs are finite; a program needn't handle non-finite values.
Results may differ from the reference program's by a relative error of at most 0.012.
Values may be sent and summed in bfloat16 or wider, within the bound.
A program may use at most 192 MiB of HBM per device.

```python
import jax
import jax.numpy as jnp
from jax import lax

D = 1024
DI = 2048
N = 16
R = 64
K = 4
TOK_DEV = 128
BLOCK = 64
CLUSTERS = 8
STREAMS = 4
LEN = 1024


def draw_cluster_lengths(key, part):
    key = jax.random.fold_in(key, 11)
    key_short, key_place = jax.random.split(key)
    longest_short = TOK_DEV // (CLUSTERS - 1)
    shorts = jax.random.randint(key_short, (STREAMS, CLUSTERS - 1), 1, longest_short + 1)
    place = jax.random.randint(key_place, (STREAMS, 1), 1, CLUSTERS - 1)
    long_len = LEN - jnp.sum(shorts, axis=1, keepdims=True)
    column = jnp.arange(CLUSTERS)[None, :]
    before = jnp.concatenate([shorts, shorts[:, -1:]], axis=1)
    after = jnp.concatenate([shorts[:, :1], shorts], axis=1)
    chosen = jnp.where(column < place, before, jnp.where(column == place, long_len, after))
    return chosen.astype(jnp.int32)


def block_scale(key, extent, cuts, smallest, top_value):
    loudness = 1.0
    for position, blocks in cuts:
        steps = jax.random.uniform(jax.random.fold_in(jax.random.fold_in(key, 6), position), (blocks,), jnp.float32, smallest / len(cuts), top_value / len(cuts))
        loudness = loudness * jnp.repeat(jnp.exp(steps), extent[position] // blocks).reshape((-1,) + (1,) * (len(extent) - 1 - position))
    return loudness


def normal_values(own_key, dims, spread, limit, cuts=(), held_as=jnp.bfloat16):
    array = jax.random.normal(own_key, dims, jnp.float32) * spread
    if len(cuts) > 0:
        array = block_scale(own_key, dims, cuts, -0.22, 0.18) * array
    return jnp.clip(array, min=-limit, max=limit).astype(held_as)


def setup_inputs(seed: int = 0) -> dict:
    key_list = jax.random.split(jax.random.key(seed), 14)
    hidden = normal_values(key_list[0], (STREAMS, LEN, D), 1.0, 6.0, ((0, 4), (1, 8)))
    cluster_lengths = draw_cluster_lengths(jax.random.fold_in(key_list[13], 71), 0)
    norm_gain = jnp.clip(1.0 + 0.1 * jax.random.normal(key_list[2], (D,), jnp.float32), 0.5, 1.5).astype(jnp.bfloat16)
    in_weight = normal_values(key_list[3], (D, 2 * DI), D ** -0.5, 0.1875, ((0, 4),))
    conv_weight = normal_values(key_list[4], (DI, K), K ** -0.5, 3.0, ((0, 4),))
    conv_bias = jnp.clip(jax.random.uniform(key_list[5], (DI,), jnp.float32, -0.5, 0.5) * block_scale(key_list[5], (DI,), ((0, 4),), -0.4, 0.0), -0.5, 0.5).astype(jnp.bfloat16)
    xproj_weight = normal_values(key_list[6], (DI, R + 2 * N), DI ** -0.5, 0.125, ((0, 4),))
    dt_weight = normal_values(key_list[7], (DI, R), R ** -0.5, 0.75, ((0, 4),))
    dt_bias = jnp.clip(-1.0 + 1.5 * jax.random.uniform(key_list[8], (DI,), jnp.float32) ** block_scale(key_list[8], (DI,), ((0, 4),), -0.2, 0.2), -1.0, 0.5).astype(jnp.bfloat16)
    a_log = jnp.clip(-3.5 + 4.0 * jax.random.uniform(key_list[9], (DI, N), jnp.float32) ** block_scale(key_list[9], (DI, N), ((0, 4),), -0.2, 0.2), -3.5, 0.5).astype(jnp.bfloat16)
    skip = jnp.clip(0.5 + 1.0 * jax.random.uniform(key_list[10], (DI,), jnp.float32) ** block_scale(key_list[10], (DI,), ((0, 4),), -0.2, 0.2), 0.5, 1.5).astype(jnp.bfloat16)
    out_weight = normal_values(key_list[11], (DI, D), DI ** -0.5, 0.125, ((0, 4),))
    cotangent = normal_values(key_list[12], (STREAMS, LEN, D), 1.0, 6.0, ((0, 4), (1, 8)))
    return {"hidden": hidden, "cluster_lengths": cluster_lengths, "norm_gain": norm_gain, "in_weight": in_weight, "conv_weight": conv_weight, "conv_bias": conv_bias, "xproj_weight": xproj_weight, "dt_weight": dt_weight, "dt_bias": dt_bias, "a_log": a_log, "skip": skip, "out_weight": out_weight, "cotangent": cotangent}


EPS = 1e-05
HIGHEST = lax.Precision.HIGHEST

@jax.custom_vjp
def low(v):
    return lax.optimization_barrier(v.astype(jnp.bfloat16)).astype(jnp.float32)

@jax.custom_vjp
def low_back(v):
    return v

def low_keep(v):
    return (low(v), None)

def low_pass(kept, grad):
    return (grad,)

def back_keep(v):
    return (v, None)

def back_low(kept, grad):
    return (low(grad),)
low.defvjp(low_keep, low_pass)
low_back.defvjp(back_keep, back_low)

def selective_scan(step_sizes, b_proj, c_proj, inputs, decay_rates, keep_mask):
    blocks = step_sizes.shape[0] // BLOCK

    def token_step(carried, token):
        size_row, b_row, c_row, input_row, keep_row = token
        factor = jnp.exp(size_row[None, :] * decay_rates) * keep_row
        carried = factor * carried + b_row[:, None] * (size_row * input_row)[None, :]
        return (carried, lax.optimization_barrier(jnp.sum(c_row[:, None] * carried, axis=0)))

    def block_step(carried, block_items):
        return lax.scan(token_step, carried, block_items)
    items = tuple((member.reshape((blocks, BLOCK) + member.shape[1:]) for member in (step_sizes, b_proj, c_proj, inputs, keep_mask)))
    _, outputs = lax.scan(jax.checkpoint(block_step), jnp.zeros_like(decay_rates), items)
    return outputs.reshape(step_sizes.shape)

def stream_forward(stream, lengths, weights):
    norm_gain, in_weight, conv_weight, conv_bias, xproj_weight, dt_weight, dt_bias, a_log, skip, out_weight = weights
    inner_width = out_weight.shape[0]
    dt_rank = dt_weight.shape[1]
    state_size = a_log.shape[1]
    conv_taps = conv_weight.shape[1]
    total = stream.shape[0]
    inv_rms = lax.rsqrt(lax.optimization_barrier(jnp.mean(stream * stream, axis=-1, keepdims=True)) + EPS)
    normed = low(stream * inv_rms * norm_gain)
    projected = low_back(jnp.dot(normed, in_weight, precision=HIGHEST))
    x_branch = low(projected[:, :inner_width])
    gate_pre = projected[:, inner_width:]
    offsets = jnp.cumsum(lengths).astype(jnp.int32)[:-1]
    positions = jnp.arange(total, dtype=jnp.int32)
    cluster_ids = lax.optimization_barrier(jnp.sum((positions[:, None] >= offsets[None, :]).astype(jnp.int32), axis=1)).astype(jnp.int32)
    starts = jnp.any(positions[:, None] == offsets[None, :], axis=1)
    keep_mask = 1.0 - starts.astype(jnp.float32)
    padded = jnp.concatenate([jnp.zeros((conv_taps - 1, inner_width), jnp.float32), x_branch], axis=0)
    pad_ids = jnp.concatenate([jnp.full((conv_taps - 1,), -1, jnp.int32), cluster_ids]).astype(jnp.int32)
    pre_act = jnp.zeros((total, inner_width), jnp.float32) + conv_bias
    for tap_index in range(conv_taps):
        same = (pad_ids[tap_index:tap_index + total] == cluster_ids).astype(jnp.float32)[:, None]
        pre_act = pre_act + conv_weight[:, tap_index] * padded[tap_index:tap_index + total] * same
    inputs = low(jax.nn.silu(pre_act))
    x_dbl = low_back(jnp.dot(inputs, xproj_weight, precision=HIGHEST))
    dt_low = low(x_dbl[:, :dt_rank])
    b_proj = x_dbl[:, dt_rank:dt_rank + state_size]
    c_proj = x_dbl[:, dt_rank + state_size:]
    step_sizes = jax.nn.softplus(low_back(jnp.dot(dt_low, dt_weight.T, precision=HIGHEST)) + dt_bias)
    decay_rates = -jnp.exp(a_log.T)
    scanned = selective_scan(step_sizes, b_proj, c_proj, inputs, decay_rates, keep_mask)
    mixed = scanned + skip * inputs
    gated = low(mixed * jax.nn.silu(gate_pre))
    return stream + jnp.dot(gated, out_weight, precision=HIGHEST)

def reference(hidden, cluster_lengths, norm_gain, in_weight, conv_weight, conv_bias, xproj_weight, dt_weight, dt_bias, a_log, skip, out_weight, cotangent):
    params = tuple((member.astype(jnp.float32) for member in (norm_gain, in_weight, conv_weight, conv_bias, xproj_weight, dt_weight, dt_bias, a_log, skip, out_weight)))

    def forward(stream_all, *weights):
        one_stream = jax.checkpoint(lambda stream, lengths: stream_forward(stream, lengths, weights))
        return lax.map(lambda stream_pair: one_stream(stream_pair[0], stream_pair[1]), (stream_all, cluster_lengths))
    result, pullback = jax.vjp(forward, hidden.astype(jnp.float32), *params)
    gradients = pullback(cotangent.astype(jnp.float32))
    return (result.astype(jnp.bfloat16), gradients[0], gradients[1], gradients[2], gradients[3], gradients[4], gradients[5], gradients[6], gradients[7], gradients[8], gradients[9], gradients[10])
```

```python
import functools
import math

import jax
import jax.numpy as jnp
from jax import lax
from jax.experimental import pallas as pl
from jax.experimental.pallas import tpu as pltpu
from jax.sharding import PartitionSpec as P

EPS = 1e-05
V = 8
LN = 128
HG = 4
TAIL = 16
LOG2E = 1.0 / math.log(2.0)
RESET = 1e30
F32 = jnp.float32
TOP, BOT = slice(0, V), slice(V, 2 * V)
BF16 = jnp.bfloat16
MESH = pl.DeviceIdType.MESH


class Dims:
    def __init__(self, S, F, tok, D, DI, N, R, K):
        self.S, self.F, self.tok, self.D, self.DI = S, F, tok, D, DI
        self.N, self.R, self.K = N, R, K
        self.H = V // F
        self.Q = tok // self.H
        self.T = F * tok
        self.TE = (self.Q + HG) * V
        self.NAT = F * (tok + TAIL)
        self.CL = DI // F
        self.NB = self.CL // LN


def dot(a, b, ca=1, cb=0):
    return lax.dot_general(a, b, (((ca,), (cb,)), ((), ())), preferred_element_type=F32)


def sigmoid(v):
    return 1.0 / (1.0 + jnp.exp(-v))


def exchange(d, items, cid):
    S, F = d.S, d.F
    n = len(items)
    greet = sorted({(ds % S, df % F) for it in items for ds, df, _, _ in it["sends"]} - {(0, 0)})
    total = sum(len(it["sends"]) for it in items)

    def kern(*refs):
        ins, outs, (ssem, rsem) = refs[:n], refs[n : 2 * n], refs[2 * n :]
        ms, mf = lax.axis_index("seq"), lax.axis_index("fsdp")
        bar = pltpu.get_barrier_semaphore()
        for ds, df in greet:
            to = {"seq": lax.rem(ms + (S - ds), S), "fsdp": lax.rem(mf + (F - df), F)}
            pl.semaphore_signal(bar, inc=1, device_id=to, device_id_type=MESH)
        pl.semaphore_wait(bar, len(greet))
        copies = []
        for it, src, dst in zip(items, ins, outs):
            for ds, df, take, put in it["sends"]:
                ps, pf = lax.rem(ms + ds % S, S), lax.rem(mf + df, F)
                i = len(copies)
                a, b = take(src, ms, mf, ps, pf), put(dst, ms, mf)
                if ds % S == 0 and df % F == 0:
                    c = pltpu.make_async_copy(a, b, rsem.at[i])
                else:
                    c = pltpu.make_async_remote_copy(
                        a, b, ssem.at[i], rsem.at[i], {"seq": ps, "fsdp": pf}, device_id_type=MESH
                    )
                c.start()
                copies.append(c)
        for c in copies:
            c.wait()

    return pl.pallas_call(
        kern,
        out_shape=[jax.ShapeDtypeStruct(it["shape"], it["src"].dtype) for it in items],
        in_specs=[pl.BlockSpec(memory_space=pl.ANY)] * n,
        out_specs=[pl.BlockSpec(memory_space=pl.ANY)] * n,
        scratch_shapes=[pltpu.SemaphoreType.DMA((total,)), pltpu.SemaphoreType.DMA((total,))],
        compiler_params=pltpu.CompilerParams(collective_id=cid, has_side_effects=True),
    )(*[it["src"] for it in items])


def gather_f(d, x):
    return dict(
        src=x,
        shape=(d.F,) + x.shape,
        sends=[(0, k, lambda r, ms, mf, ps, pf: r, lambda r, ms, mf: r.at[mf]) for k in range(d.F)],
    )


def swap_f(d, x):
    return dict(
        src=x,
        shape=x.shape,
        sends=[
            (0, k, lambda r, ms, mf, ps, pf: r.at[pf], lambda r, ms, mf: r.at[mf])
            for k in range(d.F)
        ],
    )


def swap_s(d, x):
    return dict(
        src=x,
        shape=x.shape,
        sends=[
            (k, 0, lambda r, ms, mf, ps, pf: r.at[ps], lambda r, ms, mf: r.at[ms])
            for k in range(d.S)
        ],
    )


def kernel(body, args, outs, scratch=()):
    return pl.pallas_call(
        body,
        out_shape=[jax.ShapeDtypeStruct(s, t) for s, t in outs],
        in_specs=[pl.BlockSpec(memory_space=pltpu.VMEM)] * len(args),
        out_specs=[pl.BlockSpec(memory_space=pltpu.VMEM)] * len(outs),
        scratch_shapes=list(scratch),
        compiler_params=pltpu.CompilerParams(vmem_limit_bytes=60 * 1024 * 1024),
    )(*args)


def lane(j):
    return slice(j * LN, (j + 1) * LN)


def natural_of(d, row, halo):
    q = lax.div(row, V) - halo
    v = lax.rem(row, V)
    f = lax.div(v, d.H)
    p = lax.rem(v, d.H) * d.Q + q
    return jnp.where(p >= 0, f * d.tok + p, d.T + f * TAIL + TAIL + p)


def to_scan(d, halo):
    rows, cols = (d.TE, d.NAT) if halo else (d.T, d.T)
    want = natural_of(d, lax.broadcasted_iota(jnp.int32, (rows, 1), 0), halo)
    have = lax.broadcasted_iota(jnp.int32, (rows, cols), 1)
    return jnp.where(have == want, 1.0, 0.0).astype(BF16)


def from_scan(d, halo):
    rows, cols = (d.NAT, d.TE) if halo else (d.T, d.T)
    want = natural_of(d, lax.broadcasted_iota(jnp.int32, (1, cols), 1), halo)
    have = lax.broadcasted_iota(jnp.int32, (rows, cols), 0)
    return jnp.where(have == want, 1.0, 0.0).astype(BF16)


def front(d, hid, gain, w, cp, xp, lens, normed, xb, gate, pre, inp, rel, xd, scan_s):
    CL = d.CL

    def rms(i, _):
        rows = pl.ds(pl.multiple_of(i * 64, 64), 64)
        h = hid[rows, :].astype(F32)
        inv = lax.rsqrt(jnp.mean(h * h, axis=-1, keepdims=True) + EPS)
        normed[rows, :] = (h * inv * gain[...]).astype(BF16)
        return 0

    lax.fori_loop(0, d.NAT // 64, rms, 0)
    perm = to_scan(d, HG)
    for c in range(0, d.D, 256):
        scan_s[:, c : c + 256] = dot(perm, normed[:, c : c + 256]).astype(BF16)
    for c in range(0, CL, 256):
        xb[:, c : c + 256] = dot(scan_s[...], w[0, :, c : c + 256]).astype(BF16).astype(F32)
        gate[:, c : c + 256] = dot(scan_s[HG * V :, :], w[1, :, c : c + 256])
    sub = lax.broadcasted_iota(jnp.int32, (V, LN), 0)
    stream = lax.div(sub, d.H)
    offs, run = [], jnp.zeros((V, LN), jnp.int32)
    for j in range(lens.shape[1] - 1):
        for f in range(d.F):
            run = run + jnp.where(stream == f, lens[f, j : j + 1, :], 0)
        offs.append(run)
    rel[0 : HG * V, :] = jnp.zeros((HG * V, LN), F32)
    rel[HG * V + d.T :, :] = jnp.zeros((HG * V, LN), F32)
    base = lax.axis_index("seq") * d.tok + lax.rem(sub, d.H) * d.Q

    def mark(q, _):
        pos = base + q
        last = jnp.zeros((V, LN), jnp.int32)
        for o in offs:
            last = jnp.maximum(last, jnp.where(o <= pos, o, 0))
        rel[pl.ds(pl.multiple_of((q + HG) * V, V), V), :] = jnp.where(
            pos == 0, 0.5, (pos - last).astype(F32)
        )
        return 0

    lax.fori_loop(0, d.Q, mark, 0)

    def conv(i, _):
        r0 = pl.multiple_of(i * 64, 64)
        rows = pl.ds(r0, 64)
        age = rel[pl.ds(pl.multiple_of(r0 + HG * V, V), 64), :]
        for j in range(d.NB):
            acc = jnp.zeros((64, LN), F32) + cp[4:5, lane(j)]
            for k in range(d.K):
                back = d.K - 1 - k
                xs = xb[pl.ds(pl.multiple_of(r0 + (HG - back) * V, V), 64), lane(j)]
                acc = acc + jnp.where(age >= back, xs * cp[k : k + 1, lane(j)], 0.0)
            pre[rows, lane(j)] = acc
            inp[rows, lane(j)] = (acc * sigmoid(acc)).astype(BF16)
        return 0

    lax.fori_loop(0, d.T // 64, conv, 0)
    xd[...] = dot(inp[...], xp[...])


def steps_and_local(
    d, xdp, wdt, cp, gate, inp, rel, cot, ow, dec2,
    lows, dtpre, dtd, u, bcb, gg, gy, cots, ends, e_out, sd_out,
):
    CL, T, R, N = d.CL, d.T, d.R, d.N
    xd = xdp[0]
    for f in range(1, d.F):
        xd = xd + xdp[f]
    low = xd[:, :R].astype(BF16)
    lows[...] = low
    bc = xd[:, R : R + 2 * N]
    hi = bc.astype(BF16)
    rest = (bc - hi.astype(F32)).astype(BF16)
    both = jnp.concatenate([hi, rest], axis=1)
    for n in range(0, 2 * N, 4):
        row = lax.rem(lax.broadcasted_iota(jnp.int32, (4 * N, 4 * LN), 0), 2 * N)
        col = lax.div(lax.broadcasted_iota(jnp.int32, (4 * N, 4 * LN), 1), LN) + n
        spread = jnp.where(row == col, 1.0, 0.0).astype(BF16)
        bcb[:, n * LN : (n + 4) * LN] = dot(both, spread).astype(bcb.dtype)
    perm = to_scan(d, 0)
    for c in range(0, d.D, 256):
        cots[:, c : c + 256] = dot(perm, cot[:, c : c + 256]).astype(BF16)
    for c in range(0, CL, 256):
        dtpre[:, c : c + 256] = dot(low, wdt[c : c + 256, :], 1, 1)
        gg[:, c : c + 256] = dot(cots[...], ow[c : c + 256, :], 1, 1)

    def steps(i, _):
        rows = pl.ds(pl.multiple_of(i * 64, 64), 64)
        age = rel[pl.ds(pl.multiple_of(i * 64 + HG * V, V), 64), :]
        for j in range(d.NB):
            z = dtpre[rows, lane(j)] + cp[5:6, lane(j)]
            dt = jnp.maximum(z, 0.0) + jnp.log1p(jnp.exp(-jnp.abs(z)))
            dtpre[rows, lane(j)] = z
            dtd[rows, lane(j)] = jnp.where(age == 0.0, RESET, dt)
            u[rows, lane(j)] = dt * inp[rows, lane(j)].astype(F32)
            g = gate[rows, lane(j)]
            gy[rows, lane(j)] = gg[rows, lane(j)] * (g * sigmoid(g))
        return 0

    lax.fori_loop(0, T // 64, steps, 0)
    half = N // 2
    for j in range(d.NB):
        for n0 in range(0, N, half):
            dn = [
                jnp.broadcast_to(dec2[n : n + 1, lane(j)], (V, LN)) for n in range(n0, n0 + half)
            ]

            def local(q, carry, n0=n0, j=j, dn=dn):
                hs, gs = list(carry[0]), list(carry[1])
                up = pl.ds(pl.multiple_of(q * 2 * V, 2 * V), 2 * V)
                down = pl.ds(pl.multiple_of((d.Q - 2 - 2 * q) * V, 2 * V), 2 * V)
                a_dt, a_u = dtd[up, lane(j)], u[up, lane(j)]
                b_dt, b_gy = dtd[down, lane(j)], gy[down, lane(j)]
                for i in range(half):
                    b = bcb[up, lane(n0 + i)].astype(F32)
                    c = bcb[down, lane(N + n0 + i)].astype(F32)
                    for t in (TOP, BOT):
                        hs[i] = jnp.exp2(a_dt[t] * dn[i]) * hs[i] + a_u[t] * b[t]
                    for t in (BOT, TOP):
                        gs[i] = jnp.exp2(b_dt[t] * dn[i]) * (gs[i] + b_gy[t] * c[t])
                return tuple(hs), tuple(gs)

            zero = tuple(jnp.zeros((V, LN), F32) for _ in range(half))
            hs, gs = lax.fori_loop(0, d.Q // 2, local, (zero, zero))
            for i in range(half):
                ends[0, (n0 + i) * V : (n0 + i + 1) * V, lane(j)] = hs[i]
                ends[1, (n0 + i) * V : (n0 + i + 1) * V, lane(j)] = gs[i]
        def add(q, s, j=j):
            return s + dtd[pl.ds(pl.multiple_of(q * V, V), V), lane(j)]

        own = lax.fori_loop(0, d.Q, add, jnp.zeros((V, LN), F32))
        hidx = lax.rem(lax.broadcasted_iota(jnp.int32, (V, LN), 0), d.H)
        whole, t = own, 1
        while t < d.H:
            low_half = lax.rem(lax.div(hidx, t), 2) == 0
            whole = whole + jnp.where(low_half, pltpu.roll(whole, V - t, 0), pltpu.roll(whole, t, 0))
            t *= 2
        sd_out[0:V, lane(j)] = own
        sd_out[V : 2 * V, lane(j)] = whole
        for n in range(0, N, 2):
            fw, bw = [], []
            for m in (n, n + 1):
                fac = jnp.exp2(own * dec2[m : m + 1, lane(j)])
                e = ends[0, m * V : (m + 1) * V, lane(j)]
                g = ends[1, m * V : (m + 1) * V, lane(j)]
                x, y = e, g
                for t in range(1, d.H):
                    x = jnp.where(hidx == t, fac * pltpu.roll(x, 1, 0) + e, x)
                    y = jnp.where(hidx == d.H - 1 - t, fac * pltpu.roll(y, V - 1, 0) + g, y)
                fw.append(x)
                bw.append(y)
            e_out[0, n * V : (n + 2) * V, lane(j)] = jnp.concatenate(fw, axis=0).astype(BF16)
            e_out[1, n * V : (n + 2) * V, lane(j)] = jnp.concatenate(bw, axis=0).astype(BF16)


def scan_both(
    d, epieces, sdall, ends, sd, dec2, dtpre, dtd, u, inp, bcb, gg, gy, gate, cp, cots, ow, normed, wdt, lows,
    outp, gow, giwg, gpl, gsc, gx, gdec, gwdt, gskip,
    m_s, y_s, start, x_s, gated, ggate, gated_n, ggate_n,
):
    CL, T, N, Q, NB = d.CL, d.T, d.N, d.Q, d.NB
    ms = lax.axis_index("seq")
    hidx = lax.rem(lax.broadcasted_iota(jnp.int32, (V, LN), 0), d.H)
    for j in range(NB):
        own = sd[0:V, lane(j)]
        for n0 in range(0, N, 2):
            dn = [jnp.broadcast_to(dec2[n0 + i : n0 + i + 1, lane(j)], (V, LN)) for i in (0, 1)]
            band = pl.ds(n0 * V, 2 * V)

            def join(p, acc, j=j, dn=dn, band=band):
                tot = sdall[p, :, lane(j)]
                e = epieces[p, band, lane(j)].astype(F32)
                return tuple(jnp.exp2(tot * dn[i]) * acc[i] + e[i * V : (i + 1) * V] for i in (0, 1))

            zero = (jnp.zeros((V, LN), F32),) * 2
            fw = lax.fori_loop(0, ms, join, zero)
            bw = lax.fori_loop(
                0, d.S - 1 - ms, lambda i, acc: join(d.S - 1 - i, acc), zero
            )
            for i in (0, 1):
                n = n0 + i
                rows = slice(n * V, (n + 1) * V)
                fac = jnp.exp2(own * dn[i])
                x = fw[i] if d.H == 1 else pltpu.roll(fw[i], V - (d.H - 1), 0)
                y = bw[i] if d.H == 1 else pltpu.roll(bw[i], d.H - 1, 0)
                for t in range(1, d.H):
                    xn = pltpu.roll(fac * x + ends[0, rows, lane(j)], 1, 0)
                    yn = pltpu.roll(fac * y + ends[1, rows, lane(j)], V - 1, 0)
                    x = jnp.where(hidx == t, xn, x)
                    y = jnp.where(hidx == d.H - 1 - t, yn, y)
                start[0, rows, lane(j)] = x
                start[1, rows, lane(j)] = y
    for j in range(NB):
        dn = [jnp.broadcast_to(dec2[n : n + 1, lane(j)], (V, LN)) for n in range(N)]

        def ahead(q, hs, j=j, dn=dn):
            hs = list(hs)
            rows = pl.ds(pl.multiple_of(q * 2 * V, 2 * V), 2 * V)
            t, w = dtd[rows, lane(j)], u[rows, lane(j)]
            y = [jnp.zeros((V, LN), F32), jnp.zeros((V, LN), F32)]
            for n in range(N):
                b = bcb[rows, lane(n)].astype(F32)
                c = bcb[rows, lane(N + n)].astype(F32)
                ms = []
                for k, p in enumerate((TOP, BOT)):
                    m = jnp.exp2(t[p] * dn[n]) * hs[n]
                    hs[n] = m + w[p] * b[p]
                    y[k] = y[k] + c[p] * hs[n]
                    ms.append(m)
                m_s[j, rows, lane(n)] = jnp.concatenate(ms, axis=0).astype(m_s.dtype)
            y_s[rows, lane(j)] = jnp.concatenate(y, axis=0)
            return tuple(hs)

        lax.fori_loop(0, Q // 2, ahead, tuple(start[0, n * V : (n + 1) * V, lane(j)] for n in range(N)))

    def gating(i, sk):
        rows = pl.ds(pl.multiple_of(i * 64, 64), 64)
        out = []
        for j in range(NB):
            x = inp[rows, lane(j)].astype(F32)
            mixed = y_s[rows, lane(j)] + cp[6:7, lane(j)] * x
            g = gate[rows, lane(j)]
            s = sigmoid(g)
            gated[rows, lane(j)] = (mixed * (g * s)).astype(BF16)
            ggate[rows, lane(j)] = (
                gg[rows, lane(j)] * mixed * s * (1.0 + g * (1.0 - s))
            ).astype(BF16)
            p = gy[rows, lane(j)] * x
            out.append(sk[j] + jnp.sum(p.reshape(8, V, LN), axis=0))
        return tuple(out)

    sk = lax.fori_loop(0, T // 64, gating, tuple(jnp.zeros((V, LN), F32) for _ in range(NB)))
    gskip[...] = jnp.zeros_like(gskip)
    for j in range(NB):
        gskip[0:1, lane(j)] = jnp.sum(sk[j], axis=0, keepdims=True)
    back = from_scan(d, 0)
    gated_n[...] = dot(back, gated[...]).astype(BF16)
    ggate_n[...] = dot(back, ggate[...]).astype(BF16)
    for c in range(0, d.D, 256):
        outp[:, c : c + 256] = dot(gated_n[...], ow[:, c : c + 256]).astype(BF16)
        gow[:, c : c + 256] = dot(gated[...], cots[:, c : c + 256], 0, 0).astype(BF16)
    for c in range(0, CL, 256):
        giwg[:, c : c + 256] = dot(normed[0:T, :], ggate_n[:, c : c + 256], 0, 0).astype(BF16)
    half = N // 2
    for j in range(NB):
        for n0 in range(0, N, half):
            dn = [
                jnp.broadcast_to(dec2[n : n + 1, lane(j)], (V, LN)) for n in range(n0, n0 + half)
            ]

            def behind(i, carry, n0=n0, j=j, dn=dn):
                gs, gd = list(carry[0]), list(carry[1])
                rows = pl.ds(pl.multiple_of((Q - 2 - 2 * i) * V, 2 * V), 2 * V)
                t, w, g0 = dtd[rows, lane(j)], u[rows, lane(j)], gy[rows, lane(j)]
                t0 = jnp.where(t == RESET, 0.0, t)
                gu = [jnp.zeros((V, LN), F32), jnp.zeros((V, LN), F32)]
                gt = [jnp.zeros((V, LN), F32), jnp.zeros((V, LN), F32)]
                for i in range(half):
                    n = n0 + i
                    b = bcb[rows, lane(n)].astype(F32)
                    c = bcb[rows, lane(N + n)].astype(F32)
                    m = m_s[j, rows, lane(n)].astype(F32)
                    pc = g0 * (m + w * b)
                    pb = [None, None]
                    gc = g0 * c
                    for k, p in ((1, BOT), (0, TOP)):
                        g = gs[i] + gc[p]
                        pb[k] = g * w[p]
                        gu[k] = gu[k] + g * b[p]
                        x = g * m[p]
                        gt[k] = gt[k] + x * dn[i]
                        gd[i] = gd[i] + x * t0[p]
                        gs[i] = jnp.exp2(t[p] * dn[i]) * g
                    pb = jnp.concatenate(pb, axis=0)
                    if j > 0:
                        pb = pb + x_s[rows, lane(n)]
                        pc = pc + x_s[rows, lane(N + n)]
                    x_s[rows, lane(n)] = pb
                    x_s[rows, lane(N + n)] = pc
                gu, gt = jnp.concatenate(gu, axis=0), jnp.concatenate(gt, axis=0)
                if n0 > 0:
                    gu = gu + gsc[rows, lane(j)]
                    gt = gt + y_s[rows, lane(j)]
                gsc[rows, lane(j)] = gu
                y_s[rows, lane(j)] = gt
                return tuple(gs), tuple(gd)

            zero = tuple(jnp.zeros((V, LN), F32) for _ in range(half))
            first = tuple(start[1, n * V : (n + 1) * V, lane(j)] for n in range(n0, n0 + half))
            _, gd = lax.fori_loop(0, Q // 2, behind, (first, zero))
            for i in range(half):
                dec = dec2[n0 + i : n0 + i + 1, lane(j)] * (1.0 / LOG2E)
                gdec[n0 + i : n0 + i + 1, lane(j)] = jnp.sum(gd[i], axis=0, keepdims=True) * dec

    def finish(i, acc):
        rows = pl.ds(pl.multiple_of(i * 64, 64), 64)
        out = []
        for j in range(NB):
            x = inp[rows, lane(j)].astype(F32)
            z = dtpre[rows, lane(j)]
            gu = gsc[rows, lane(j)]
            gt = y_s[rows, lane(j)] * (1.0 / LOG2E) + gu * x
            dt = jnp.maximum(z, 0.0) + jnp.log1p(jnp.exp(-jnp.abs(z)))
            gz = gt * sigmoid(z)
            gpl[rows, lane(j)] = gz.astype(BF16)
            gsc[rows, lane(j)] = gu * dt + gy[rows, lane(j)] * cp[6:7, lane(j)]
            out.append(acc[j] + jnp.sum(gz.reshape(8, V, LN), axis=0))
        return tuple(out)

    db = lax.fori_loop(0, T // 64, finish, tuple(jnp.zeros((V, LN), F32) for _ in range(NB)))
    for j in range(NB):
        gskip[1:2, lane(j)] = jnp.sum(db[j], axis=0, keepdims=True)
    gwdt[...] = dot(gpl[...], lows[...], 0, 0)
    gx[:, 0 : d.R] = dot(gpl[...], wdt[...])
    acc = jnp.zeros((T, 2 * N), F32)
    for n in range(0, 2 * N, 4):
        row = lax.div(lax.broadcasted_iota(jnp.int32, (4 * LN, 2 * N), 0), LN) + n
        col = lax.broadcasted_iota(jnp.int32, (4 * LN, 2 * N), 1)
        pick = jnp.where(row == col, 1.0, 0.0).astype(BF16)
        acc = acc + dot(x_s[:, n * LN : (n + 4) * LN].astype(BF16), pick)
    gx[:, d.R : d.R + 2 * N] = acc


def rear(
    d, gxp, inp, gsc, xp, pre, rel, xb, cp, hid, normed, w, ggate_n, gain, gskip, gdec, gwdt,
    gnp, giwx, small, ggain,
    ga, gxe, gpn, rowsum,
):
    CL, T, NB = d.CL, d.T, d.NB
    s = gxp[0]
    for f in range(1, d.F):
        s = s + gxp[f]
    gxd = s.astype(BF16)
    W = d.R + 2 * d.N
    pad = HG * V
    for c in range(0, CL, 256):
        ga[pad : pad + T, c : c + 256] = gsc[:, c : c + 256] + dot(gxd, xp[c : c + 256, :], 1, 1)
    ga[0:pad, :] = jnp.zeros((pad, CL), F32)
    ga[pad + T :, :] = jnp.zeros((pad, CL), F32)

    def act(i, acc):
        r0 = pl.multiple_of(i * 64, 64)
        rows = pl.ds(r0, 64)
        shift = pl.ds(pl.multiple_of(r0 + pad, V), 64)
        age = rel[shift, :]
        out = []
        for j in range(NB):
            p = pre[rows, lane(j)]
            q = sigmoid(p)
            g = ga[shift, lane(j)] * q * (1.0 + p * (1.0 - q))
            ga[shift, lane(j)] = g
            a = list(acc[j])
            a[4] = a[4] + jnp.sum(g.reshape(8, V, LN), axis=0)
            for k in range(d.K):
                back = d.K - 1 - k
                xs = xb[pl.ds(pl.multiple_of(r0 + (HG - back) * V, V), 64), lane(j)]
                t = jnp.where(age >= back, g * xs, 0.0)
                a[k] = a[k] + jnp.sum(t.reshape(8, V, LN), axis=0)
            out.append(tuple(a))
        return tuple(out)

    zero = tuple(tuple(jnp.zeros((V, LN), F32) for _ in range(5)) for _ in range(NB))
    acc = lax.fori_loop(0, T // 64, act, zero)
    rowsum[...] = jnp.zeros_like(rowsum)
    for j in range(NB):
        for k in range(5):
            rowsum[k : k + 1, lane(j)] = jnp.sum(acc[j][k], axis=0, keepdims=True)
    rowsum[5:6, :] = gskip[1:2, :]
    rowsum[6:7, :] = gskip[0:1, :]
    rowsum[8 : 8 + d.N, :] = gdec[...]
    small[:, 0:LN] = rowsum[...].T.astype(BF16)
    small[:, LN : LN + W] = dot(inp[...], gxd, 0, 0).astype(BF16)
    small[:, LN + W : LN + W + d.R] = gwdt[...].astype(BF16)
    small[:, LN + W + d.R :] = jnp.zeros((CL, 3 * LN - LN - W - d.R), BF16)

    def spread(i, _):
        r0 = pl.multiple_of(i * 32, 32)
        for j in range(NB):
            acc = jnp.zeros((32, LN), F32)
            for k in range(d.K):
                back = d.K - 1 - k
                src = pl.ds(pl.multiple_of(r0 + back * V, V), 32)
                acc = acc + jnp.where(
                    rel[src, :] >= back, ga[src, lane(j)] * cp[k : k + 1, lane(j)], 0.0
                )
            gxe[pl.ds(r0, 32), lane(j)] = acc.astype(BF16)
        return 0

    lax.fori_loop(0, d.TE // 32, spread, 0)
    back_m = from_scan(d, HG)
    for c in range(0, CL, 256):
        gpn[:, c : c + 256] = dot(back_m, gxe[:, c : c + 256]).astype(BF16)
    gpn[0:T, CL:] = ggate_n[...]
    gpn[T:, CL:] = jnp.zeros((d.NAT - T, CL), BF16)
    for c in range(0, CL, 256):
        giwx[:, c : c + 256] = dot(normed[...], gpn[:, c : c + 256], 0, 0).astype(BF16)
    for c in range(0, d.D, 256):
        g = dot(gpn[:, 0:CL], w[0, c : c + 256, :], 1, 1) + dot(gpn[:, CL:], w[1, c : c + 256, :], 1, 1)
        gnp[:, c : c + 256] = g.astype(BF16)
    ggain[...] = jnp.zeros_like(ggain)

    def gains(i, acc):
        rows = pl.ds(pl.multiple_of(i * 64, 64), 64)
        h = hid[rows, :].astype(F32)
        inv = lax.rsqrt(jnp.mean(h * h, axis=-1, keepdims=True) + EPS)
        return acc + jnp.sum((gnp[rows, :].astype(F32) * h * inv).reshape(8, V, d.D), axis=0)

    tot = lax.fori_loop(0, d.NAT // 64, gains, jnp.zeros((V, d.D), F32))
    ggain[0:1, :] = jnp.sum(tot, axis=0, keepdims=True)


def vm(*shape, dtype=F32):
    return pltpu.VMEM(shape, dtype)


def per_device(
    d, hidden, cluster_lengths, norm_gain, in_weight, conv_weight, conv_bias, xproj_weight,
    dt_weight, dt_bias, a_log, skip, out_weight, cotangent,
):
    S, F, T, D, CL, N, tok = d.S, d.F, d.T, d.D, d.CL, d.N, d.tok
    fs, ss = range(F), range(S)
    DF = D // F
    part = functools.partial
    lens = jnp.broadcast_to(cluster_lengths[0][:, None], (cluster_lengths.shape[1], LN))
    gain8 = jnp.broadcast_to(norm_gain.astype(F32)[None, :], (V, DF))
    whole = lambda r, ms, mf, ps, pf: r
    hid_item = dict(
        src=hidden[0],
        shape=(d.NAT, D),
        sends=[(0, k, whole, lambda r, ms, mf: r.at[pl.ds(mf * tok, tok)]) for k in fs]
        + [
            (
                1,
                k,
                lambda r, ms, mf, ps, pf: r.at[pl.ds(tok - TAIL, TAIL)],
                lambda r, ms, mf: r.at[pl.ds(T + mf * TAIL, TAIL)],
            )
            for k in fs
        ],
    )
    w_item = dict(
        src=in_weight,
        shape=(2, D, CL),
        sends=[
            (
                0,
                k,
                lambda r, ms, mf, ps, pf, g=g: r.at[:, pl.ds(pl.multiple_of(g * d.DI + pf * CL, LN), CL)],
                lambda r, ms, mf, g=g: r.at[g, pl.ds(mf * DF, DF)],
            )
            for k in fs
            for g in (0, 1)
        ],
    )
    hid, w, cot, gains, lens = exchange(
        d, [hid_item, w_item, gather_f(d, cotangent[0]), gather_f(d, gain8), gather_f(d, lens)], 0
    )
    cot = cot.reshape(T, D)
    gain = gains[:, 0, :].reshape(1, D)
    rows = [conv_weight.astype(F32).T, conv_bias, dt_bias, skip]
    cp = jnp.concatenate([r.astype(F32).reshape(-1, CL) for r in rows], axis=0)
    cp = jnp.pad(cp, ((0, V - cp.shape[0]), (0, 0)))
    dec2 = -jnp.exp(a_log.astype(F32).T) * LOG2E
    W = d.R + 2 * N
    xp = jnp.pad(xproj_weight, ((0, 0), (0, LN - W)))
    TP = T + 2 * HG * V

    normed, xb, gate, pre, inp, rel, xd = kernel(
        part(front, d),
        (hid, gain, w, cp, xp, lens),
        [((d.NAT, D), BF16), ((d.TE, CL), F32), ((T, CL), F32), ((T, CL), F32), ((T, CL), BF16),
         ((TP, LN), F32), ((T, LN), F32)],
        [vm(d.TE, D, dtype=BF16)],
    )
    (xdp,) = exchange(d, [gather_f(d, xd.astype(BF16))], 1)
    lows, dtpre, dtd, u, bcb, gg, gy, cots, ends, e_out, sd = kernel(
        part(steps_and_local, d),
        (xdp.astype(F32), dt_weight, cp, gate, inp, rel, cot, out_weight, dec2),
        [((T, d.R), BF16), ((T, CL), F32), ((T, CL), F32), ((T, CL), F32), ((T, 2 * N * LN), F32 if T <= 512 else BF16),
         ((T, CL), F32), ((T, CL), F32), ((T, D), BF16), ((2, N * V, CL), F32),
         ((2, N * V, CL), BF16), ((2 * V, CL), F32)],
    )
    pieces = dict(
        src=e_out,
        shape=(S, N * V, CL),
        sends=[
            (
                k,
                0,
                lambda r, ms, mf, ps, pf: r.at[jnp.where(ps > ms, 0, 1)],
                lambda r, ms, mf: r.at[ms],
            )
            for k in ss
            if k > 0
        ],
    )
    totals = dict(
        src=sd[V:],
        shape=(S, V, CL),
        sends=[(k, 0, whole, lambda r, ms, mf: r.at[ms]) for k in ss if k > 0],
    )
    epieces, sdall = exchange(d, [pieces, totals], 2)
    outp, gow, giwg, gpl, gsc, gx, gdec, gwdt, gskip, ggate_n = kernel(
        lambda *r: scan_both(d, *r[:28], *r[29:36], r[28]),
        (epieces, sdall, ends, sd, dec2, dtpre, dtd, u, inp, bcb, gg, gy, gate, cp, cots, out_weight,
         normed, dt_weight, lows),
        [((T, D), BF16), ((CL, D), BF16), ((D, CL), BF16), ((T, CL), BF16), ((T, CL), F32),
         ((T, LN), F32), ((N, CL), F32), ((CL, d.R), F32), ((V, CL), F32), ((T, CL), BF16)],
        [vm(d.NB, T, N * LN, dtype=BF16), vm(T, CL), vm(2, N * V, CL), vm(T, 2 * N * LN),
         vm(T, CL, dtype=BF16), vm(T, CL, dtype=BF16), vm(T, CL, dtype=BF16)],
    )
    (gxp,) = exchange(d, [gather_f(d, gx.astype(BF16))], 3)
    gnp, giwx, small, ggain = kernel(
        part(rear, d),
        (gxp[:, :, :W].astype(F32), inp, gsc, xproj_weight, pre, rel, xb, cp, hid, normed, w, ggate_n, gain, gskip,
         gdec, gwdt),
        [((d.NAT, D), BF16), ((D, CL), BF16), ((CL, 3 * LN), BF16), ((V, D), F32)],
        [vm(TP, CL), vm(d.TE, CL, dtype=BF16), vm(d.NAT, 2 * CL, dtype=BF16), vm(LN, CL)],
    )
    normal = dict(
        src=gnp,
        shape=(F * (tok + TAIL), D),
        sends=[
            (
                0,
                k,
                lambda r, ms, mf, ps, pf: r.at[pl.ds(pf * tok, tok)],
                lambda r, ms, mf: r.at[pl.ds(mf * tok, tok)],
            )
            for k in fs
        ]
        + [
            (
                -1,
                k,
                lambda r, ms, mf, ps, pf: r.at[pl.ds(T + pf * TAIL, TAIL)],
                lambda r, ms, mf: r.at[pl.ds(T + mf * TAIL, TAIL)],
            )
            for k in fs
        ],
    )
    blocks = lambda a: a.reshape((S, a.shape[0] // S) + a.shape[1:])
    ggain = jnp.swapaxes(ggain.reshape(V, S, D // S), 0, 1)
    gnr, outr, gowr, smallr, gxr, ggr, gar = exchange(
        d,
        [normal, swap_f(d, outp.reshape(F, tok, D))]
        + [swap_s(d, a) for a in (blocks(gow), blocks(small), blocks(giwx), blocks(giwg), ggain)],
        4,
    )
    add = lambda a: jnp.sum(a.astype(F32), axis=0)
    DS = D // (S * F)
    gwx, gwg = (add(a).astype(BF16).reshape(F, DS, CL) for a in (gxr, ggr))
    ga = jnp.swapaxes(add(gar).reshape(V, F, DS), 0, 1)
    wx, wg, gg = exchange(d, [swap_f(d, a) for a in (gwx, gwg, ga)], 5)
    g_in = jnp.concatenate(
        [jnp.swapaxes(a, 0, 1).reshape(DS, d.DI) for a in (wx, wg)], axis=1
    ).astype(F32)
    g_gain = add(gg)[0]
    packed = jnp.concatenate([add(gowr), add(smallr)], axis=1).astype(BF16)
    perm = [(j * F + f, f * S + j) for f in fs for j in ss]
    packed = lax.ppermute(packed, ("seq", "fsdp"), perm).astype(F32)
    g_out, sm = packed[:, :D], packed[:, D:]
    h = hidden[0].astype(F32)
    inv = lax.rsqrt(jnp.mean(h * h, axis=-1, keepdims=True) + EPS)
    gn = add(gnr[:T].reshape(F, tok, D))
    gn = gn + jnp.pad(add(gnr[T:].reshape(F, TAIL, D)), ((tok - TAIL, 0), (0, 0)))
    g2 = gn * gain
    mean = jnp.mean(g2 * h, axis=-1, keepdims=True)
    g_hid = cotangent[0].astype(F32) + inv * g2 - h * (inv * inv * inv) * mean
    output = (h + add(outr)).astype(BF16)
    return (
        output[None],
        g_hid[None],
        g_gain,
        g_in,
        sm[:, 0 : d.K],
        sm[:, 4],
        sm[:, LN : LN + W],
        sm[:, LN + W : LN + W + d.R],
        sm[:, 5],
        sm[:, V : V + N],
        sm[:, 6],
        g_out,
    )


def solution(mesh):
    S, F = mesh.shape["seq"], mesh.shape["fsdp"]

    def run(*args):
        tok, D = args[0].shape[1] // S, args[0].shape[2]
        d = Dims(
            S, F, tok, D, args[11].shape[0], args[9].shape[1], args[7].shape[1], args[4].shape[1]
        )
        return jax.shard_map(
            functools.partial(per_device, d),
            mesh=mesh,
            in_specs=(
                P("fsdp", "seq", None), P("fsdp", None), P("fsdp"), P("fsdp", None),
                P("fsdp", None), P("fsdp"), P("fsdp", None), P("fsdp", None), P("fsdp"),
                P("fsdp", None), P("fsdp"), P("fsdp", None), P("fsdp", "seq", None),
            ),
            out_specs=(
                P("fsdp", "seq", None), P("fsdp", "seq", None), P(("seq", "fsdp")),
                P(("seq", "fsdp"), None), P(("seq", "fsdp"), None), P(("seq", "fsdp")),
                P(("seq", "fsdp"), None), P(("seq", "fsdp"), None), P(("seq", "fsdp")),
                P(("seq", "fsdp"), None), P(("seq", "fsdp")), P(("seq", "fsdp"), None),
            ),
            check_vma=False,
        )(*args)

    return run
```

```python
import functools
import math

import jax
import jax.numpy as jnp
from jax import lax
from jax.experimental import pallas as pl
from jax.experimental.pallas import tpu as pltpu
from jax.sharding import PartitionSpec as P

EPS = 1e-05
V = 8
LN = 128
HG = 4
TAIL = 16
LOG2E = 1.0 / math.log(2.0)
RESET = 1e30
F32 = jnp.float32
TOP, BOT = slice(0, V), slice(V, 2 * V)
BF16 = jnp.bfloat16
MESH = pl.DeviceIdType.MESH


class Dims:
    def __init__(self, S, F, tok, D, DI, N, R, K, clusters):
        self.S, self.F, self.tok, self.D, self.DI = S, F, tok, D, DI
        self.N, self.R, self.K, self.clusters = N, R, K, clusters
        self.H = V // F
        self.Q = tok // self.H
        self.T = F * tok
        self.TE = (self.Q + HG) * V
        self.NAT = F * (tok + TAIL)
        self.CL = DI // F
        self.NB = self.CL // LN


def dot(a, b, ca=1, cb=0):
    return lax.dot_general(a, b, (((ca,), (cb,)), ((), ())), preferred_element_type=F32)


def sigmoid(v):
    return 1.0 / (1.0 + jnp.exp(-v))


def kernel(body, args, outs, scratch=()):
    return pl.pallas_call(
        body,
        out_shape=[jax.ShapeDtypeStruct(s, t) for s, t in outs],
        in_specs=[pl.BlockSpec(memory_space=pltpu.VMEM)] * len(args),
        out_specs=[pl.BlockSpec(memory_space=pltpu.VMEM)] * len(outs),
        scratch_shapes=list(scratch),
        compiler_params=pltpu.CompilerParams(vmem_limit_bytes=60 * 1024 * 1024),
    )(*args)


def lane(j):
    return slice(j * LN, (j + 1) * LN)


def natural_of(d, row, halo):
    q = lax.div(row, V) - halo
    v = lax.rem(row, V)
    f = lax.div(v, d.H)
    p = lax.rem(v, d.H) * d.Q + q
    return jnp.where(p >= 0, f * d.tok + p, d.T + f * TAIL + TAIL + p)


def to_scan(d, halo):
    rows, cols = (d.TE, d.NAT) if halo else (d.T, d.T)
    want = natural_of(d, lax.broadcasted_iota(jnp.int32, (rows, 1), 0), halo)
    have = lax.broadcasted_iota(jnp.int32, (rows, cols), 1)
    return jnp.where(have == want, 1.0, 0.0).astype(BF16)


def from_scan(d, halo):
    rows, cols = (d.NAT, d.TE) if halo else (d.T, d.T)
    want = natural_of(d, lax.broadcasted_iota(jnp.int32, (1, cols), 1), halo)
    have = lax.broadcasted_iota(jnp.int32, (rows, cols), 0)
    return jnp.where(have == want, 1.0, 0.0).astype(BF16)


class Refs:
    pass


class Copy:
    def __init__(self, copy, remote):
        self.copy, self.sent, self.got = copy, not remote, False
        self.remote = remote

    def wait_send(self):
        if not self.sent:
            self.copy.wait_send()
            self.sent = True

    def wait_recv(self):
        if not self.got:
            if self.remote:
                self.copy.wait_recv()
            else:
                self.copy.wait()
            self.got = True

    def wait(self):
        self.wait_send()
        self.wait_recv()


class Net:
    def __init__(self, d, ssem, rsem):
        self.d, self.ssem, self.rsem, self.used = d, ssem, rsem, 0
        self.ms, self.mf = lax.axis_index("seq"), lax.axis_index("fsdp")
        self.open = []

    def at(self, ds, df):
        return lax.rem(self.ms + ds % self.d.S, self.d.S), lax.rem(self.mf + df % self.d.F, self.d.F)

    def start(self, copy, remote):
        copy.start()
        self.open.append(Copy(copy, remote))
        return self.open[-1]

    def send(self, src, dst, ps, pf):
        i = self.used
        self.used += 1
        return self.start(
            pltpu.make_async_remote_copy(
                src, dst, self.ssem.at[i], self.rsem.at[i], {"seq": ps, "fsdp": pf}, device_id_type=MESH
            ),
            True,
        )

    def local(self, src, dst):
        i = self.used
        self.used += 1
        return self.start(pltpu.make_async_copy(src, dst, self.rsem.at[i]), False)

    def drain(self):
        for c in self.open:
            c.wait()


class Scatter:
    def __init__(self, net, mine, near, far):
        self.net, self.mine, self.near, self.far = net, mine, near, far
        d = net.d
        self.half = d.S // 2
        self.x, self.z = lax.rem(net.ms, 2), lax.div(net.ms, 2)
        self.pal = net.ms + 1 - 2 * self.x
        self.order = [lax.rem(self.z + k, self.half) for k in list(range(1, self.half)) + [0]]
        self.out, self.ins = [], []

    def first(self):
        for z in self.order:
            self.out.append(
                self.net.send(self.mine.at[1 - self.x, z], self.near.at[z], self.pal, self.net.mf)
            )

    def second(self):
        for k, z in enumerate(self.order):
            self.out[k].wait()
            both = self.mine[self.x, z].astype(F32) + self.near[z].astype(F32)
            self.mine[self.x, z] = both.astype(self.mine.dtype)
            if k < self.half - 1:
                self.ins.append(
                    self.net.send(
                        self.mine.at[self.x, z], self.far.at[k], z * 2 + self.x, self.net.mf
                    )
                )

    def total(self):
        acc = self.mine[self.x, self.z].astype(F32)
        for k, c in enumerate(self.ins):
            c.wait()
            acc = acc + self.far[k].astype(F32)
        return acc


def layer(d, names, *refs):
    r = Refs()
    for name, ref in zip(names, refs):
        setattr(r, name, ref)
    S, F, CL, T, N, Q, NB, D, tok, H = d.S, d.F, d.CL, d.T, d.N, d.Q, d.NB, d.D, d.tok, d.H
    DF = D // F
    net = Net(d, r.ssem, r.rsem)
    ms, mf = net.ms, net.mf
    x_bit = lax.rem(ms, 2)
    pal = ms + 1 - 2 * x_bit
    core = mf + 1 - 2 * lax.rem(mf, 2)
    spot = mf * S + ms
    home_s, home_f = lax.div(spot, F), lax.rem(spot, F)
    mine = ms * F + mf
    from_s, from_f = lax.rem(mine, S), lax.div(mine, S)
    moves = spot != mine
    greet = {(0, k) for k in range(F)} | {(k, 0) for k in range(S)}
    greet |= {(k % S, g) for k in (1, -1) for g in range(F)}
    greet = sorted(greet - {(0, 0)})
    bar = pltpu.get_barrier_semaphore()
    for ds, df in greet:
        ps, pf = net.at(-ds, -df)
        pl.semaphore_signal(bar, inc=1, device_id={"seq": ps, "fsdp": pf}, device_id_type=MESH)

    @pl.when(moves)
    def _():
        pl.semaphore_signal(
            bar, inc=1, device_id={"seq": from_s, "fsdp": from_f}, device_id_type=MESH
        )

    own = [
        net.local(r.hidden, r.hid.at[pl.ds(mf * tok, tok)]),
        net.local(r.params, r.pg.at[mf]),
        net.local(r.in_weight.at[:, pl.ds(pl.multiple_of(mf * CL, LN), CL)], r.w.at[0, pl.ds(mf * DF, DF)]),
        net.local(
            r.in_weight.at[:, pl.ds(pl.multiple_of(d.DI + mf * CL, LN), CL)],
            r.w.at[1, pl.ds(mf * DF, DF)],
        ),
        net.local(r.cotangent, r.cot.at[pl.ds(mf * tok, tok)]),
        net.local(r.out_weight, r.ow),
        net.local(r.xproj_weight, r.xp),
        net.local(r.dt_weight, r.wdt),
        net.local(r.conv_weight, r.cw),
        net.local(r.a_log, r.al),
    ]
    pl.semaphore_wait(bar, len(greet) + moves.astype(jnp.int32))

    rows_of = lambda ref, f, n: ref.at[pl.ds(f * n, n)]
    same_core = [lax.rem(mf + 2 * k, F) for k in range(1, F // 2)]
    other_chip = [(lax.rem(mf + 2 * k, F), lax.rem(core + 2 * k, F)) for k in range(1, F // 2)]

    def spread_rows(src, dst):
        direct = [net.send(src, rows_of(dst, mf, tok), ms, f) for f in same_core]
        beside = [net.send(src, rows_of(dst, mf, tok), ms, core)]
        return direct, beside

    def relay_rows(dst, direct, beside):
        for k, c in enumerate(direct):
            c.wait()
            f = lax.rem(mf + F - 2 * (k + 1), F)
            beside.append(net.send(rows_of(dst, f, tok), rows_of(dst, f, tok), ms, core))

    pgs = [net.send(r.params, r.pg.at[mf], ms, net.at(0, k)[1]) for k in range(1, F)]
    h_direct, h_beside = spread_rows(r.hidden, r.hid)
    halo = [
        net.send(
            r.hidden.at[pl.ds(tok - TAIL, TAIL)],
            r.hid.at[pl.ds(T + mf * TAIL, TAIL)],
            *net.at(1, k),
        )
        for k in range(F)
    ]

    def w_slice(g, f):
        return r.in_weight.at[:, pl.ds(pl.multiple_of(g * d.DI + f * CL, LN), CL)]

    w_beside = [net.send(w_slice(g, core), r.w.at[g, pl.ds(mf * DF, DF)], ms, core) for g in (0, 1)]
    HF = DF // 2

    def w_far(g):
        out = []
        for pair in other_chip:
            for f in pair:
                src = r.in_weight.at[
                    pl.ds(x_bit * HF, HF), pl.ds(pl.multiple_of(g * d.DI + f * CL, LN), CL)
                ]
                out.append(net.send(src, r.w.at[g, pl.ds(mf * DF + x_bit * HF, HF)], ms, f))
        return out

    def w_relay(g, far):
        out = []
        i = 0
        for k in range(1, F // 2):
            for flip in (0, 1):
                far[i].wait()
                i += 1
                f0 = lax.rem(mf + F - 2 * k, F)
                if flip:
                    f0 = f0 + 1 - 2 * lax.rem(f0, 2)
                place = r.w.at[g, pl.ds(f0 * DF + x_bit * HF, HF)]
                out.append(net.send(place, place, pal, mf))
        return out

    back0 = from_scan(d, 0)
    for c in h_direct:
        c.wait_send()
    wx_far = w_far(0)
    for k, c in enumerate(h_direct):
        c.wait_recv()
        f = lax.rem(mf + F - 2 * (k + 1), F)
        h_beside.append(net.send(rows_of(r.hid, f, tok), rows_of(r.hid, f, tok), ms, core))
    for c in pgs + own[:2]:
        c.wait()
    for f in range(F):
        r.gain[0:1, f * DF : (f + 1) * DF] = r.pg[f, 3:4, 0:DF]
    sub = lax.broadcasted_iota(jnp.int32, (V, LN), 0)
    hidx = lax.rem(sub, H)
    stream = lax.div(sub, H)
    offs, run = [], jnp.zeros((V, LN), F32)
    for j in range(d.clusters - 1):
        for f in range(F):
            run = run + jnp.where(stream == f, r.pg[f, 4:5, j : j + 1], 0.0)
        offs.append(run)
    base = ms * tok + hidx * Q
    r.rel[0 : HG * V, :] = jnp.zeros((HG * V, LN), F32)
    r.rel[HG * V + T :, :] = jnp.zeros((HG * V, LN), F32)

    def mark(q, _):
        pos = (base + q).astype(F32)
        last = jnp.zeros((V, LN), F32)
        for o in offs:
            last = jnp.maximum(last, jnp.where(o <= pos, o, 0.0))
        r.rel[pl.ds(pl.multiple_of((q + HG) * V, V), V), :] = jnp.where(pos == 0.0, 0.5, pos - last)
        return 0

    lax.fori_loop(0, Q, mark, 0)
    own[8].wait()
    own[9].wait()
    eye = lambda n: jnp.where(
        lax.broadcasted_iota(jnp.int32, (n, n), 0) == lax.broadcasted_iota(jnp.int32, (n, n), 1), 1.0, 0.0
    ).astype(BF16)
    r.cp[0 : d.K, :] = dot(eye(d.K), r.cw[...], 1, 1)
    r.cp[4:7, :] = r.pg[mf, 0:3, :]
    r.dec[...] = -LOG2E * jnp.exp(dot(eye(N), r.al[...], 1, 1))
    for c in h_beside + halo:
        c.wait()

    def rms(i, _):
        rows = pl.ds(pl.multiple_of(i * 64, 64), 64)
        h = r.hid[rows, :].astype(F32)
        inv = lax.rsqrt(jnp.mean(h * h, axis=-1, keepdims=True) + EPS)
        r.normed[rows, :] = (h * inv * r.gain[...]).astype(BF16)
        return 0

    lax.fori_loop(0, d.NAT // 64, rms, 0)
    perm = to_scan(d, HG)
    for c in range(0, D, 256):
        r.big[:, c : c + 256] = dot(perm, r.normed[:, c : c + 256]).astype(BF16)
    wx_near = w_relay(0, wx_far)
    wg_far = w_far(1)
    c_direct, c_beside = spread_rows(r.cotangent, r.cot)
    own[2].wait()
    w_beside[0].wait()
    for c in wx_near:
        c.wait()
    for c in range(0, CL, 256):
        r.xb[:, c : c + 256] = (
            dot(r.big[:, :], r.w[0, :, c : c + 256]).astype(BF16).astype(F32)
        )

    def conv(i, _):
        r0 = pl.multiple_of(i * 64, 64)
        rows = pl.ds(r0, 64)
        age = r.rel[pl.ds(pl.multiple_of(r0 + HG * V, V), 64), :]
        for j in range(NB):
            acc = jnp.zeros((64, LN), F32) + r.cp[4:5, lane(j)]
            for k in range(d.K):
                back = d.K - 1 - k
                xs = r.xb[pl.ds(pl.multiple_of(r0 + (HG - back) * V, V), 64), lane(j)]
                acc = acc + jnp.where(age >= back, xs * r.cp[k : k + 1, lane(j)], 0.0)
            r.pre[rows, lane(j)] = acc
            r.inp[rows, lane(j)] = (acc * sigmoid(acc)).astype(BF16)
        return 0

    lax.fori_loop(0, T // 64, conv, 0)
    own[6].wait()
    W = d.R + 2 * N
    r.xd[:, 0:W] = dot(r.inp[...], r.xp[...]).astype(BF16)
    xds = [net.send(r.xd, r.xdr.at[k - 1], *net.at(0, k)) for k in range(1, F)]
    wg_near = w_relay(1, wg_far)
    relay_rows(r.cot, c_direct, c_beside)
    for c in [own[3], own[4], own[5], w_beside[1]] + wg_near + c_beside:
        c.wait()
    for c in range(0, CL, 256):
        r.gate[:, c : c + 256] = dot(r.big[HG * V :, :], r.w[1, :, c : c + 256])
    perm = to_scan(d, 0)
    for c in range(0, D, 256):
        r.big[0:T, c : c + 256] = dot(perm, r.cot[:, c : c + 256]).astype(BF16)
    for c in range(0, CL, 256):
        r.gg[0:T, c : c + 256] = dot(r.big[0:T, :], r.ow[c : c + 256, :], 1, 1)

    def gys(i, _):
        rows = pl.ds(pl.multiple_of(i * 64, 64), 64)
        for j in range(NB):
            g = r.gate[rows, lane(j)]
            r.gy[rows, lane(j)] = r.gg[rows, lane(j)] * (g * sigmoid(g))
        return 0

    lax.fori_loop(0, T // 64, gys, 0)
    for c in xds:
        c.wait()
    xd = r.xd[:, 0:W].astype(F32)
    for k in range(F - 1):
        xd = xd + r.xdr[k, :, 0:W].astype(F32)
    own[7].wait()
    low = xd[:, : d.R].astype(BF16)
    r.xd[:, 0 : d.R] = low
    for c in range(0, CL, 256):
        r.dtpre[:, c : c + 256] = dot(low, r.wdt[c : c + 256, :], 1, 1)

    def steps(i, acc):
        rows = pl.ds(pl.multiple_of(i * 64, 64), 64)
        age = r.rel[pl.ds(pl.multiple_of(i * 64 + HG * V, V), 64), :]
        out = []
        for j in range(NB):
            z = r.dtpre[rows, lane(j)] + r.cp[5:6, lane(j)]
            dt = jnp.maximum(z, 0.0) + jnp.log1p(jnp.exp(-jnp.abs(z)))
            r.dtpre[rows, lane(j)] = z
            e = jnp.where(age == 0.0, RESET, dt)
            r.dtd[rows, lane(j)] = e
            r.u[rows, lane(j)] = dt * r.inp[rows, lane(j)].astype(F32)
            out.append(acc[j] + jnp.sum(e.reshape(8, V, LN), axis=0))
        return tuple(out)

    sums = lax.fori_loop(0, T // 64, steps, tuple(jnp.zeros((V, LN), F32) for _ in range(NB)))
    for j in range(NB):
        whole, t = sums[j], 1
        while t < H:
            low_half = lax.rem(lax.div(hidx, t), 2) == 0
            whole = whole + jnp.where(low_half, pltpu.roll(whole, V - t, 0), pltpu.roll(whole, t, 0))
            t *= 2
        r.sd[0:V, lane(j)] = sums[j]
        r.tot[:, lane(j)] = whole
    tots = [net.send(r.tot, r.totr.at[k - 1], *net.at(k, 0)) for k in range(1, S)]
    bc = xd[:, d.R : W]
    hi = bc.astype(BF16)
    rest = (bc - hi.astype(F32)).astype(BF16)
    both = jnp.concatenate([hi, rest], axis=1)
    for n in range(0, 2 * N, 4):
        row = lax.rem(lax.broadcasted_iota(jnp.int32, (4 * N, 4 * LN), 0), 2 * N)
        col = lax.div(lax.broadcasted_iota(jnp.int32, (4 * N, 4 * LN), 1), LN) + n
        pick = jnp.where(row == col, 1.0, 0.0).astype(BF16)
        r.bcb[:, n * LN : (n + 4) * LN] = dot(both, pick).astype(r.bcb.dtype)

    half = N // 2
    row_n = lambda n: slice(n * V, (n + 1) * V)
    dec_of = lambda n, j: jnp.broadcast_to(r.dec[n : n + 1, lane(j)], (V, LN))

    def own_ends(j):
        for n0 in range(0, N, half):
            dn = [dec_of(n, j) for n in range(n0, n0 + half)]

            def local(q, carry, n0=n0, dn=dn):
                hs, gs = list(carry[0]), list(carry[1])
                up = pl.ds(pl.multiple_of(q * 2 * V, 2 * V), 2 * V)
                down = pl.ds(pl.multiple_of((Q - 2 - 2 * q) * V, 2 * V), 2 * V)
                a_dt, a_u = r.dtd[up, lane(j)], r.u[up, lane(j)]
                b_dt, b_gy = r.dtd[down, lane(j)], r.gy[down, lane(j)]
                for i in range(half):
                    b = r.bcb[up, lane(n0 + i)].astype(F32)
                    c = r.bcb[down, lane(N + n0 + i)].astype(F32)
                    for t in (TOP, BOT):
                        hs[i] = jnp.exp2(a_dt[t] * dn[i]) * hs[i] + a_u[t] * b[t]
                    for t in (BOT, TOP):
                        gs[i] = jnp.exp2(b_dt[t] * dn[i]) * (gs[i] + b_gy[t] * c[t])
                return tuple(hs), tuple(gs)

            zero = tuple(jnp.zeros((V, LN), F32) for _ in range(half))
            hs, gs = lax.fori_loop(0, Q // 2, local, (zero, zero))
            for i in range(half):
                r.ends[0, row_n(n0 + i), lane(j)] = hs[i]
                r.ends[1, row_n(n0 + i), lane(j)] = gs[i]
        one = r.sd[0:V, lane(j)]
        fw, bw = [], []
        for n0 in range(0, N, H):
            a, b = jnp.zeros((V, LN), F32), jnp.zeros((V, LN), F32)
            for t in range(H):
                fac = jnp.exp2(one * dec_of(n0 + t, j))
                e, g = r.ends[0, row_n(n0 + t), lane(j)], r.ends[1, row_n(n0 + t), lane(j)]
                x, y = e, g
                for h in range(1, H):
                    x = jnp.where(hidx == h, fac * pltpu.roll(x, 1, 0) + e, x)
                    y = jnp.where(hidx == H - 1 - h, fac * pltpu.roll(y, V - 1, 0) + g, y)
                a = jnp.where(hidx == t, turn(x, t - (H - 1)), a)
                b = jnp.where(hidx == t, turn(y, t), b)
            fw.append(a)
            bw.append(b)
        for i in range(0, len(fw), 2):
            band = slice(i * V, (i + 2) * V)
            r.epack[0, j, band, :] = jnp.concatenate(fw[i : i + 2], axis=0).astype(BF16)
            r.epack[1, j, band, :] = jnp.concatenate(bw[i : i + 2], axis=0).astype(BF16)
        out = []
        for k in range(1, S):
            ps, pf = net.at(k, 0)
            out.append(
                net.send(r.epack.at[jnp.where(ps > ms, 0, 1), j], r.eget.at[j, ms], ps, pf)
            )
        return out

    def turn(x, by):
        return x if by % V == 0 else pltpu.roll(x, by % V, 0)

    def begin(j, copies):
        for c in copies:
            c.wait()
        tiles = N // H
        dn = []
        for i in range(tiles):
            x = dec_of(i * H, j)
            for t in range(1, H):
                x = jnp.where(hidx == t, dec_of(i * H + t, j), x)
            dn.append(x)

        def join(p, acc):
            tot = r.totr[lax.rem(ms + S - p, S) - 1, :, lane(j)]
            e = r.eget[j, p].astype(F32)
            return tuple(jnp.exp2(tot * dn[i]) * acc[i] + e[row_n(i)] for i in range(tiles))

        zero = tuple(jnp.zeros((V, LN), F32) for _ in range(tiles))
        fw = lax.fori_loop(0, ms, join, zero)
        bw = lax.fori_loop(0, S - 1 - ms, lambda i, acc: join(S - 1 - i, acc), zero)
        one = r.sd[0:V, lane(j)]
        for i in range(tiles):
            for t in range(H):
                n = i * H + t
                fac = jnp.exp2(one * dec_of(n, j))
                x, y = turn(fw[i], -t), turn(bw[i], H - 1 - t)
                for h in range(1, H):
                    xn = pltpu.roll(fac * x + r.ends[0, row_n(n), lane(j)], 1, 0)
                    yn = pltpu.roll(fac * y + r.ends[1, row_n(n), lane(j)], V - 1, 0)
                    x = jnp.where(hidx == h, xn, x)
                    y = jnp.where(hidx == H - 1 - h, yn, y)
                r.start[0, row_n(n), lane(j)] = x
                r.start[1, row_n(n), lane(j)] = y

    def forward(j):
        dn = [dec_of(n, j) for n in range(N)]

        def ahead(q, hs):
            hs = list(hs)
            rows = pl.ds(pl.multiple_of(q * 2 * V, 2 * V), 2 * V)
            t, w = r.dtd[rows, lane(j)], r.u[rows, lane(j)]
            y = [jnp.zeros((V, LN), F32), jnp.zeros((V, LN), F32)]
            for n in range(N):
                b = r.bcb[rows, lane(n)].astype(F32)
                c = r.bcb[rows, lane(N + n)].astype(F32)
                keep = []
                for k, p in enumerate((TOP, BOT)):
                    m = jnp.exp2(t[p] * dn[n]) * hs[n]
                    hs[n] = m + w[p] * b[p]
                    y[k] = y[k] + c[p] * hs[n]
                    keep.append(m)
                r.m_s[j, rows, lane(n)] = jnp.concatenate(keep, axis=0).astype(BF16)
            r.y_s[rows, lane(j)] = jnp.concatenate(y, axis=0)
            return tuple(hs)

        lax.fori_loop(0, Q // 2, ahead, tuple(r.start[0, row_n(n), lane(j)] for n in range(N)))

    def backward(j):
        for n0 in range(0, N, half):
            dn = [dec_of(n, j) for n in range(n0, n0 + half)]

            def behind(i, carry, n0=n0, dn=dn):
                gs, gd = list(carry[0]), list(carry[1])
                rows = pl.ds(pl.multiple_of((Q - 2 - 2 * i) * V, 2 * V), 2 * V)
                t, w, g0 = r.dtd[rows, lane(j)], r.u[rows, lane(j)], r.gy[rows, lane(j)]
                t0 = jnp.where(t == RESET, 0.0, t)
                gu = [jnp.zeros((V, LN), F32), jnp.zeros((V, LN), F32)]
                gt = [jnp.zeros((V, LN), F32), jnp.zeros((V, LN), F32)]
                for i in range(half):
                    n = n0 + i
                    b = r.bcb[rows, lane(n)].astype(F32)
                    c = r.bcb[rows, lane(N + n)].astype(F32)
                    m = r.m_s[j, rows, lane(n)].astype(F32)
                    pc = g0 * (m + w * b)
                    pb = [None, None]
                    gc = g0 * c
                    for k, p in ((1, BOT), (0, TOP)):
                        g = gs[i] + gc[p]
                        pb[k] = g * w[p]
                        gu[k] = gu[k] + g * b[p]
                        x = g * m[p]
                        gt[k] = gt[k] + x * dn[i]
                        gd[i] = gd[i] + x * t0[p]
                        gs[i] = jnp.exp2(t[p] * dn[i]) * g
                    pb = jnp.concatenate(pb, axis=0)
                    if j > 0:
                        pb = pb + r.x_s[rows, lane(n)].astype(F32)
                        pc = pc + r.x_s[rows, lane(N + n)].astype(F32)
                    r.x_s[rows, lane(n)] = pb.astype(r.x_s.dtype)
                    r.x_s[rows, lane(N + n)] = pc.astype(r.x_s.dtype)
                gu, gt = jnp.concatenate(gu, axis=0), jnp.concatenate(gt, axis=0)
                if n0 > 0:
                    gu = gu + r.gsc[rows, lane(j)]
                    gt = gt + r.y_s[rows, lane(j)]
                r.gsc[rows, lane(j)] = gu
                r.y_s[rows, lane(j)] = gt
                return tuple(gs), tuple(gd)

            zero = tuple(jnp.zeros((V, LN), F32) for _ in range(half))
            first = tuple(r.start[1, row_n(n), lane(j)] for n in range(n0, n0 + half))
            _, gd = lax.fori_loop(0, Q // 2, behind, (first, zero))
            for i in range(half):
                dec = r.dec[n0 + i : n0 + i + 1, lane(j)] * (1.0 / LOG2E)
                r.rowsum[8 + n0 + i : 9 + n0 + i, lane(j)] = (
                    jnp.sum(gd[i], axis=0, keepdims=True) * dec
                )

    def gating(j):
        def body(i, sk):
            rows = pl.ds(pl.multiple_of(i * 64, 64), 64)
            x = r.inp[rows, lane(j)].astype(F32)
            mixed = r.y_s[rows, lane(j)] + r.cp[6:7, lane(j)] * x
            g = r.gate[rows, lane(j)]
            s = sigmoid(g)
            r.gated[rows, lane(j)] = (mixed * (g * s)).astype(BF16)
            r.ggate[rows, lane(j)] = (
                r.gg[rows, lane(j)] * mixed * s * (1.0 + g * (1.0 - s))
            ).astype(BF16)
            p = r.gy[rows, lane(j)] * x
            return sk + jnp.sum(p.reshape(8, V, LN), axis=0)

        sk = lax.fori_loop(0, T // 64, body, jnp.zeros((V, LN), F32))
        r.rowsum[6:7, lane(j)] = jnp.sum(sk, axis=0, keepdims=True)

    r.rowsum[...] = jnp.zeros_like(r.rowsum)
    states = [own_ends(j) for j in range(NB)]
    for c in tots:
        c.wait()
    for j in range(NB):
        begin(j, states[j])
        forward(j)
        gating(j)
        if 0 < j < NB - 1:
            backward(j - 1)
    late = list(range(max(NB - 2, 0), NB))

    def put(dst, first, res):
        n = dst.shape[2]
        for t in range(res.shape[0] // n):
            s = first // n + t
            dst[s % 2, s // 2] = res[t * n : (t + 1) * n].astype(dst.dtype)

    back0 = from_scan(d, 0)
    r.gatn[...] = dot(back0, r.ggate[0:T, :]).astype(BF16)
    for c in range(0, D, LN):
        put(r.giwg, c, dot(r.normed[0:T, c : c + LN], r.gatn[...], 0, 0))
    sum_g = Scatter(net, r.giwg, r.giwg_n, r.giwg_f)
    sum_g.first()
    for j in range(NB):
        put(r.gow, j * LN, dot(r.gated[0:T, lane(j)], r.big[0:T, :], 0, 0))
    sum_o = Scatter(net, r.gow, r.gow_n, r.gow_f)
    sum_o.first()
    r.gated[0:T, :] = dot(back0, r.gated[0:T, :]).astype(BF16)
    for c in range(0, D, 256):
        r.cot[:, c : c + 256] = dot(r.gated[0:T, :], r.ow[:, c : c + 256]).astype(BF16)
    outs = [net.send(rows_of(r.cot, net.at(0, k)[1], tok), r.outr.at[mf], *net.at(0, k)) for k in range(1, F)]
    outs.append(net.local(rows_of(r.cot, mf, tok), r.outr.at[mf]))
    for i, j in enumerate(late):
        backward(j)
        if i == 0:
            sum_g.second()
            sum_o.second()

    def finish(i, acc):
        rows = pl.ds(pl.multiple_of(i * 64, 64), 64)
        out = []
        for j in range(NB):
            x = r.inp[rows, lane(j)].astype(F32)
            z = r.dtpre[rows, lane(j)]
            gu = r.gsc[rows, lane(j)]
            gt = r.y_s[rows, lane(j)] * (1.0 / LOG2E) + gu * x
            dt = jnp.maximum(z, 0.0) + jnp.log1p(jnp.exp(-jnp.abs(z)))
            gz = gt * sigmoid(z)
            r.ggate[rows, lane(j)] = gz.astype(BF16)
            r.gsc[rows, lane(j)] = gu * dt + r.gy[rows, lane(j)] * r.cp[6:7, lane(j)]
            out.append(acc[j] + jnp.sum(gz.reshape(8, V, LN), axis=0))
        return tuple(out)

    db = lax.fori_loop(0, T // 64, finish, tuple(jnp.zeros((V, LN), F32) for _ in range(NB)))
    for j in range(NB):
        r.rowsum[5:6, lane(j)] = jnp.sum(db[j], axis=0, keepdims=True)
    r.gx[:, 0 : d.R] = dot(r.ggate[0:T, :], r.wdt[...]).astype(BF16)
    acc = jnp.zeros((T, 2 * N), F32)
    for n in range(0, 2 * N, 4):
        row = lax.div(lax.broadcasted_iota(jnp.int32, (4 * LN, 2 * N), 0), LN) + n
        col = lax.broadcasted_iota(jnp.int32, (4 * LN, 2 * N), 1)
        pick = jnp.where(row == col, 1.0, 0.0).astype(BF16)
        acc = acc + dot(r.x_s[:, n * LN : (n + 4) * LN].astype(BF16), pick)
    r.gx[:, d.R : W] = acc.astype(BF16)
    gxs = [net.send(r.gx, r.gxr.at[k - 1], *net.at(0, k)) for k in range(1, F)]

    def to_rows(total, out, keep):
        n = total.shape[0] // F
        for f in range(F):
            keep[f] = total[f * n : (f + 1) * n].astype(keep.dtype)
        cs = [net.send(keep.at[net.at(0, k)[1]], out.at[mf], *net.at(0, k)) for k in range(1, F)]
        return cs + [net.local(keep.at[mf], out.at[mf])]

    def to_home(total, keep, out):
        keep[...] = total.astype(keep.dtype)
        i = net.used
        net.used += 2
        far = pltpu.make_async_remote_copy(
            keep, out, r.ssem.at[i], r.rsem.at[i], {"seq": home_s, "fsdp": home_f}, device_id_type=MESH
        )
        near = pltpu.make_async_copy(keep, out, r.rsem.at[i + 1])

        @pl.when(moves)
        def _():
            far.start()

        @pl.when(jnp.logical_not(moves))
        def _():
            near.start()

        return far, near

    def home_wait(pair):
        @pl.when(moves)
        def _():
            pair[0].wait()

        @pl.when(jnp.logical_not(moves))
        def _():
            pair[1].wait()

    g_cs = to_rows(sum_g.total(), r.o_wg, r.k_wg)
    o_cs = to_home(sum_o.total(), r.k_out, r.o_out)
    gwdt = dot(r.ggate[0:T, :], r.xd[:, 0 : d.R], 0, 0)

    for c in gxs:
        c.wait()
    s = r.gx[:, 0:W].astype(F32)
    for k in range(F - 1):
        s = s + r.gxr[k, :, 0:W].astype(F32)
    gxd = s.astype(BF16)
    pad = HG * V
    r.gg[0:pad, :] = jnp.zeros((pad, CL), F32)
    r.gg[pad + T :, :] = jnp.zeros((pad, CL), F32)
    for c in range(0, CL, 256):
        r.gg[pad : pad + T, c : c + 256] = r.gsc[:, c : c + 256] + dot(gxd, r.xp[c : c + 256, :], 1, 1)

    def act(i, acc):
        r0 = pl.multiple_of(i * 64, 64)
        rows = pl.ds(r0, 64)
        shift = pl.ds(pl.multiple_of(r0 + pad, V), 64)
        age = r.rel[shift, :]
        out = []
        for j in range(NB):
            p = r.pre[rows, lane(j)]
            q = sigmoid(p)
            g = r.gg[shift, lane(j)] * q * (1.0 + p * (1.0 - q))
            r.gg[shift, lane(j)] = g
            a = list(acc[j])
            a[4] = a[4] + jnp.sum(g.reshape(8, V, LN), axis=0)
            for k in range(d.K):
                back = d.K - 1 - k
                xs = r.xb[pl.ds(pl.multiple_of(r0 + (HG - back) * V, V), 64), lane(j)]
                t = jnp.where(age >= back, g * xs, 0.0)
                a[k] = a[k] + jnp.sum(t.reshape(8, V, LN), axis=0)
            out.append(tuple(a))
        return tuple(out)

    zero = tuple(tuple(jnp.zeros((V, LN), F32) for _ in range(5)) for _ in range(NB))
    acc = lax.fori_loop(0, T // 64, act, zero)
    for j in range(NB):
        for k in range(5):
            r.rowsum[k : k + 1, lane(j)] = jnp.sum(acc[j][k], axis=0, keepdims=True)

    def gather_taps(i, _):
        r0 = pl.multiple_of(i * 32, 32)
        for j in range(NB):
            acc = jnp.zeros((32, LN), F32)
            for k in range(d.K):
                back = d.K - 1 - k
                src = pl.ds(pl.multiple_of(r0 + back * V, V), 32)
                acc = acc + jnp.where(
                    r.rel[src, :] >= back, r.gg[src, lane(j)] * r.cp[k : k + 1, lane(j)], 0.0
                )
            r.gated[pl.ds(r0, 32), lane(j)] = acc.astype(BF16)
        return 0

    lax.fori_loop(0, d.TE // 32, gather_taps, 0)
    r.ggate[...] = dot(from_scan(d, HG), r.gated[...]).astype(BF16)
    for c in range(0, D, LN):
        put(r.giwx, c, dot(r.normed[:, c : c + LN], r.ggate[...], 0, 0))
    sum_x = Scatter(net, r.giwx, r.giwx_n, r.giwx_f)
    sum_x.first()
    r.y_s[0:CL, 0:LN] = r.rowsum[...].T
    r.y_s[0:CL, LN : LN + W] = dot(r.inp[...], gxd, 0, 0)
    r.y_s[0:CL, LN + W : 2 * LN] = jnp.zeros((CL, LN - W), F32)
    r.y_s[0:CL, 32 : 32 + d.R] = gwdt
    put(r.small, 0, r.y_s[0:CL, 0 : 2 * LN])
    sum_s = Scatter(net, r.small, r.small_n, r.small_f)
    sum_s.first()
    for c in range(0, D, 256):
        g = dot(r.ggate[...], r.w[0, c : c + 256, :], 1, 1)
        r.hid[0:T, c : c + 256] = (
            g[0:T] + dot(r.gatn[...], r.w[1, c : c + 256, :], 1, 1)
        ).astype(BF16)
        r.hid[T:, c : c + 256] = g[T:].astype(BF16)
    gns = [
        net.send(rows_of(r.hid, net.at(0, k)[1], tok), rows_of(r.o_gn, mf, tok), *net.at(0, k))
        for k in range(1, F)
    ]
    gns.append(net.local(rows_of(r.hid, mf, tok), rows_of(r.o_gn, mf, tok)))
    for k in range(F):
        ps, pf = net.at(-1, k)
        gns.append(
            net.send(
                r.hid.at[pl.ds(T + pf * TAIL, TAIL)], r.o_gn.at[pl.ds(T + mf * TAIL, TAIL)], ps, pf
            )
        )
    sum_x.second()
    sum_s.second()

    def gains(i, acc):
        rows = pl.ds(pl.multiple_of(i * 64, 64), 64)
        t = r.hid[rows, :].astype(F32) * r.normed[rows, :].astype(F32)
        return acc + jnp.sum(t.reshape(8, V, D), axis=0)

    gtot = lax.fori_loop(0, d.NAT // 64, gains, jnp.zeros((V, D), F32)) / r.gain[...]
    n = D // S
    for s in range(S):
        r.gg8[s % 2, s // 2] = gtot[:, s * n : (s + 1) * n]
    sum_n = Scatter(net, r.gg8, r.gg8_n, r.gg8_f)
    sum_n.first()
    sum_n.second()
    x_cs = to_rows(sum_x.total(), r.o_wx, r.k_wx)
    s_cs = to_home(sum_s.total(), r.k_small, r.o_small)
    r.k_gain[...] = sum_n.total()
    n_cs = [net.send(r.k_gain, r.o_gain.at[mf], *net.at(0, k)) for k in range(1, F)]
    n_cs.append(net.local(r.k_gain, r.o_gain.at[mf]))
    net.drain()
    home_wait(o_cs)
    home_wait(s_cs)


def close(d, gn, outr, hid, cot, gain, wx, wg, out, small, ggain,
          o_out, o_hid, o_gain, o_in, o_conv, o_rows, o_xp, o_dt, o_al, o_gout):
    F, T, tok, D = d.F, d.T, d.tok, d.D
    W = d.R + 2 * d.N

    def rows_(i, _):
        rows = pl.ds(pl.multiple_of(i * 16, 16), 16)
        h = hid[rows, :].astype(F32)
        g = gn[pl.ds(pl.multiple_of(i * 16, 16), 16), :].astype(F32)
        o = outr[0, rows, :].astype(F32)
        for f in range(1, F):
            g = g + gn[pl.ds(pl.multiple_of(f * tok + i * 16, 16), 16), :].astype(F32)
            o = o + outr[f, rows, :].astype(F32)
        late = jnp.zeros((TAIL, D), F32)
        for f in range(F):
            late = late + gn[T + f * TAIL : T + (f + 1) * TAIL, :].astype(F32)
        g = g + jnp.where(i == tok // 16 - 1, late, 0.0)
        inv = lax.rsqrt(jnp.mean(h * h, axis=-1, keepdims=True) + EPS)
        g2 = g * gain[...]
        mean = jnp.mean(g2 * h, axis=-1, keepdims=True)
        o_hid[0, rows, :] = cot[rows, :].astype(F32) + inv * g2 - h * (inv * inv * inv) * mean
        o_out[0, rows, :] = (h + o).astype(BF16)
        return 0

    lax.fori_loop(0, tok // 16, rows_, 0)
    for f in range(F):
        o_in[:, f * d.CL : (f + 1) * d.CL] = wx[f].astype(F32)
        o_in[:, d.DI + f * d.CL : d.DI + (f + 1) * d.CL] = wg[f].astype(F32)
    o_gout[...] = out[...].astype(F32)
    sm = small[...]
    o_conv[...] = sm[:, 0 : d.K]
    o_al[...] = sm[:, V : V + d.N]
    o_dt[...] = sm[:, 32 : 32 + d.R]
    o_xp[...] = sm[:, LN : LN + W]
    o_rows[...] = sm[:, 0:LN].T[0:V, :]
    tot = ggain[0]
    for f in range(1, F):
        tot = tot + ggain[f]
    n, k = D // d.S, D // d.S // F
    row = lax.broadcasted_iota(jnp.int32, (n, k), 0) - lax.axis_index("fsdp") * k
    pick = jnp.where(row == lax.broadcasted_iota(jnp.int32, (n, k), 1), 1.0, 0.0)
    one = lax.dot_general(
        jnp.sum(tot, axis=0, keepdims=True) + jnp.zeros((V, n), F32), pick, (((1,), (0,)), ((), ())),
        precision=lax.Precision.HIGHEST, preferred_element_type=F32,
    )
    o_gain[...] = one[0:1, :]


def vm(*shape, dtype=F32):
    return pltpu.VMEM(shape, dtype)


def per_device(
    d, hidden, cluster_lengths, norm_gain, in_weight, conv_weight, conv_bias, xproj_weight,
    dt_weight, dt_bias, a_log, skip, out_weight, cotangent,
):
    S, F, T, D, CL, N, NB, R = d.S, d.F, d.T, d.D, d.CL, d.N, d.NB, d.R
    wide = lambda a: jnp.pad(a.astype(F32), (0, CL - a.shape[0]))
    params = jnp.stack(
        [conv_bias.astype(F32), dt_bias.astype(F32), skip.astype(F32), wide(norm_gain),
         wide(cluster_lengths[0])] + [jnp.zeros((CL,), F32)] * (V - 5)
    )
    ins = dict(
        hidden=hidden[0], params=params, in_weight=in_weight, conv_weight=conv_weight,
        xproj_weight=xproj_weight, dt_weight=dt_weight, a_log=a_log, out_weight=out_weight,
        cotangent=cotangent[0],
    )
    DS, CS, W, W2 = D // S, CL // S, R + 2 * N, 2 * LN
    TP = T + 2 * HG * V
    outs = dict(
        o_gn=((d.NAT, D), BF16), outr=((F, d.tok, D), BF16), gain=((1, D), F32),
        o_wx=((F, DS // F, CL), BF16), o_wg=((F, DS // F, CL), BF16), o_out=((CS, D), F32),
        o_small=((CS, W2), F32), o_gain=((F, V, DS), F32),
    )
    rt = BF16 if CS >= 16 else F32
    small_t = T <= 512
    half = S // 2
    EP = N // d.H * V
    scratch = dict(
        hid=((d.NAT, D), BF16), normed=((d.NAT, D), BF16), big=((d.TE, D), BF16),
        cot=((T, D), BF16), w=((2, D, CL), BF16), ow=((CL, D), BF16),
        xp=((CL, W), BF16), wdt=((CL, R), BF16), cw=((CL, d.K), BF16), al=((CL, N), BF16),
        pg=((F, V, CL), F32), cp=((V, CL), F32), dec=((N, CL), F32), rel=((TP, LN), F32),
        xb=((d.TE, CL), F32), gate=((T, CL), F32), pre=((T, CL), F32), inp=((T, CL), BF16),
        xd=((T, LN), BF16), xdr=((F - 1, T, LN), BF16),
        dtpre=((T, CL), F32), dtd=((T, CL), F32), u=((T, CL), F32), gg=((TP, CL), F32),
        gy=((T, CL), F32), bcb=((T, 2 * N * LN), F32 if small_t else BF16),
        sd=((V, CL), F32), tot=((V, CL), F32), totr=((S - 1, V, CL), F32),
        ends=((2, N * V, CL), F32), epack=((2, NB, EP, LN), BF16), eget=((NB, S, EP, LN), BF16),
        start=((2, N * V, CL), F32), m_s=((NB, T, N * LN), BF16), y_s=((T, CL), F32),
        gsc=((T, CL), F32), x_s=((T, 2 * N * LN), F32 if small_t else BF16),
        gated=((d.TE, CL), BF16), ggate=((d.NAT, CL), BF16), gatn=((T, CL), BF16),
        gx=((T, LN), BF16), gxr=((F - 1, T, LN), BF16), rowsum=((LN, CL), F32),

        giwg=((2, half, DS, CL), BF16), giwg_n=((half, DS, CL), BF16), giwg_f=((half - 1, DS, CL), BF16),
        giwx=((2, half, DS, CL), BF16), giwx_n=((half, DS, CL), BF16), giwx_f=((half - 1, DS, CL), BF16),
        gow=((2, half, CS, D), rt), gow_n=((half, CS, D), rt), gow_f=((half - 1, CS, D), rt),
        small=((2, half, CS, W2), rt), small_n=((half, CS, W2), rt), small_f=((half - 1, CS, W2), rt),
        gg8=((2, half, V, DS), F32), gg8_n=((half, V, DS), F32), gg8_f=((half - 1, V, DS), F32),
        k_wg=((F, DS // F, CL), BF16), k_wx=((F, DS // F, CL), BF16), k_out=((CS, D), F32),
        k_small=((CS, W2), F32), k_gain=((V, DS), F32),
    )
    names = list(ins) + list(outs) + list(scratch) + ["ssem", "rsem"]
    sems = 160 + (NB + 6) * S + 12 * F
    res = pl.pallas_call(
        functools.partial(layer, d, names),
        out_shape=[jax.ShapeDtypeStruct(*o) for o in outs.values()],
        in_specs=[pl.BlockSpec(memory_space=pl.ANY)] * len(ins),
        out_specs=[
            pl.BlockSpec(memory_space=pltpu.VMEM if k == "gain" else pl.ANY) for k in outs
        ],
        scratch_shapes=[vm(*s, dtype=t) for s, t in scratch.values()]
        + [pltpu.SemaphoreType.DMA((sems,)), pltpu.SemaphoreType.DMA((sems,))],
        compiler_params=pltpu.CompilerParams(
            collective_id=0, has_side_effects=True, vmem_limit_bytes=65250 * 1024
        ),
    )(*ins.values())
    o = dict(zip(outs, res))
    fin = kernel(
        functools.partial(close, d),
        (o["o_gn"], o["outr"], hidden[0], cotangent[0], o["gain"], o["o_wx"], o["o_wg"], o["o_out"],
         o["o_small"], o["o_gain"]),
        [((1, d.tok, D), BF16), ((1, d.tok, D), F32), ((1, DS // F), F32), ((DS // F, 2 * d.DI), F32),
         ((CS, d.K), F32), ((V, CS), F32), ((CS, W), F32), ((CS, R), F32), ((CS, N), F32), ((CS, D), F32)],
    )
    out, g_hid, g_gain, g_in, g_conv, rows, g_xp, g_dt, g_al, g_out = fin
    return (
        out, g_hid, g_gain[0], g_in, g_conv, rows[4], g_xp, g_dt, rows[5], g_al, rows[6], g_out,
    )


def solution(mesh):
    S, F = mesh.shape["seq"], mesh.shape["fsdp"]

    def run(*args):
        tok, D = args[0].shape[1] // S, args[0].shape[2]
        d = Dims(
            S, F, tok, D, args[11].shape[0], args[9].shape[1], args[7].shape[1], args[4].shape[1],
            args[1].shape[1],
        )
        return jax.shard_map(
            functools.partial(per_device, d),
            mesh=mesh,
            in_specs=(
                P("fsdp", "seq", None), P("fsdp", None), P("fsdp"), P("fsdp", None),
                P("fsdp", None), P("fsdp"), P("fsdp", None), P("fsdp", None), P("fsdp"),
                P("fsdp", None), P("fsdp"), P("fsdp", None), P("fsdp", "seq", None),
            ),
            out_specs=(
                P("fsdp", "seq", None), P("fsdp", "seq", None), P(("seq", "fsdp")),
                P(("seq", "fsdp"), None), P(("seq", "fsdp"), None), P(("seq", "fsdp")),
                P(("seq", "fsdp"), None), P(("seq", "fsdp"), None), P(("seq", "fsdp")),
                P(("seq", "fsdp"), None), P(("seq", "fsdp")), P(("seq", "fsdp"), None),
            ),
            check_vma=False,
        )(*args)

    return run
```

```python
import functools
import math

import jax
import jax.numpy as jnp
from jax import lax
from jax.experimental import pallas as pl
from jax.experimental.pallas import tpu as pltpu
from jax.sharding import PartitionSpec as P

EPS = 1e-05
V = 8
LN = 128
HG = 4
TAIL = 16
LOG2E = 1.0 / math.log(2.0)
RESET = 1e30
F32 = jnp.float32
TOP, BOT = slice(0, V), slice(V, 2 * V)
BF16 = jnp.bfloat16
MESH = pl.DeviceIdType.MESH


class Dims:
    def __init__(self, S, F, tok, D, DI, N, R, K, clusters):
        self.S, self.F, self.tok, self.D, self.DI = S, F, tok, D, DI
        self.N, self.R, self.K, self.clusters = N, R, K, clusters
        self.H = V // F
        self.Q = tok // self.H
        self.T = F * tok
        self.TE = (self.Q + HG) * V
        self.NAT = F * (tok + TAIL)
        self.CL = DI // F
        self.NB = self.CL // LN


def dot(a, b, ca=1, cb=0):
    return lax.dot_general(a, b, (((ca,), (cb,)), ((), ())), preferred_element_type=F32)


def sigmoid(v):
    return 1.0 / (1.0 + jnp.exp(-v))


def kernel(body, args, outs, scratch=()):
    return pl.pallas_call(
        body,
        out_shape=[jax.ShapeDtypeStruct(s, t) for s, t in outs],
        in_specs=[pl.BlockSpec(memory_space=pltpu.VMEM)] * len(args),
        out_specs=[pl.BlockSpec(memory_space=pltpu.VMEM)] * len(outs),
        scratch_shapes=list(scratch),
        compiler_params=pltpu.CompilerParams(vmem_limit_bytes=60 * 1024 * 1024),
    )(*args)


def lane(j):
    return slice(j * LN, (j + 1) * LN)


def natural_of(d, row, halo):
    q = lax.div(row, V) - halo
    v = lax.rem(row, V)
    f = lax.div(v, d.H)
    p = lax.rem(v, d.H) * d.Q + q
    return jnp.where(p >= 0, f * d.tok + p, d.T + f * TAIL + TAIL + p)


def to_scan(d, halo):
    rows, cols = (d.TE, d.NAT) if halo else (d.T, d.T)
    want = natural_of(d, lax.broadcasted_iota(jnp.int32, (rows, 1), 0), halo)
    have = lax.broadcasted_iota(jnp.int32, (rows, cols), 1)
    return jnp.where(have == want, 1.0, 0.0).astype(BF16)


def from_scan(d, halo):
    rows, cols = (d.NAT, d.TE) if halo else (d.T, d.T)
    want = natural_of(d, lax.broadcasted_iota(jnp.int32, (1, cols), 1), halo)
    have = lax.broadcasted_iota(jnp.int32, (rows, cols), 0)
    return jnp.where(have == want, 1.0, 0.0).astype(BF16)


class Refs:
    pass


class Copy:
    def __init__(self, copy, remote):
        self.copy, self.sent, self.got = copy, not remote, False
        self.remote = remote

    def wait_send(self):
        if not self.sent:
            self.copy.wait_send()
            self.sent = True

    def wait_recv(self):
        if not self.got:
            if self.remote:
                self.copy.wait_recv()
            else:
                self.copy.wait()
            self.got = True

    def wait(self):
        self.wait_send()
        self.wait_recv()


class Batch:
    def __init__(self, net, sends, whole):
        i, j = net.pair()
        self.open = True
        for src, dst, ps, pf in sends:
            net.remote(src, dst, i, j, ps, pf).start()
        self.all = net.remote(whole, whole, i, j, *net.at(0, 1))

    def wait(self):
        if self.open:
            self.all.wait_send()
            self.all.wait_recv()
            self.open = False


class Net:
    def __init__(self, d, ssem, rsem):
        self.d, self.ssem, self.rsem, self.s_used, self.r_used = d, ssem, rsem, 0, 0
        self.ms, self.mf = lax.axis_index("seq"), lax.axis_index("fsdp")
        self.open = []

    def at(self, ds, df):
        return lax.rem(self.ms + ds % self.d.S, self.d.S), lax.rem(self.mf + df % self.d.F, self.d.F)

    def pair(self):
        self.s_used += 1
        self.r_used += 1
        return self.s_used - 1, self.r_used - 1

    def remote(self, src, dst, i, j, ps, pf):
        return pltpu.make_async_remote_copy(
            src, dst, self.ssem.at[i], self.rsem.at[j], {"seq": ps, "fsdp": pf}, device_id_type=MESH
        )

    def start(self, copy, remote):
        copy.start()
        self.open.append(Copy(copy, remote))
        return self.open[-1]

    def send(self, src, dst, ps, pf):
        i, j = self.pair()
        return self.start(self.remote(src, dst, i, j, ps, pf), True)

    def batch(self, sends, whole):
        self.open.append(Batch(self, sends, whole))
        return self.open[-1]

    def local(self, src, dst):
        self.r_used += 1
        return self.start(pltpu.make_async_copy(src, dst, self.rsem.at[self.r_used - 1]), False)

    def drain(self):
        for c in self.open:
            c.wait()


class Scatter:
    def __init__(self, net, mine, near, out, spread, split=True):
        self.net, self.mine, self.near, self.out_ref = net, mine, near, out
        self.spread, self.split = spread, split
        d = net.d
        self.half = d.S // 2
        self.x, self.z = lax.rem(net.ms, 2), lax.div(net.ms, 2)
        self.pal = net.ms + 1 - 2 * self.x
        self.order = [lax.rem(self.z + k, self.half) for k in list(range(1, self.half)) + [0]]
        self.first = [
            net.send(mine.at[1 - self.x, z], near.at[z], self.pal, net.mf) for z in self.order
        ]
        self.done, self.tails = 0, []
        self.into = net.r_used
        net.r_used += 1
        net.open.append(self)

    def step(self, upto=None):
        net, d = self.net, self.net.d
        upto = self.half if upto is None else upto
        while self.done < upto:
            k, z = self.done, self.order[self.done]
            self.done += 1
            self.first[k].wait()
            both = self.mine[self.x, z].astype(F32) + self.near[z].astype(F32)
            self.mine[self.x, z] = both.astype(self.mine.dtype)
            i = net.s_used
            net.s_used += 1
            if self.spread:
                last = k == self.half - 1
                for g in range(1, d.F + (0 if last else 1)):
                    f = lax.rem(net.mf + g, d.F)
                    src = self.mine.at[self.x, z, f] if self.split else self.mine.at[self.x, z]
                    net.remote(
                        src, self.out_ref.at[k, net.mf], i, self.into, z * 2 + self.x, f
                    ).start()
                if last:
                    src = self.mine.at[self.x, z, net.mf] if self.split else self.mine.at[self.x, z]
                    pltpu.make_async_copy(
                        src, self.out_ref.at[k, net.mf], net.rsem.at[self.into]
                    ).start()
                sent = self.out_ref.at[k, pl.ds(0, d.F - 1)] if last else self.out_ref.at[k]
                self.tails.append((None, net.remote(sent, sent, i, self.into, *net.at(0, 1))))
            else:
                spot = net.mf * d.S + z * 2 + self.x
                away = spot != net.ms * d.F + net.mf
                src, dst = self.mine.at[self.x, z], self.out_ref.at[self.z]
                far = net.remote(src, dst, i, self.into, lax.div(spot, d.F), lax.rem(spot, d.F))
                near = pltpu.make_async_copy(src, dst, net.rsem.at[self.into])
                pl.when(away)(far.start)
                pl.when(jnp.logical_not(away))(near.start)
                self.tails.append((away, far))

    def wait(self):
        for away, c in self.tails:
            if away is None:
                c.wait_send()
            else:
                pl.when(away)(c.wait_send)
        net = self.net
        net.remote(self.out_ref, self.out_ref, 0, self.into, *net.at(0, 1)).wait_recv()


def layer(d, names, *refs):
    r = Refs()
    for name, ref in zip(names, refs):
        setattr(r, name, ref)
    S, F, CL, T, N, Q, NB, D, tok, H = d.S, d.F, d.CL, d.T, d.N, d.Q, d.NB, d.D, d.tok, d.H
    DF = D // F
    net = Net(d, r.ssem, r.rsem)
    ms, mf = net.ms, net.mf
    core = mf + 1 - 2 * lax.rem(mf, 2)
    greet = [(i, k) for i in range(S) for k in range(F) if (i, k) != (0, 0)]
    bar = pltpu.get_barrier_semaphore()
    for ds, df in greet:
        ps, pf = net.at(-ds, -df)
        pl.semaphore_signal(bar, inc=1, device_id={"seq": ps, "fsdp": pf}, device_id_type=MESH)

    own = [
        net.local(r.hidden, r.hid.at[pl.ds(mf * tok, tok)]),
        net.local(r.norm_gain, r.row_g),
        net.local(r.in_weight.at[:, pl.ds(pl.multiple_of(mf * CL, LN), CL)], r.w.at[0, pl.ds(mf * DF, DF)]),
        net.local(
            r.in_weight.at[:, pl.ds(pl.multiple_of(d.DI + mf * CL, LN), CL)],
            r.w.at[1, pl.ds(mf * DF, DF)],
        ),
        net.local(r.cotangent, r.cot.at[pl.ds(mf * tok, tok)]),
        net.local(r.out_weight, r.ow),
        net.local(r.xproj_weight, r.xp),
        net.local(r.dt_weight, r.wdt),
        net.local(r.conv_weight, r.cw),
        net.local(r.a_log, r.al),
        net.local(r.lens, r.row_l),
        net.local(r.conv_bias, r.row_cb),
        net.local(r.dt_bias, r.row_db),
        net.local(r.skip, r.row_sk),
    ]
    pl.semaphore_wait(bar, len(greet))

    rows_of = lambda ref, f, n: ref.at[pl.ds(f * n, n)]
    same_core = [lax.rem(mf + 2 * k, F) for k in range(1, F // 2)]
    other_chip = [(lax.rem(mf + 2 * k, F), lax.rem(core + 2 * k, F)) for k in range(1, F // 2)]

    for i in (1, 10):
        own[i].wait()
    as_row = lambda ref: ref[...].astype(F32).reshape(1, ref.shape[-1])
    r.pg_own[0:1, :] = as_row(r.row_g)
    r.pg_own[1:2, 0 : d.clusters] = as_row(r.row_l)
    r.pg[mf] = r.pg_own[...]

    def spread_rows(src, dst):
        direct = [net.send(src, rows_of(dst, mf, tok), ms, f) for f in same_core]
        beside = [net.send(src, rows_of(dst, mf, tok), ms, core)]
        return direct, beside

    def relay_rows(dst, direct, beside):
        for k, c in enumerate(direct):
            c.wait()
            f = lax.rem(mf + F - 2 * (k + 1), F)
            beside.append(net.send(rows_of(dst, f, tok), rows_of(dst, f, tok), ms, core))

    def w_slice(g, f):
        return r.in_weight.at[:, pl.ds(pl.multiple_of(g * d.DI + f * CL, LN), CL)]

    quart, ring = lax.rem(ms, 4), ms - lax.rem(ms, 4)
    QF = DF // 4

    def w_far(g):
        out = []
        for pair in other_chip:
            for f in pair:
                src = r.in_weight.at[
                    pl.ds(quart * QF, QF), pl.ds(pl.multiple_of(g * d.DI + f * CL, LN), CL)
                ]
                out.append(net.send(src, r.w.at[g, pl.ds(mf * DF + quart * QF, QF)], ms, f))
        return out

    def w_relay(g, far):
        out = []
        i = 0
        for k in range(1, F // 2):
            for flip in (0, 1):
                far[i].wait_recv()
                i += 1
                f0 = lax.rem(mf + F - 2 * k, F)
                if flip:
                    f0 = f0 + 1 - 2 * lax.rem(f0, 2)
                place = r.w.at[g, pl.ds(f0 * DF + quart * QF, QF)]
                for t in (1, 2, 3):
                    out.append(net.send(place, place, ring + lax.rem(quart + t, 4), mf))
        return out

    wx_far = w_far(0)
    pgs = [net.send(r.pg_own, r.pg.at[mf], *net.at(0, k)) for k in range(1, F)]
    w_beside = [net.send(w_slice(g, core), r.w.at[g, pl.ds(mf * DF, DF)], ms, core) for g in (0, 1)]
    for c in wx_far:
        c.wait_send()
    h_direct, h_beside = spread_rows(r.hidden, r.hid)
    halo = [
        net.send(
            r.hidden.at[pl.ds(tok - TAIL, TAIL)],
            r.hid.at[pl.ds(T + mf * TAIL, TAIL)],
            *net.at(1, k),
        )
        for k in range(F)
    ]
    wx_near = w_relay(0, wx_far)
    for c in pgs + own[:1]:
        c.wait()
    for f in range(F):
        r.gain[0:1, f * DF : (f + 1) * DF] = r.pg[f, 0:1, :]
    sub = lax.broadcasted_iota(jnp.int32, (V, LN), 0)
    hidx = lax.rem(sub, H)
    stream = lax.div(sub, H)
    offs, run = [], jnp.zeros((V, LN), F32)
    for j in range(d.clusters - 1):
        for f in range(F):
            run = run + jnp.where(stream == f, r.pg[f, 1:2, j : j + 1], 0.0)
        offs.append(run)
    base = ms * tok + hidx * Q
    r.rel[0 : HG * V, :] = jnp.zeros((HG * V, LN), F32)
    r.rel[HG * V + T :, :] = jnp.zeros((HG * V, LN), F32)

    def mark(q, _):
        pos = (base + q).astype(F32)
        last = jnp.zeros((V, LN), F32)
        for o in offs:
            last = jnp.maximum(last, jnp.where(o <= pos, o, 0.0))
        r.rel[pl.ds(pl.multiple_of((q + HG) * V, V), V), :] = jnp.where(pos == 0.0, 0.5, pos - last)
        return 0

    lax.fori_loop(0, Q, mark, 0)
    for c in own[8:]:
        c.wait()
    r.cp[0 : d.K, :] = r.cw[...].astype(F32)
    for i, ref in enumerate((r.row_cb, r.row_db, r.row_sk)):
        r.cp[4 + i : 5 + i, :] = as_row(ref)
    r.dec[...] = -LOG2E * jnp.exp(r.al[...].astype(F32))
    for c in h_direct:
        c.wait_send()
    c_direct, c_beside = spread_rows(r.cotangent, r.cot)
    for k, c in enumerate(h_direct):
        c.wait_recv()
        f = lax.rem(mf + F - 2 * (k + 1), F)
        h_beside.append(net.send(rows_of(r.hid, f, tok), rows_of(r.hid, f, tok), ms, core))
    for c in h_beside + halo:
        c.wait()

    def rms(i, _):
        rows = pl.ds(pl.multiple_of(i * 64, 64), 64)
        h = r.hid[rows, :].astype(F32)
        inv = lax.rsqrt(jnp.mean(h * h, axis=-1, keepdims=True) + EPS)
        r.normed[rows, :] = (h * inv * r.gain[...]).astype(BF16)
        return 0

    lax.fori_loop(0, d.NAT // 64, rms, 0)
    perm = to_scan(d, HG)
    for c in range(0, D, 256):
        r.big[:, c : c + 256] = dot(perm, r.normed[:, c : c + 256]).astype(BF16)
    wg_far = w_far(1)
    own[2].wait()
    w_beside[0].wait()
    for c in wx_near:
        c.wait()
    for c in range(0, CL, 256):
        r.xb[:, c : c + 256] = (
            dot(r.big[:, :], r.w[0, :, c : c + 256]).astype(BF16).astype(F32)
        )

    def conv(i, _):
        r0 = pl.multiple_of(i * 64, 64)
        rows = pl.ds(r0, 64)
        age = r.rel[pl.ds(pl.multiple_of(r0 + HG * V, V), 64), :]
        for j in range(NB):
            acc = jnp.zeros((64, LN), F32) + r.cp[4:5, lane(j)]
            for k in range(d.K):
                back = d.K - 1 - k
                xs = r.xb[pl.ds(pl.multiple_of(r0 + (HG - back) * V, V), 64), lane(j)]
                acc = acc + jnp.where(age >= back, xs * r.cp[k : k + 1, lane(j)], 0.0)
            r.pre[rows, lane(j)] = acc
            r.inp[rows, lane(j)] = (acc * sigmoid(acc)).astype(BF16)
        return 0

    lax.fori_loop(0, T // 64, conv, 0)
    own[6].wait()
    W = d.R + 2 * N
    r.xd[:, 0:W] = dot(r.inp[...], r.xp[...], 1, 1).astype(BF16)
    xd_near = net.send(r.xd, r.xdn, ms, core)

    def chips(src, near_copy, near, far):
        near_copy.wait()
        src[...] = (src[...].astype(F32) + near[...].astype(F32)).astype(BF16)
        return net.batch([(src, far.at[k - 1], *net.at(0, 2 * k)) for k in range(1, F // 2)], far)

    def chips_total(src, batch, far):
        batch.wait()
        tot = src[:, 0:W].astype(F32)
        for k in range(F // 2 - 1):
            tot = tot + far[k, :, 0:W].astype(F32)
        return tot

    xd_far = chips(r.xd, xd_near, r.xdn, r.xdr)
    wg_near = w_relay(1, wg_far)
    relay_rows(r.cot, c_direct, c_beside)
    for c in [own[3], own[4], own[5], w_beside[1]] + wg_near + c_beside:
        c.wait()
    for c in range(0, CL, 256):
        r.gate[:, c : c + 256] = dot(r.big[HG * V :, :], r.w[1, :, c : c + 256])
    perm = to_scan(d, 0)
    for c in range(0, D, 256):
        r.big[0:T, c : c + 256] = dot(perm, r.cot[:, c : c + 256]).astype(BF16)
    for c in range(0, CL, 256):
        r.gg[0:T, c : c + 256] = dot(r.big[0:T, :], r.ow[c : c + 256, :], 1, 1)

    def gys(i, _):
        rows = pl.ds(pl.multiple_of(i * 64, 64), 64)
        for j in range(NB):
            g = r.gate[rows, lane(j)]
            r.gy[rows, lane(j)] = r.gg[rows, lane(j)] * (g * sigmoid(g))
        return 0

    lax.fori_loop(0, T // 64, gys, 0)
    xd = chips_total(r.xd, xd_far, r.xdr)
    own[7].wait()
    low = xd[:, : d.R].astype(BF16)
    r.xd[:, 0 : d.R] = low
    for c in range(0, CL, 256):
        r.dtpre[:, c : c + 256] = dot(low, r.wdt[:, c : c + 256])

    def steps(i, acc):
        rows = pl.ds(pl.multiple_of(i * 64, 64), 64)
        age = r.rel[pl.ds(pl.multiple_of(i * 64 + HG * V, V), 64), :]
        out = []
        for j in range(NB):
            z = r.dtpre[rows, lane(j)] + r.cp[5:6, lane(j)]
            dt = jnp.maximum(z, 0.0) + jnp.log1p(jnp.exp(-jnp.abs(z)))
            r.dtpre[rows, lane(j)] = z
            e = jnp.where(age == 0.0, RESET, dt)
            r.dtd[rows, lane(j)] = e
            r.u[rows, lane(j)] = dt * r.inp[rows, lane(j)].astype(F32)
            out.append(acc[j] + jnp.sum(e.reshape(8, V, LN), axis=0))
        return tuple(out)

    sums = lax.fori_loop(0, T // 64, steps, tuple(jnp.zeros((V, LN), F32) for _ in range(NB)))
    for j in range(NB):
        whole, t = sums[j], 1
        while t < H:
            low_half = lax.rem(lax.div(hidx, t), 2) == 0
            whole = whole + jnp.where(low_half, pltpu.roll(whole, V - t, 0), pltpu.roll(whole, t, 0))
            t *= 2
        r.sd[0:V, lane(j)] = sums[j]
        r.tot[:, lane(j)] = whole
    tots = net.batch([(r.tot, r.totr.at[k - 1], *net.at(k, 0)) for k in range(1, S)], r.totr)
    bc = xd[:, d.R : W]
    hi = bc.astype(BF16)
    rest = (bc - hi.astype(F32)).astype(BF16)
    both = jnp.concatenate([hi, rest], axis=1)
    for n in range(0, 2 * N, 4):
        row = lax.rem(lax.broadcasted_iota(jnp.int32, (4 * N, 4 * LN), 0), 2 * N)
        col = lax.div(lax.broadcasted_iota(jnp.int32, (4 * N, 4 * LN), 1), LN) + n
        pick = jnp.where(row == col, 1.0, 0.0).astype(BF16)
        r.bcb[:, n * LN : (n + 4) * LN] = dot(both, pick).astype(r.bcb.dtype)

    half = N // 2
    row_n = lambda n: slice(n * V, (n + 1) * V)
    dec_of = lambda n, j: jnp.broadcast_to(r.dec[n : n + 1, lane(j)], (V, LN))

    def own_ends(j):
        for n0 in range(0, N, half):
            dn = [dec_of(n, j) for n in range(n0, n0 + half)]

            def local(q, carry, n0=n0, dn=dn):
                hs, gs = list(carry[0]), list(carry[1])
                up = pl.ds(pl.multiple_of(q * 2 * V, 2 * V), 2 * V)
                down = pl.ds(pl.multiple_of((Q - 2 - 2 * q) * V, 2 * V), 2 * V)
                a_dt, a_u = r.dtd[up, lane(j)], r.u[up, lane(j)]
                b_dt, b_gy = r.dtd[down, lane(j)], r.gy[down, lane(j)]
                for i in range(half):
                    b = r.bcb[up, lane(n0 + i)].astype(F32)
                    c = r.bcb[down, lane(N + n0 + i)].astype(F32)
                    for t in (TOP, BOT):
                        hs[i] = jnp.exp2(a_dt[t] * dn[i]) * hs[i] + a_u[t] * b[t]
                    for t in (BOT, TOP):
                        gs[i] = jnp.exp2(b_dt[t] * dn[i]) * (gs[i] + b_gy[t] * c[t])
                return tuple(hs), tuple(gs)

            zero = tuple(jnp.zeros((V, LN), F32) for _ in range(half))
            hs, gs = lax.fori_loop(0, Q // 2, local, (zero, zero))
            for i in range(half):
                r.ends[0, row_n(n0 + i), lane(j)] = hs[i]
                r.ends[1, row_n(n0 + i), lane(j)] = gs[i]
        one = r.sd[0:V, lane(j)]
        fw, bw = [], []
        for n0 in range(0, N, H):
            a, b = jnp.zeros((V, LN), F32), jnp.zeros((V, LN), F32)
            for t in range(H):
                fac = jnp.exp2(one * dec_of(n0 + t, j))
                e, g = r.ends[0, row_n(n0 + t), lane(j)], r.ends[1, row_n(n0 + t), lane(j)]
                x, y = e, g
                for h in range(1, H):
                    x = jnp.where(hidx == h, fac * pltpu.roll(x, 1, 0) + e, x)
                    y = jnp.where(hidx == H - 1 - h, fac * pltpu.roll(y, V - 1, 0) + g, y)
                a = jnp.where(hidx == t, turn(x, t - (H - 1)), a)
                b = jnp.where(hidx == t, turn(y, t), b)
            fw.append(a)
            bw.append(b)
        for i in range(0, len(fw), 2):
            band = slice(i * V, (i + 2) * V)
            r.epack[0, j, band, :] = jnp.concatenate(fw[i : i + 2], axis=0).astype(BF16)
            r.epack[1, j, band, :] = jnp.concatenate(bw[i : i + 2], axis=0).astype(BF16)
        out = []
        for k in range(1, S):
            ps, pf = net.at(k, 0)
            out.append((r.epack.at[jnp.where(ps > ms, 0, 1), j], r.eget.at[j, k - 1], ps, pf))
        return net.batch(out, r.eget.at[j])

    def turn(x, by):
        return x if by % V == 0 else pltpu.roll(x, by % V, 0)

    def begin(j, copies):
        copies.wait()
        tiles = N // H
        dn = []
        for i in range(tiles):
            x = dec_of(i * H, j)
            for t in range(1, H):
                x = jnp.where(hidx == t, dec_of(i * H + t, j), x)
            dn.append(x)

        def join(p, acc):
            slot = lax.rem(ms + S - p, S) - 1
            tot = r.totr[slot, :, lane(j)]
            e = r.eget[j, slot].astype(F32)
            return tuple(jnp.exp2(tot * dn[i]) * acc[i] + e[row_n(i)] for i in range(tiles))

        zero = tuple(jnp.zeros((V, LN), F32) for _ in range(tiles))
        fw = lax.fori_loop(0, ms, join, zero)
        bw = lax.fori_loop(0, S - 1 - ms, lambda i, acc: join(S - 1 - i, acc), zero)
        one = r.sd[0:V, lane(j)]
        for i in range(tiles):
            for t in range(H):
                n = i * H + t
                fac = jnp.exp2(one * dec_of(n, j))
                x, y = turn(fw[i], -t), turn(bw[i], H - 1 - t)
                for h in range(1, H):
                    xn = pltpu.roll(fac * x + r.ends[0, row_n(n), lane(j)], 1, 0)
                    yn = pltpu.roll(fac * y + r.ends[1, row_n(n), lane(j)], V - 1, 0)
                    x = jnp.where(hidx == h, xn, x)
                    y = jnp.where(hidx == H - 1 - h, yn, y)
                r.start[0, row_n(n), lane(j)] = x
                r.start[1, row_n(n), lane(j)] = y

    def forward(j):
        dn = [dec_of(n, j) for n in range(N)]

        def ahead(q, hs):
            hs = list(hs)
            rows = pl.ds(pl.multiple_of(q * 2 * V, 2 * V), 2 * V)
            t, w = r.dtd[rows, lane(j)], r.u[rows, lane(j)]
            y = [jnp.zeros((V, LN), F32), jnp.zeros((V, LN), F32)]
            for n in range(N):
                b = r.bcb[rows, lane(n)].astype(F32)
                c = r.bcb[rows, lane(N + n)].astype(F32)
                keep = []
                for k, p in enumerate((TOP, BOT)):
                    m = jnp.exp2(t[p] * dn[n]) * hs[n]
                    hs[n] = m + w[p] * b[p]
                    y[k] = y[k] + c[p] * hs[n]
                    keep.append(m)
                r.m_s[j, rows, lane(n)] = jnp.concatenate(keep, axis=0).astype(BF16)
            r.y_s[rows, lane(j)] = jnp.concatenate(y, axis=0)
            return tuple(hs)

        lax.fori_loop(0, Q // 2, ahead, tuple(r.start[0, row_n(n), lane(j)] for n in range(N)))

    def backward(j):
        for n0 in range(0, N, half):
            dn = [dec_of(n, j) for n in range(n0, n0 + half)]

            def behind(i, carry, n0=n0, dn=dn):
                gs, gd = list(carry[0]), list(carry[1])
                rows = pl.ds(pl.multiple_of((Q - 2 - 2 * i) * V, 2 * V), 2 * V)
                t, w, g0 = r.dtd[rows, lane(j)], r.u[rows, lane(j)], r.gy[rows, lane(j)]
                t0 = jnp.where(t == RESET, 0.0, t)
                gu = [jnp.zeros((V, LN), F32), jnp.zeros((V, LN), F32)]
                gt = [jnp.zeros((V, LN), F32), jnp.zeros((V, LN), F32)]
                for i in range(half):
                    n = n0 + i
                    b = r.bcb[rows, lane(n)].astype(F32)
                    c = r.bcb[rows, lane(N + n)].astype(F32)
                    m = r.m_s[j, rows, lane(n)].astype(F32)
                    pc = g0 * (m + w * b)
                    pb = [None, None]
                    gc = g0 * c
                    for k, p in ((1, BOT), (0, TOP)):
                        g = gs[i] + gc[p]
                        pb[k] = g * w[p]
                        gu[k] = gu[k] + g * b[p]
                        x = g * m[p]
                        gt[k] = gt[k] + x * dn[i]
                        gd[i] = gd[i] + x * t0[p]
                        gs[i] = jnp.exp2(t[p] * dn[i]) * g
                    pb = jnp.concatenate(pb, axis=0)
                    if j > 0:
                        pb = pb + r.x_s[rows, lane(n)].astype(F32)
                        pc = pc + r.x_s[rows, lane(N + n)].astype(F32)
                    r.x_s[rows, lane(n)] = pb.astype(r.x_s.dtype)
                    r.x_s[rows, lane(N + n)] = pc.astype(r.x_s.dtype)
                gu, gt = jnp.concatenate(gu, axis=0), jnp.concatenate(gt, axis=0)
                if n0 > 0:
                    gu = gu + r.gsc[rows, lane(j)]
                    gt = gt + r.y_s[rows, lane(j)]
                r.gsc[rows, lane(j)] = gu
                r.y_s[rows, lane(j)] = gt
                return tuple(gs), tuple(gd)

            zero = tuple(jnp.zeros((V, LN), F32) for _ in range(half))
            first = tuple(r.start[1, row_n(n), lane(j)] for n in range(n0, n0 + half))
            _, gd = lax.fori_loop(0, Q // 2, behind, (first, zero))
            for i in range(half):
                dec = r.dec[n0 + i : n0 + i + 1, lane(j)] * (1.0 / LOG2E)
                r.rowsum[8 + n0 + i : 9 + n0 + i, lane(j)] = (
                    jnp.sum(gd[i], axis=0, keepdims=True) * dec
                )

    def gating(j):
        def body(i, sk):
            rows = pl.ds(pl.multiple_of(i * 64, 64), 64)
            x = r.inp[rows, lane(j)].astype(F32)
            mixed = r.y_s[rows, lane(j)] + r.cp[6:7, lane(j)] * x
            g = r.gate[rows, lane(j)]
            s = sigmoid(g)
            r.gated[rows, lane(j)] = (mixed * (g * s)).astype(BF16)
            r.ggate[rows, lane(j)] = (
                r.gg[rows, lane(j)] * mixed * s * (1.0 + g * (1.0 - s))
            ).astype(BF16)
            p = r.gy[rows, lane(j)] * x
            return sk + jnp.sum(p.reshape(8, V, LN), axis=0)

        sk = lax.fori_loop(0, T // 64, body, jnp.zeros((V, LN), F32))
        r.rowsum[6:7, lane(j)] = jnp.sum(sk, axis=0, keepdims=True)

    r.rowsum[...] = jnp.zeros_like(r.rowsum)
    states = [own_ends(j) for j in range(NB)]
    tots.wait()
    for j in range(NB):
        begin(j, states[j])
        forward(j)
        gating(j)
        if j == NB - 2:
            backward(0)
    late = list(range(1, NB))

    def put(dst, first, res):
        n = dst.shape[2]
        for t in range(res.shape[0] // n):
            s = first // n + t
            dst[s % 2, s // 2] = res[t * n : (t + 1) * n].astype(dst.dtype)

    def put_split(dst, first, res):
        n = dst.shape[3]
        for t in range(res.shape[0] // n):
            s, f = divmod(first // n + t, F)
            dst[s % 2, s // 2, f] = res[t * n : (t + 1) * n].astype(dst.dtype)

    back0 = from_scan(d, 0)
    r.gatn[...] = dot(back0, r.ggate[0:T, :]).astype(BF16)
    for c in range(0, D, LN):
        put_split(r.giwg, c, dot(r.normed[0:T, c : c + LN], r.gatn[...], 0, 0))
    sum_g = Scatter(net, r.giwg, r.giwg_n, r.o_wg, True)
    for j in range(NB):
        put(r.gow, j * LN, dot(r.gated[0:T, lane(j)], r.big[0:T, :], 0, 0))
    sum_o = Scatter(net, r.gow, r.gow_n, r.o_out, False)
    r.gated[0:T, :] = dot(back0, r.gated[0:T, :]).astype(BF16)
    for c in range(0, D, 256):
        r.cot[:, c : c + 256] = dot(r.gated[0:T, :], r.ow[:, c : c + 256]).astype(BF16)
    outs = [net.send(rows_of(r.cot, net.at(0, k)[1], tok), r.outr.at[mf], *net.at(0, k)) for k in range(1, F)]
    outs.append(net.local(rows_of(r.cot, mf, tok), r.outr.at[mf]))
    for i, j in enumerate(late):
        backward(j)
        if i > 0:
            sum_g.step((S // 2) * i // (len(late) - 1))

    def finish(i, acc):
        rows = pl.ds(pl.multiple_of(i * 64, 64), 64)
        out = []
        for j in range(NB):
            x = r.inp[rows, lane(j)].astype(F32)
            z = r.dtpre[rows, lane(j)]
            gu = r.gsc[rows, lane(j)]
            gt = r.y_s[rows, lane(j)] * (1.0 / LOG2E) + gu * x
            dt = jnp.maximum(z, 0.0) + jnp.log1p(jnp.exp(-jnp.abs(z)))
            gz = gt * sigmoid(z)
            r.ggate[rows, lane(j)] = gz.astype(BF16)
            r.gsc[rows, lane(j)] = gu * dt + r.gy[rows, lane(j)] * r.cp[6:7, lane(j)]
            out.append(acc[j] + jnp.sum(gz.reshape(8, V, LN), axis=0))
        return tuple(out)

    db = lax.fori_loop(0, T // 64, finish, tuple(jnp.zeros((V, LN), F32) for _ in range(NB)))
    for j in range(NB):
        r.rowsum[5:6, lane(j)] = jnp.sum(db[j], axis=0, keepdims=True)
    r.gx[:, 0 : d.R] = dot(r.ggate[0:T, :], r.wdt[...], 1, 1).astype(BF16)
    acc = jnp.zeros((T, 2 * N), F32)
    for n in range(0, 2 * N, 4):
        row = lax.div(lax.broadcasted_iota(jnp.int32, (4 * LN, 2 * N), 0), LN) + n
        col = lax.broadcasted_iota(jnp.int32, (4 * LN, 2 * N), 1)
        pick = jnp.where(row == col, 1.0, 0.0).astype(BF16)
        acc = acc + dot(r.x_s[:, n * LN : (n + 4) * LN].astype(BF16), pick)
    r.gx[:, d.R : W] = acc.astype(BF16)
    gx_near = net.send(r.gx, r.gxn, ms, core)
    gx_far = chips(r.gx, gx_near, r.gxn, r.gxr)

    sum_g.step()
    sum_o.step(S // 4)
    gwdt = dot(r.ggate[0:T, :], r.xd[:, 0 : d.R], 0, 0)

    gxd = chips_total(r.gx, gx_far, r.gxr).astype(BF16)
    pad = HG * V
    r.gg[0:pad, :] = jnp.zeros((pad, CL), F32)
    r.gg[pad + T :, :] = jnp.zeros((pad, CL), F32)
    for c in range(0, CL, 256):
        r.gg[pad : pad + T, c : c + 256] = r.gsc[:, c : c + 256] + dot(gxd, r.xp[:, c : c + 256])

    def act(i, acc):
        r0 = pl.multiple_of(i * 64, 64)
        rows = pl.ds(r0, 64)
        shift = pl.ds(pl.multiple_of(r0 + pad, V), 64)
        age = r.rel[shift, :]
        out = []
        for j in range(NB):
            p = r.pre[rows, lane(j)]
            q = sigmoid(p)
            g = r.gg[shift, lane(j)] * q * (1.0 + p * (1.0 - q))
            r.gg[shift, lane(j)] = g
            a = list(acc[j])
            a[4] = a[4] + jnp.sum(g.reshape(8, V, LN), axis=0)
            for k in range(d.K):
                back = d.K - 1 - k
                xs = r.xb[pl.ds(pl.multiple_of(r0 + (HG - back) * V, V), 64), lane(j)]
                t = jnp.where(age >= back, g * xs, 0.0)
                a[k] = a[k] + jnp.sum(t.reshape(8, V, LN), axis=0)
            out.append(tuple(a))
        return tuple(out)

    zero = tuple(tuple(jnp.zeros((V, LN), F32) for _ in range(5)) for _ in range(NB))
    acc = lax.fori_loop(0, T // 64, act, zero)
    for j in range(NB):
        for k in range(5):
            r.rowsum[k : k + 1, lane(j)] = jnp.sum(acc[j][k], axis=0, keepdims=True)

    def gather_taps(i, _):
        r0 = pl.multiple_of(i * 32, 32)
        for j in range(NB):
            acc = jnp.zeros((32, LN), F32)
            for k in range(d.K):
                back = d.K - 1 - k
                src = pl.ds(pl.multiple_of(r0 + back * V, V), 32)
                acc = acc + jnp.where(
                    r.rel[src, :] >= back, r.gg[src, lane(j)] * r.cp[k : k + 1, lane(j)], 0.0
                )
            r.gated[pl.ds(r0, 32), lane(j)] = acc.astype(BF16)
        return 0

    lax.fori_loop(0, d.TE // 32, gather_taps, 0)
    r.ggate[...] = dot(from_scan(d, HG), r.gated[...]).astype(BF16)
    for c in range(0, D, LN):
        put_split(r.giwx, c, dot(r.normed[:, c : c + LN], r.ggate[...], 0, 0))
    sum_x = Scatter(net, r.giwx, r.giwx_n, r.o_wx, True)
    r.y_s[0:CL, 0:LN] = r.rowsum[...].T
    r.y_s[0:CL, LN : LN + W] = dot(r.inp[...], gxd, 0, 0)
    r.y_s[0:CL, LN + W : 2 * LN] = jnp.zeros((CL, LN - W), F32)
    r.y_s[0:CL, 32 : 32 + d.R] = gwdt
    put(r.small, 0, r.y_s[0:CL, 0 : 2 * LN])
    sum_s = Scatter(net, r.small, r.small_n, r.o_small, False)
    sum_o.step()
    for c in range(0, D, 256):
        g = dot(r.ggate[...], r.w[0, c : c + 256, :], 1, 1)
        r.hid[0:T, c : c + 256] = (
            g[0:T] + dot(r.gatn[...], r.w[1, c : c + 256, :], 1, 1)
        ).astype(BF16)
        r.hid[T:, c : c + 256] = g[T:].astype(BF16)
    gns = [
        net.send(rows_of(r.hid, net.at(0, k)[1], tok), rows_of(r.o_gn, mf, tok), *net.at(0, k))
        for k in range(1, F)
    ]
    gns.append(net.local(rows_of(r.hid, mf, tok), rows_of(r.o_gn, mf, tok)))
    for k in range(F):
        ps, pf = net.at(-1, k)
        gns.append(
            net.send(
                r.hid.at[pl.ds(T + pf * TAIL, TAIL)], r.o_gn.at[pl.ds(T + mf * TAIL, TAIL)], ps, pf
            )
        )
    sum_x.step()
    sum_s.step()

    def gains(i, acc):
        rows = pl.ds(pl.multiple_of(i * 64, 64), 64)
        t = r.hid[rows, :].astype(F32) * r.normed[rows, :].astype(F32)
        return acc + jnp.sum(t.reshape(8, V, D), axis=0)

    gtot = lax.fori_loop(0, d.NAT // 64, gains, jnp.zeros((V, D), F32)) / r.gain[...]
    n = D // S
    for s in range(S):
        r.gg8[s % 2, s // 2] = gtot[:, s * n : (s + 1) * n]
    sum_n = Scatter(net, r.gg8, r.gg8_n, r.o_gain, True, False)
    sum_n.step()
    net.drain()
    assert (net.s_used, net.r_used) == semaphores(d), (net.s_used, net.r_used)


def close(d, gn, outr, hid, cot, gain, wx, wg, out, small, ggain,
          o_out, o_hid, o_gain, o_in, o_conv, o_cb, o_db, o_sk, o_xp, o_dt, o_al, o_gout):
    F, T, tok, D = d.F, d.T, d.tok, d.D
    W = d.R + 2 * d.N

    def rows_(i, _):
        rows = pl.ds(pl.multiple_of(i * 16, 16), 16)
        h = hid[rows, :].astype(F32)
        g = gn[pl.ds(pl.multiple_of(i * 16, 16), 16), :].astype(F32)
        o = outr[0, rows, :].astype(F32)
        for f in range(1, F):
            g = g + gn[pl.ds(pl.multiple_of(f * tok + i * 16, 16), 16), :].astype(F32)
            o = o + outr[f, rows, :].astype(F32)
        late = jnp.zeros((TAIL, D), F32)
        for f in range(F):
            late = late + gn[T + f * TAIL : T + (f + 1) * TAIL, :].astype(F32)
        g = g + jnp.where(i == tok // 16 - 1, late, 0.0)
        inv = lax.rsqrt(jnp.mean(h * h, axis=-1, keepdims=True) + EPS)
        g2 = g * gain[...]
        mean = jnp.mean(g2 * h, axis=-1, keepdims=True)
        o_hid[0, rows, :] = cot[rows, :].astype(F32) + inv * g2 - h * (inv * inv * inv) * mean
        o_out[0, rows, :] = (h + o).astype(BF16)
        return 0

    lax.fori_loop(0, tok // 16, rows_, 0)
    for f in range(F):
        for at, part in ((f * d.CL, wx), (d.DI + f * d.CL, wg)):
            o_in[:, at : at + d.CL] = jnp.sum(part[:, f].astype(F32), axis=0)
    o_gout[...] = jnp.sum(out[...].astype(F32), axis=0)
    sm = jnp.sum(small[...].astype(F32), axis=0)
    first = sm[:, 0:LN].T
    for i, o_row in enumerate((o_cb, o_db, o_sk)):
        o_row[...] = first[4 + i : 5 + i, :]
    o_conv[...] = first[0 : d.K, :]
    o_al[...] = first[V : V + d.N, :]
    o_dt[...] = sm[:, 32 : 32 + d.R]
    o_xp[...] = sm[:, LN : LN + W]
    tot = jnp.zeros(ggain.shape[2:], F32)
    for k in range(ggain.shape[0]):
        for f in range(F):
            tot = tot + ggain[k, f]
    n, k = D // d.S, D // d.S // F
    row = lax.broadcasted_iota(jnp.int32, (n, k), 0) - lax.axis_index("fsdp") * k
    pick = jnp.where(row == lax.broadcasted_iota(jnp.int32, (n, k), 1), 1.0, 0.0)
    one = lax.dot_general(
        jnp.sum(tot, axis=0, keepdims=True) + jnp.zeros((V, n), F32), pick, (((1,), (0,)), ((), ())),
        precision=lax.Precision.HIGHEST, preferred_element_type=F32,
    )
    o_gain[...] = one[0:1, :]


def semaphores(d):
    half, far = d.S // 2, d.F // 2 - 1
    one = (d.F - 1) + 2 * (2 * far + 1) + d.F + 2 * (2 * far) + 2 + 2 * (6 * far) + (d.F - 1) + (2 * d.F - 1)
    one += 2 * 2 + 1 + d.NB
    return one + 5 * 2 * half, one + 5 * (half + 1) + 16


def vm(*shape, dtype=F32):
    return pltpu.VMEM(shape, dtype)


def per_device(
    d, hidden, cluster_lengths, norm_gain, in_weight, conv_weight, conv_bias, xproj_weight,
    dt_weight, dt_bias, a_log, skip, out_weight, cotangent,
):
    S, F, T, D, CL, N, NB, R = d.S, d.F, d.T, d.D, d.CL, d.N, d.NB, d.R
    ins = dict(
        hidden=hidden[0], lens=cluster_lengths, norm_gain=norm_gain, conv_bias=conv_bias,
        dt_bias=dt_bias, skip=skip, in_weight=in_weight, conv_weight=conv_weight.T,
        xproj_weight=xproj_weight.T, dt_weight=dt_weight.T, a_log=a_log.T, out_weight=out_weight,
        cotangent=cotangent[0],
    )
    DS, CS, W, W2 = D // S, CL // S, R + 2 * N, 2 * LN
    TP = T + 2 * HG * V
    rt = BF16 if CS >= 16 else F32
    half = S // 2
    outs = dict(
        o_gn=((d.NAT, D), BF16), outr=((F, d.tok, D), BF16), gain=((1, D), F32),
        o_wx=((half, F, DS // F, CL), BF16), o_wg=((half, F, DS // F, CL), BF16),
        o_out=((half, CS, D), rt), o_small=((half, CS, W2), rt), o_gain=((half, F, V, DS), F32),
    )
    small_t = T <= 512
    EP = N // d.H * V
    scratch = dict(
        hid=((d.NAT, D), BF16), normed=((d.NAT, D), BF16), big=((d.TE, D), BF16),
        cot=((T, D), BF16), w=((2, D, CL), BF16), ow=((CL, D), BF16),
        xp=((W, CL), BF16), wdt=((R, CL), BF16), cw=((d.K, CL), BF16), al=((N, CL), BF16),
        row_cb=((CL,), BF16), row_db=((CL,), BF16), row_sk=((CL,), BF16), row_g=((D // F,), BF16),
        row_l=((1, d.clusters), jnp.int32), pg=((F, V, D // F), F32), pg_own=((V, D // F), F32), cp=((V, CL), F32), dec=((N, CL), F32), rel=((TP, LN), F32),
        xb=((d.TE, CL), F32), gate=((T, CL), F32), pre=((T, CL), F32), inp=((T, CL), BF16),
        xd=((T, LN), BF16), xdn=((T, LN), BF16), xdr=((F // 2 - 1, T, LN), BF16),
        dtpre=((T, CL), F32), dtd=((T, CL), F32), u=((T, CL), F32), gg=((TP, CL), F32),
        gy=((T, CL), F32), bcb=((T, 2 * N * LN), F32 if small_t else BF16),
        sd=((V, CL), F32), tot=((V, CL), F32), totr=((S - 1, V, CL), F32),
        ends=((2, N * V, CL), F32), epack=((2, NB, EP, LN), BF16), eget=((NB, S - 1, EP, LN), BF16),
        start=((2, N * V, CL), F32), m_s=((NB, T, N * LN), BF16), y_s=((T, CL), F32),
        gsc=((T, CL), F32), x_s=((T, 2 * N * LN), F32 if small_t else BF16),
        gated=((d.TE, CL), BF16), ggate=((d.NAT, CL), BF16), gatn=((T, CL), BF16),
        gx=((T, LN), BF16), gxn=((T, LN), BF16), gxr=((F // 2 - 1, T, LN), BF16), rowsum=((LN, CL), F32),

        giwg=((2, half, F, DS // F, CL), BF16), giwg_n=((half, F, DS // F, CL), BF16),
        giwx=((2, half, F, DS // F, CL), BF16), giwx_n=((half, F, DS // F, CL), BF16),
        gow=((2, half, CS, D), rt), gow_n=((half, CS, D), rt),
        small=((2, half, CS, W2), rt), small_n=((half, CS, W2), rt),
        gg8=((2, half, V, DS), F32), gg8_n=((half, V, DS), F32),
    )
    names = list(ins) + list(outs) + list(scratch) + ["ssem", "rsem"]
    sends, gets = semaphores(d)
    res = pl.pallas_call(
        functools.partial(layer, d, names),
        out_shape=[jax.ShapeDtypeStruct(*o) for o in outs.values()],
        in_specs=[pl.BlockSpec(memory_space=pl.ANY)] * len(ins),
        out_specs=[
            pl.BlockSpec(memory_space=pltpu.VMEM if k == "gain" else pl.ANY) for k in outs
        ],
        scratch_shapes=[vm(*s, dtype=t) for s, t in scratch.values()]
        + [pltpu.SemaphoreType.DMA((sends,)), pltpu.SemaphoreType.DMA((gets,))],
        compiler_params=pltpu.CompilerParams(
            collective_id=0, has_side_effects=True, vmem_limit_bytes=65250 * 1024
        ),
    )(*ins.values())
    o = dict(zip(outs, res))
    fin = kernel(
        functools.partial(close, d),
        (o["o_gn"], o["outr"], hidden[0], cotangent[0], o["gain"], o["o_wx"], o["o_wg"], o["o_out"],
         o["o_small"], o["o_gain"]),
        [((1, d.tok, D), BF16), ((1, d.tok, D), F32), ((1, DS // F), F32), ((DS // F, 2 * d.DI), F32),
         ((d.K, CS), F32), ((1, CS), F32), ((1, CS), F32), ((1, CS), F32), ((CS, W), F32), ((CS, R), F32),
         ((N, CS), F32), ((CS, D), F32)],
    )
    out, g_hid, g_gain, g_in, g_conv, g_cb, g_db, g_sk, g_xp, g_dt, g_al, g_out = fin
    return (
        out, g_hid, g_gain[0], g_in, g_conv.T, g_cb[0], g_xp, g_dt, g_db[0], g_al.T, g_sk[0], g_out,
    )


def solution(mesh):
    S, F = mesh.shape["seq"], mesh.shape["fsdp"]

    def run(*args):
        tok, D = args[0].shape[1] // S, args[0].shape[2]
        d = Dims(
            S, F, tok, D, args[11].shape[0], args[9].shape[1], args[7].shape[1], args[4].shape[1],
            args[1].shape[1],
        )
        return jax.shard_map(
            functools.partial(per_device, d),
            mesh=mesh,
            in_specs=(
                P("fsdp", "seq", None), P("fsdp", None), P("fsdp"), P("fsdp", None),
                P("fsdp", None), P("fsdp"), P("fsdp", None), P("fsdp", None), P("fsdp"),
                P("fsdp", None), P("fsdp"), P("fsdp", None), P("fsdp", "seq", None),
            ),
            out_specs=(
                P("fsdp", "seq", None), P("fsdp", "seq", None), P(("seq", "fsdp")),
                P(("seq", "fsdp"), None), P(("seq", "fsdp"), None), P(("seq", "fsdp")),
                P(("seq", "fsdp"), None), P(("seq", "fsdp"), None), P(("seq", "fsdp")),
                P(("seq", "fsdp"), None), P(("seq", "fsdp")), P(("seq", "fsdp"), None),
            ),
            check_vma=False,
        )(*args)

    return run
```

```python
import functools
import math

import jax
import jax.numpy as jnp
from jax import lax
from jax.experimental import pallas as pl
from jax.experimental.pallas import tpu as pltpu
from jax.sharding import PartitionSpec as P

EPS = 1e-05
V = 8
LN = 128
HG = 4
TAIL = 16
LOG2E = 1.0 / math.log(2.0)
RESET = 1e30
F32 = jnp.float32
TOP, BOT = slice(0, V), slice(V, 2 * V)
BF16 = jnp.bfloat16
MESH = pl.DeviceIdType.MESH


class Dims:
    def __init__(self, S, F, tok, D, DI, N, R, K, clusters):
        self.S, self.F, self.tok, self.D, self.DI = S, F, tok, D, DI
        self.N, self.R, self.K, self.clusters = N, R, K, clusters
        self.H = V // F
        self.Q = tok // self.H
        self.T = F * tok
        self.TE = (self.Q + HG) * V
        self.NAT = F * (tok + TAIL)
        self.CL = DI // F
        self.NB = self.CL // LN


def dot(a, b, ca=1, cb=0):
    return lax.dot_general(a, b, (((ca,), (cb,)), ((), ())), preferred_element_type=F32)


def sigmoid(v):
    return 1.0 / (1.0 + jnp.exp(-v))


def kernel(body, args, outs, scratch=()):
    return pl.pallas_call(
        body,
        out_shape=[jax.ShapeDtypeStruct(s, t) for s, t in outs],
        in_specs=[pl.BlockSpec(memory_space=pltpu.VMEM)] * len(args),
        out_specs=[pl.BlockSpec(memory_space=pltpu.VMEM)] * len(outs),
        scratch_shapes=list(scratch),
        compiler_params=pltpu.CompilerParams(vmem_limit_bytes=60 * 1024 * 1024),
    )(*args)


def lane(j):
    return slice(j * LN, (j + 1) * LN)


def natural_of(d, row, halo):
    q = lax.div(row, V) - halo
    v = lax.rem(row, V)
    f = lax.div(v, d.H)
    p = lax.rem(v, d.H) * d.Q + q
    return jnp.where(p >= 0, f * d.tok + p, d.T + f * TAIL + TAIL + p)


def to_scan(d, halo):
    rows, cols = (d.TE, d.NAT) if halo else (d.T, d.T)
    want = natural_of(d, lax.broadcasted_iota(jnp.int32, (rows, 1), 0), halo)
    have = lax.broadcasted_iota(jnp.int32, (rows, cols), 1)
    return jnp.where(have == want, 1.0, 0.0).astype(BF16)


def from_scan(d, halo):
    rows, cols = (d.NAT, d.TE) if halo else (d.T, d.T)
    want = natural_of(d, lax.broadcasted_iota(jnp.int32, (1, cols), 1), halo)
    have = lax.broadcasted_iota(jnp.int32, (rows, cols), 0)
    return jnp.where(have == want, 1.0, 0.0).astype(BF16)


class Refs:
    pass


class Copy:
    def __init__(self, copy, remote):
        self.copy, self.sent, self.got = copy, not remote, False
        self.remote = remote

    def wait_send(self):
        if not self.sent:
            self.copy.wait_send()
            self.sent = True

    def wait_recv(self):
        if not self.got:
            if self.remote:
                self.copy.wait_recv()
            else:
                self.copy.wait()
            self.got = True

    def wait(self):
        self.wait_send()
        self.wait_recv()


class Batch:
    def __init__(self, net, sends, whole):
        i, j = net.pair()
        self.open = True
        for src, dst, ps, pf in sends:
            net.remote(src, dst, i, j, ps, pf).start()
        self.all = net.remote(whole, whole, i, j, *net.at(0, 1))

    def wait(self):
        if self.open:
            self.all.wait_send()
            self.all.wait_recv()
            self.open = False


class Net:
    def __init__(self, d, ssem, rsem):
        self.d, self.ssem, self.rsem, self.s_used, self.r_used = d, ssem, rsem, 0, 0
        self.ms, self.mf = lax.axis_index("seq"), lax.axis_index("fsdp")
        self.open = []

    def at(self, ds, df):
        return lax.rem(self.ms + ds % self.d.S, self.d.S), lax.rem(self.mf + df % self.d.F, self.d.F)

    def pair(self):
        self.s_used += 1
        self.r_used += 1
        return self.s_used - 1, self.r_used - 1

    def remote(self, src, dst, i, j, ps, pf):
        return pltpu.make_async_remote_copy(
            src, dst, self.ssem.at[i], self.rsem.at[j], {"seq": ps, "fsdp": pf}, device_id_type=MESH
        )

    def start(self, copy, remote):
        copy.start()
        self.open.append(Copy(copy, remote))
        return self.open[-1]

    def send(self, src, dst, ps, pf):
        i, j = self.pair()
        return self.start(self.remote(src, dst, i, j, ps, pf), True)

    def batch(self, sends, whole):
        self.open.append(Batch(self, sends, whole))
        return self.open[-1]

    def local(self, src, dst):
        self.r_used += 1
        return self.start(pltpu.make_async_copy(src, dst, self.rsem.at[self.r_used - 1]), False)

    def drain(self):
        for c in self.open:
            c.wait()


def flip(value, mask):
    bit = 0
    out = value
    while 1 << bit <= mask:
        if mask >> bit & 1:
            out = out + (1 - 2 * lax.rem(lax.div(value, 1 << bit), 2)) * (1 << bit)
        bit += 1
    return out


class Scatter:
    def __init__(self, net, mine, near, out, bits, spread, split=True):
        self.net, self.mine, self.near, self.out = net, mine, near, out
        self.bits, self.spread, self.split = bits, spread, split
        self.tails, self.queue, self.last = [], [], {}
        self.into = net.r_used
        net.r_used += 1
        slot = 0
        self.slots = []
        for level in range(len(bits) - 1):
            sides = self.sides(level)
            self.slots.append({side: slot + i for i, side in enumerate(sides)})
            slot += len(sides)
            self.queue += [(level, side) for side in sides]
        self.copies = {}
        for side in self.sides(0):
            self.push(0, side)
        self.done = 0
        net.open.append(self)

    def sides(self, level):
        masks = [0]
        for bit in reversed(self.bits[level + 1 :]):
            masks = [m | 1 << bit for m in masks] + masks
        return masks

    def push(self, level, side):
        net = self.net
        to = flip(net.ms, 1 << self.bits[level])
        self.copies[level, side] = net.send(
            self.mine.at[flip(to, side)], self.near.at[self.slots[level][side]], to, net.mf
        )

    def step(self, count=1000):
        net = self.net
        for level, side in self.queue[self.done : self.done + count]:
            self.done += 1
            self.copies[level, side].wait()
            at = flip(net.ms, side)
            both = self.mine[at].astype(F32) + self.near[self.slots[level][side]].astype(F32)
            self.mine[at] = both.astype(self.mine.dtype)
            bit = 1 << self.bits[level + 1]
            if level + 2 < len(self.bits):
                if side & bit:
                    self.push(level + 1, side ^ bit)
            else:
                self.finish(at, 1 if side else 0)

    def finish(self, at, side):
        net, d = self.net, self.net.d
        i = net.s_used
        net.s_used += 1
        if self.spread:
            for g in range(1 - side, d.F):
                f = lax.rem(net.mf + g, d.F)
                src = self.mine.at[at, f] if self.split else self.mine.at[at]
                net.remote(src, self.out.at[side, net.mf], i, self.into, at, f).start()
            if not side:
                src = self.mine.at[at, net.mf] if self.split else self.mine.at[at]
                pltpu.make_async_copy(src, self.out.at[0, net.mf], net.rsem.at[self.into]).start()
            sent = self.out.at[side] if side else self.out.at[0, pl.ds(0, d.F - 1)]
            self.tails.append((None, net.remote(sent, sent, i, self.into, *net.at(0, 1))))
        else:
            spot = net.mf * d.S + at
            away = spot != net.ms * d.F + net.mf
            src, dst = self.mine.at[at], self.out.at[side]
            far = net.remote(src, dst, i, self.into, lax.div(spot, d.F), lax.rem(spot, d.F))
            near = pltpu.make_async_copy(src, dst, net.rsem.at[self.into])
            pl.when(away)(far.start)
            pl.when(jnp.logical_not(away))(near.start)
            self.tails.append((away, far))

    def wait(self):
        self.step()
        for away, c in self.tails:
            if away is None:
                c.wait_send()
            else:
                pl.when(away)(c.wait_send)
        net = self.net
        net.remote(self.out, self.out, 0, self.into, *net.at(0, 1)).wait_recv()


class Rows:
    def __init__(self, net, core, src, land, out):
        self.net, self.src, self.land, self.out = net, src, land, out
        d = net.d
        self.rows = lambda f: src.at[pl.ds(f * d.tok, d.tok)]
        self.far = range(1, d.F // 2)
        step = lambda f, k: lax.rem(f + 2 * k, d.F)
        self.to = [step(net.mf, k) for k in self.far]
        self.near = [
            net.send(self.rows(step(core, k)), land.at[pl.ds((k - 1) * d.tok, d.tok)], net.ms, core)
            for k in self.far
        ]
        net.send(self.rows(core), out.at[1], net.ms, core)
        net.local(self.rows(net.mf), out.at[0])

    def cross(self):
        net, d = self.net, self.net.d
        for k, f, c in zip(self.far, self.to, self.near):
            c.wait()

            def add(i, _, k=k, f=f):
                here = pl.ds(pl.multiple_of(f * d.tok + i * 32, 32), 32)
                there = pl.ds(pl.multiple_of((k - 1) * d.tok + i * 32, 32), 32)
                self.src[here, :] = (
                    self.src[here, :].astype(F32) + self.land[there, :].astype(F32)
                ).astype(BF16)
                return 0

            lax.fori_loop(0, d.tok // 32, add, 0)
            net.send(self.rows(f), self.out.at[1 + k], net.ms, f)


def layer(d, names, *refs):
    r = Refs()
    for name, ref in zip(names, refs):
        setattr(r, name, ref)
    S, F, CL, T, N, Q, NB, D, tok, H = d.S, d.F, d.CL, d.T, d.N, d.Q, d.NB, d.D, d.tok, d.H
    DF = D // F
    net = Net(d, r.ssem, r.rsem)
    ms, mf = net.ms, net.mf
    core = mf + 1 - 2 * lax.rem(mf, 2)
    greet = [(i, k) for i in range(S) for k in range(F) if (i, k) != (0, 0)]
    bar = pltpu.get_barrier_semaphore()
    for ds, df in greet:
        ps, pf = net.at(-ds, -df)
        pl.semaphore_signal(bar, inc=1, device_id={"seq": ps, "fsdp": pf}, device_id_type=MESH)

    own = [
        net.local(r.hidden, r.hid.at[pl.ds(mf * tok, tok)]),
        net.local(r.norm_gain, r.row_g),
        net.local(r.in_weight.at[:, pl.ds(pl.multiple_of(mf * CL, LN), CL)], r.w.at[0, pl.ds(mf * DF, DF)]),
        net.local(
            r.in_weight.at[:, pl.ds(pl.multiple_of(d.DI + mf * CL, LN), CL)],
            r.w.at[1, pl.ds(mf * DF, DF)],
        ),
        net.local(r.cotangent, r.cot.at[pl.ds(mf * tok, tok)]),
        net.local(r.out_weight, r.ow),
        net.local(r.xproj_weight, r.xp),
        net.local(r.dt_weight, r.wdt),
        net.local(r.conv_weight, r.cw),
        net.local(r.a_log, r.al),
        net.local(r.lens, r.row_l),
        net.local(r.conv_bias, r.row_cb),
        net.local(r.dt_bias, r.row_db),
        net.local(r.skip, r.row_sk),
    ]
    pl.semaphore_wait(bar, len(greet))

    rows_of = lambda ref, f, n: ref.at[pl.ds(f * n, n)]
    same_core = [lax.rem(mf + 2 * k, F) for k in range(1, F // 2)]
    other_chip = [(lax.rem(mf + 2 * k, F), lax.rem(core + 2 * k, F)) for k in range(1, F // 2)]

    for i in (1, 10):
        own[i].wait()
    as_row = lambda ref: ref[...].astype(F32).reshape(1, ref.shape[-1])
    r.pg_own[0:1, :] = as_row(r.row_g)
    r.pg_own[1:2, 0 : d.clusters] = as_row(r.row_l)
    r.pg[mf] = r.pg_own[...]

    def spread_rows(src, dst):
        direct = [net.send(src, rows_of(dst, mf, tok), ms, f) for f in same_core]
        beside = [net.send(src, rows_of(dst, mf, tok), ms, core)]
        return direct, beside

    def relay_rows(dst, direct, beside):
        for k, c in enumerate(direct):
            c.wait()
            f = lax.rem(mf + F - 2 * (k + 1), F)
            beside.append(net.send(rows_of(dst, f, tok), rows_of(dst, f, tok), ms, core))

    def w_slice(g, f):
        return r.in_weight.at[:, pl.ds(pl.multiple_of(g * d.DI + f * CL, LN), CL)]

    quart, ring = lax.rem(ms, 4), ms - lax.rem(ms, 4)
    QF = DF // 4

    def w_far(g):
        out = []
        for pair in other_chip:
            for f in pair:
                src = r.in_weight.at[
                    pl.ds(quart * QF, QF), pl.ds(pl.multiple_of(g * d.DI + f * CL, LN), CL)
                ]
                out.append(net.send(src, r.w.at[g, pl.ds(mf * DF + quart * QF, QF)], ms, f))
        return out

    def w_relay(g, far):
        out = []
        i = 0
        for k in range(1, F // 2):
            for flip in (0, 1):
                far[i].wait_recv()
                i += 1
                f0 = lax.rem(mf + F - 2 * k, F)
                if flip:
                    f0 = f0 + 1 - 2 * lax.rem(f0, 2)
                place = r.w.at[g, pl.ds(f0 * DF + quart * QF, QF)]
                for t in (1, 2, 3):
                    out.append(net.send(place, place, ring + lax.rem(quart + t, 4), mf))
        return out

    wx_far = w_far(0)
    pgs = [net.send(r.pg_own, r.pg.at[mf], *net.at(0, k)) for k in range(1, F)]
    w_beside = [net.send(w_slice(g, core), r.w.at[g, pl.ds(mf * DF, DF)], ms, core) for g in (0, 1)]
    for c in wx_far:
        c.wait_send()
    h_direct, h_beside = spread_rows(r.hidden, r.hid)
    halo = [
        net.send(
            r.hidden.at[pl.ds(tok - TAIL, TAIL)],
            r.hid.at[pl.ds(T + mf * TAIL, TAIL)],
            *net.at(1, k),
        )
        for k in range(F)
    ]
    wx_near = w_relay(0, wx_far)
    for c in pgs + own[:1]:
        c.wait()
    for f in range(F):
        r.gain[0:1, f * DF : (f + 1) * DF] = r.pg[f, 0:1, :]
    sub = lax.broadcasted_iota(jnp.int32, (V, LN), 0)
    hidx = lax.rem(sub, H)
    stream = lax.div(sub, H)
    offs, run = [], jnp.zeros((V, LN), F32)
    for j in range(d.clusters - 1):
        for f in range(F):
            run = run + jnp.where(stream == f, r.pg[f, 1:2, j : j + 1], 0.0)
        offs.append(run)
    base = ms * tok + hidx * Q
    r.rel[0 : HG * V, :] = jnp.zeros((HG * V, LN), F32)
    r.rel[HG * V + T :, :] = jnp.zeros((HG * V, LN), F32)

    def mark(q, _):
        pos = (base + q).astype(F32)
        last = jnp.zeros((V, LN), F32)
        for o in offs:
            last = jnp.maximum(last, jnp.where(o <= pos, o, 0.0))
        r.rel[pl.ds(pl.multiple_of((q + HG) * V, V), V), :] = jnp.where(pos == 0.0, 0.5, pos - last)
        return 0

    lax.fori_loop(0, Q, mark, 0)
    for c in own[8:]:
        c.wait()
    r.cp[0 : d.K, :] = r.cw[...].astype(F32)
    for i, ref in enumerate((r.row_cb, r.row_db, r.row_sk)):
        r.cp[4 + i : 5 + i, :] = as_row(ref)
    r.dec[...] = -LOG2E * jnp.exp(r.al[...].astype(F32))
    for c in h_direct:
        c.wait_send()
    c_direct, c_beside = spread_rows(r.cotangent, r.cot)
    wg_far = w_far(1)
    for k, c in enumerate(h_direct):
        c.wait_recv()
        f = lax.rem(mf + F - 2 * (k + 1), F)
        h_beside.append(net.send(rows_of(r.hid, f, tok), rows_of(r.hid, f, tok), ms, core))
    perm = to_scan(d, HG)

    def rms(first, count):
        def body(i, _):
            rows = pl.ds(pl.multiple_of(first + i * 64, 64), 64)
            h = r.hid[rows, :].astype(F32)
            inv = lax.rsqrt(jnp.mean(h * h, axis=-1, keepdims=True) + EPS)
            r.normed[rows, :] = (h * inv * r.gain[...]).astype(BF16)
            return 0

        lax.fori_loop(0, count // 64, body, 0)

    for k in range(F // 2):
        rms(lax.rem(mf + F - 2 * k, F) * tok, tok)
    for k, c in enumerate(h_beside):
        c.wait()
        rms(lax.rem(core + F - 2 * k, F) * tok, tok)
    for c in halo:
        c.wait()
    rms(T, F * TAIL)
    for c in range(0, D, 256):
        r.big[:, c : c + 256] = dot(perm, r.normed[:, c : c + 256]).astype(BF16)
    own[2].wait()
    w_beside[0].wait()
    for c in wx_near:
        c.wait()
    for c in range(0, CL, 256):
        r.xb[:, c : c + 256] = (
            dot(r.big[:, :], r.w[0, :, c : c + 256]).astype(BF16).astype(F32)
        )

    def conv(i, _):
        r0 = pl.multiple_of(i * 64, 64)
        rows = pl.ds(r0, 64)
        age = r.rel[pl.ds(pl.multiple_of(r0 + HG * V, V), 64), :]
        for j in range(NB):
            acc = jnp.zeros((64, LN), F32) + r.cp[4:5, lane(j)]
            for k in range(d.K):
                back = d.K - 1 - k
                xs = r.xb[pl.ds(pl.multiple_of(r0 + (HG - back) * V, V), 64), lane(j)]
                acc = acc + jnp.where(age >= back, xs * r.cp[k : k + 1, lane(j)], 0.0)
            r.pre[rows, lane(j)] = acc
            r.inp[rows, lane(j)] = (acc * sigmoid(acc)).astype(BF16)
        return 0

    lax.fori_loop(0, T // 64, conv, 0)
    own[6].wait()
    W = d.R + 2 * N
    r.xd[:, 0:W] = dot(r.inp[...], r.xp[...], 1, 1).astype(BF16)
    xd_near = net.send(r.xd, r.xdn, ms, core)

    def chips(src, near_copy, near, far):
        near_copy.wait()
        src[...] = (src[...].astype(F32) + near[...].astype(F32)).astype(BF16)
        return net.batch([(src, far.at[k - 1], *net.at(0, 2 * k)) for k in range(1, F // 2)], far)

    def chips_total(src, batch, far):
        batch.wait()
        tot = src[:, 0:W].astype(F32)
        for k in range(F // 2 - 1):
            tot = tot + far[k, :, 0:W].astype(F32)
        return tot

    xd_far = chips(r.xd, xd_near, r.xdn, r.xdr)
    relay_rows(r.cot, c_direct, c_beside)
    wg_near = w_relay(1, wg_far)
    perm = to_scan(d, 0)
    for c in [own[4], own[5]] + c_beside:
        c.wait()
    for c in range(0, D, 256):
        r.cot[:, c : c + 256] = dot(perm, r.cot[:, c : c + 256]).astype(BF16)
    for c in range(0, CL, 256):
        r.gg[0:T, c : c + 256] = dot(r.cot[...], r.ow[c : c + 256, :], 1, 1)
    xd = chips_total(r.xd, xd_far, r.xdr)
    own[7].wait()
    low = xd[:, : d.R].astype(BF16)
    r.xd[:, 0 : d.R] = low
    for c in range(0, CL, 256):
        r.dtpre[:, c : c + 256] = dot(low, r.wdt[:, c : c + 256])

    def steps(i, acc):
        rows = pl.ds(pl.multiple_of(i * 64, 64), 64)
        age = r.rel[pl.ds(pl.multiple_of(i * 64 + HG * V, V), 64), :]
        out = []
        for j in range(NB):
            z = r.dtpre[rows, lane(j)] + r.cp[5:6, lane(j)]
            dt = jnp.maximum(z, 0.0) + jnp.log1p(jnp.exp(-jnp.abs(z)))
            r.dtpre[rows, lane(j)] = z
            e = jnp.where(age == 0.0, RESET, dt)
            r.dtd[rows, lane(j)] = e
            r.u[rows, lane(j)] = dt * r.inp[rows, lane(j)].astype(F32)
            out.append(acc[j] + jnp.sum(e.reshape(8, V, LN), axis=0))
        return tuple(out)

    sums = lax.fori_loop(0, T // 64, steps, tuple(jnp.zeros((V, LN), F32) for _ in range(NB)))
    for j in range(NB):
        whole, t = sums[j], 1
        while t < H:
            low_half = lax.rem(lax.div(hidx, t), 2) == 0
            whole = whole + jnp.where(low_half, pltpu.roll(whole, V - t, 0), pltpu.roll(whole, t, 0))
            t *= 2
        r.sd[0:V, lane(j)] = sums[j]
        r.tot[:, lane(j)] = whole
    tots = net.batch([(r.tot, r.totr.at[k - 1], *net.at(k, 0)) for k in range(1, S)], r.totr)
    bc = xd[:, d.R : W]
    hi = bc.astype(BF16)
    rest = (bc - hi.astype(F32)).astype(BF16)
    both = jnp.concatenate([hi, rest], axis=1)
    for n in range(0, 2 * N, 4):
        row = lax.rem(lax.broadcasted_iota(jnp.int32, (4 * N, 4 * LN), 0), 2 * N)
        col = lax.div(lax.broadcasted_iota(jnp.int32, (4 * N, 4 * LN), 1), LN) + n
        pick = jnp.where(row == col, 1.0, 0.0).astype(BF16)
        r.bcb[:, n * LN : (n + 4) * LN] = dot(both, pick).astype(r.bcb.dtype)

    half = N // 2
    row_n = lambda n: slice(n * V, (n + 1) * V)
    dec_of = lambda n, j: jnp.broadcast_to(r.dec[n : n + 1, lane(j)], (V, LN))

    def state_scan(j):
        dn = [dec_of(n, j) for n in range(N)]

        def ahead(q, hs):
            hs = list(hs)
            rows = pl.ds(pl.multiple_of(q * 2 * V, 2 * V), 2 * V)
            t, w = r.dtd[rows, lane(j)], r.u[rows, lane(j)]
            for n in range(N):
                b = r.bcb[rows, lane(n)].astype(F32)
                for p in (TOP, BOT):
                    hs[n] = jnp.exp2(t[p] * dn[n]) * hs[n] + w[p] * b[p]
            return tuple(hs)

        hs = lax.fori_loop(0, Q // 2, ahead, tuple(jnp.zeros((V, LN), F32) for _ in range(N)))
        for n in range(N):
            r.ends[0, row_n(n), lane(j)] = hs[n]

    def adjoint_scan(j):
        dn = [dec_of(n, j) for n in range(N)]

        def behind(q, gs):
            gs = list(gs)
            rows = pl.ds(pl.multiple_of((Q - 2 - 2 * q) * V, 2 * V), 2 * V)
            t, g0 = r.dtd[rows, lane(j)], r.gy[rows, lane(j)]
            for n in range(N):
                c = r.bcb[rows, lane(N + n)].astype(F32)
                for p in (BOT, TOP):
                    gs[n] = jnp.exp2(t[p] * dn[n]) * (gs[n] + g0[p] * c[p])
            return tuple(gs)

        gs = lax.fori_loop(0, Q // 2, behind, tuple(jnp.zeros((V, LN), F32) for _ in range(N)))
        for n in range(N):
            r.ends[1, row_n(n), lane(j)] = gs[n]

    def piece_ends(j, way):
        one = r.sd[0:V, lane(j)]
        tiles = []
        for n0 in range(0, N, H):
            a = jnp.zeros((V, LN), F32)
            for t in range(H):
                fac = jnp.exp2(one * dec_of(n0 + t, j))
                e = r.ends[way, row_n(n0 + t), lane(j)]
                x = e
                for h in range(1, H):
                    at = H - 1 - h if way else h
                    x = jnp.where(hidx == at, fac * pltpu.roll(x, V - 1 if way else 1, 0) + e, x)
                a = jnp.where(hidx == t, turn(x, t if way else t - (H - 1)), a)
            tiles.append(a)
        for i in range(0, len(tiles), 2):
            band = slice(i * V, (i + 2) * V)
            r.epack[way, j, band, :] = jnp.concatenate(tiles[i : i + 2], axis=0).astype(BF16)
        for k in range(1, S):
            ps, pf = net.at(k, 0)
            copy = net.remote(r.epack.at[way, j], r.eget.at[j, k - 1], *state_sems[j], ps, pf)
            pl.when(ps < ms if way else ps > ms)(copy.start)

    def turn(x, by):
        return x if by % V == 0 else pltpu.roll(x, by % V, 0)

    def begin(j, copies):
        copies.wait_send()
        copies.wait_recv()
        tiles = N // H
        dn = []
        for i in range(tiles):
            x = dec_of(i * H, j)
            for t in range(1, H):
                x = jnp.where(hidx == t, dec_of(i * H + t, j), x)
            dn.append(x)

        def join(p, acc):
            slot = lax.rem(ms + S - p, S) - 1
            tot = r.totr[slot, :, lane(j)]
            e = r.eget[j, slot].astype(F32)
            return tuple(jnp.exp2(tot * dn[i]) * acc[i] + e[row_n(i)] for i in range(tiles))

        zero = tuple(jnp.zeros((V, LN), F32) for _ in range(tiles))
        fw = lax.fori_loop(0, ms, join, zero)
        bw = lax.fori_loop(0, S - 1 - ms, lambda i, acc: join(S - 1 - i, acc), zero)
        one = r.sd[0:V, lane(j)]
        for i in range(tiles):
            for t in range(H):
                n = i * H + t
                fac = jnp.exp2(one * dec_of(n, j))
                x, y = turn(fw[i], -t), turn(bw[i], H - 1 - t)
                for h in range(1, H):
                    xn = pltpu.roll(fac * x + r.ends[0, row_n(n), lane(j)], 1, 0)
                    yn = pltpu.roll(fac * y + r.ends[1, row_n(n), lane(j)], V - 1, 0)
                    x = jnp.where(hidx == h, xn, x)
                    y = jnp.where(hidx == H - 1 - h, yn, y)
                r.start[0, row_n(n), lane(j)] = x
                r.start[1, row_n(n), lane(j)] = y

    def forward(j):
        dn = [dec_of(n, j) for n in range(N)]

        def ahead(q, hs):
            hs = list(hs)
            rows = pl.ds(pl.multiple_of(q * 2 * V, 2 * V), 2 * V)
            t, w = r.dtd[rows, lane(j)], r.u[rows, lane(j)]
            y = [jnp.zeros((V, LN), F32), jnp.zeros((V, LN), F32)]
            for n in range(N):
                b = r.bcb[rows, lane(n)].astype(F32)
                c = r.bcb[rows, lane(N + n)].astype(F32)
                keep = []
                for k, p in enumerate((TOP, BOT)):
                    m = jnp.exp2(t[p] * dn[n]) * hs[n]
                    hs[n] = m + w[p] * b[p]
                    y[k] = y[k] + c[p] * hs[n]
                    keep.append(m)
                r.m_s[j, rows, lane(n)] = jnp.concatenate(keep, axis=0).astype(BF16)
            r.y_s[rows, lane(j)] = jnp.concatenate(y, axis=0)
            return tuple(hs)

        lax.fori_loop(0, Q // 2, ahead, tuple(r.start[0, row_n(n), lane(j)] for n in range(N)))

    def backward(j):
        for n0 in range(0, N, half):
            dn = [dec_of(n, j) for n in range(n0, n0 + half)]

            def behind(i, carry, n0=n0, dn=dn):
                gs, gd = list(carry[0]), list(carry[1])
                rows = pl.ds(pl.multiple_of((Q - 2 - 2 * i) * V, 2 * V), 2 * V)
                t, w, g0 = r.dtd[rows, lane(j)], r.u[rows, lane(j)], r.gy[rows, lane(j)]
                t0 = jnp.where(t == RESET, 0.0, t)
                gu = [jnp.zeros((V, LN), F32), jnp.zeros((V, LN), F32)]
                gt = [jnp.zeros((V, LN), F32), jnp.zeros((V, LN), F32)]
                for i in range(half):
                    n = n0 + i
                    b = r.bcb[rows, lane(n)].astype(F32)
                    c = r.bcb[rows, lane(N + n)].astype(F32)
                    m = r.m_s[j, rows, lane(n)].astype(F32)
                    pc = g0 * (m + w * b)
                    pb = [None, None]
                    gc = g0 * c
                    for k, p in ((1, BOT), (0, TOP)):
                        g = gs[i] + gc[p]
                        pb[k] = g * w[p]
                        gu[k] = gu[k] + g * b[p]
                        x = g * m[p]
                        gt[k] = gt[k] + x * dn[i]
                        gd[i] = gd[i] + x * t0[p]
                        gs[i] = jnp.exp2(t[p] * dn[i]) * g
                    pb = jnp.concatenate(pb, axis=0)
                    if j > 0:
                        pb = pb + r.x_s[rows, lane(n)].astype(F32)
                        pc = pc + r.x_s[rows, lane(N + n)].astype(F32)
                    r.x_s[rows, lane(n)] = pb.astype(r.x_s.dtype)
                    r.x_s[rows, lane(N + n)] = pc.astype(r.x_s.dtype)
                gu, gt = jnp.concatenate(gu, axis=0), jnp.concatenate(gt, axis=0)
                if n0 > 0:
                    gu = gu + r.gsc[rows, lane(j)]
                    gt = gt + r.y_s[rows, lane(j)]
                r.gsc[rows, lane(j)] = gu
                r.y_s[rows, lane(j)] = gt
                return tuple(gs), tuple(gd)

            zero = tuple(jnp.zeros((V, LN), F32) for _ in range(half))
            first = tuple(r.start[1, row_n(n), lane(j)] for n in range(n0, n0 + half))
            _, gd = lax.fori_loop(0, Q // 2, behind, (first, zero))
            for i in range(half):
                dec = r.dec[n0 + i : n0 + i + 1, lane(j)] * (1.0 / LOG2E)
                r.rowsum[8 + n0 + i : 9 + n0 + i, lane(j)] = (
                    jnp.sum(gd[i], axis=0, keepdims=True) * dec
                )

    def gating(j):
        def body(i, sk):
            rows = pl.ds(pl.multiple_of(i * 64, 64), 64)
            x = r.inp[rows, lane(j)].astype(F32)
            mixed = r.y_s[rows, lane(j)] + r.cp[6:7, lane(j)] * x
            g = r.gate[rows, lane(j)]
            s = sigmoid(g)
            r.gated[rows, lane(j)] = (mixed * (g * s)).astype(BF16)
            r.ggate[rows, lane(j)] = (
                r.gg[rows, lane(j)] * mixed * s * (1.0 + g * (1.0 - s))
            ).astype(BF16)
            p = r.gy[rows, lane(j)] * x
            return sk + jnp.sum(p.reshape(8, V, LN), axis=0)

        sk = lax.fori_loop(0, T // 64, body, jnp.zeros((V, LN), F32))
        r.rowsum[6:7, lane(j)] = jnp.sum(sk, axis=0, keepdims=True)

    def put(dst, first, res):
        n = dst.shape[1]
        for t in range(res.shape[0] // n):
            dst[first // n + t] = res[t * n : (t + 1) * n].astype(dst.dtype)

    def put_split(dst, first, res):
        n = dst.shape[2]
        for t in range(res.shape[0] // n):
            s, f = divmod(first // n + t, F)
            dst[s, f] = res[t * n : (t + 1) * n].astype(dst.dtype)

    levels = list(range(S.bit_length() - 1))
    orders = (levels, [1, 0] + levels[2:])

    def start_sum(name, out, t, spread):
        parts = getattr(r, name + t), getattr(r, name + t + "n"), getattr(r, out + t)
        return Scatter(net, *parts, orders["ab".index(t)], spread)

    def sum_pair(name, out, spread):
        return [start_sum(name, out, t, spread) for t in "ab"]

    def both_halves(putter, name, first, res):
        n = getattr(r, name + "a").shape[-1]
        putter(getattr(r, name + "a"), first, res[:, :n])
        putter(getattr(r, name + "b"), first, res[:, n:])

    def step(sums, count=S - 2):
        for _ in range(count):
            for one in sums:
                one.step(1)

    back0 = from_scan(d, 0)
    cut = r.giwga.shape[-1]

    def gate_grads(t, cols):
        r.gatn[:, cols] = dot(back0, r.ggate[0:T, cols]).astype(BF16)
        for c in range(0, D, 256):
            res = dot(r.normed[0:T, c : c + 256], r.gatn[:, cols], 0, 0)
            put_split(getattr(r, "giwg" + t), c, res)
        return start_sum("giwg", "o_wg", t, True)

    r.rowsum[...] = jnp.zeros_like(r.rowsum)
    state_sems = [net.pair() for _ in range(NB)]
    states = [
        net.remote(r.eget.at[j], r.eget.at[j], *state_sems[j], *net.at(0, 1)) for j in range(NB)
    ]
    for j in range(NB):
        state_scan(j)
        piece_ends(j, 0)
    for c in [own[3], w_beside[1]] + wg_near:
        c.wait()
    for c in range(0, CL, 256):
        r.gate[:, c : c + 256] = dot(r.big[HG * V :, :], r.w[1, :, c : c + 256])

    def gys(i, _):
        rows = pl.ds(pl.multiple_of(i * 64, 64), 64)
        for j in range(NB):
            g = r.gate[rows, lane(j)]
            r.gy[rows, lane(j)] = r.gg[rows, lane(j)] * (g * sigmoid(g))
        return 0

    lax.fori_loop(0, T // 64, gys, 0)
    for j in range(NB):
        adjoint_scan(j)
        piece_ends(j, 1)
    tots.wait()
    for j in range(NB):
        begin(j, states[j])
        forward(j)
        gating(j)
        if (j + 1) * LN == cut:
            sum_g = [gate_grads("a", slice(0, cut))]
        if j == NB - 2:
            backward(0)
    late = list(range(1, NB))

    sum_g.append(gate_grads("b", slice(cut, CL)))
    for j in range(NB):
        both_halves(put, "gow", j * LN, dot(r.gated[0:T, lane(j)], r.cot[...], 0, 0))
    r.gated[0:T, :] = dot(back0, r.gated[0:T, :]).astype(BF16)
    for c in range(0, D, 256):
        r.cot[:, c : c + 256] = dot(r.gated[0:T, :], r.ow[:, c : c + 256]).astype(BF16)
    outs = Rows(net, core, r.cot, r.hid, r.outr)
    for i, j in enumerate(late):
        backward(j)
        if i == 0:
            outs.cross()
            sum_o = sum_pair("gow", "o_out", False)
        if j == NB - 2:
            step(sum_g, S // 2)
    step(sum_o, S // 4)
    def finish(i, acc):
        rows = pl.ds(pl.multiple_of(i * 64, 64), 64)
        out = []
        for j in range(NB):
            x = r.inp[rows, lane(j)].astype(F32)
            z = r.dtpre[rows, lane(j)]
            gu = r.gsc[rows, lane(j)]
            gt = r.y_s[rows, lane(j)] * (1.0 / LOG2E) + gu * x
            dt = jnp.maximum(z, 0.0) + jnp.log1p(jnp.exp(-jnp.abs(z)))
            gz = gt * sigmoid(z)
            r.ggate[rows, lane(j)] = gz.astype(BF16)
            r.gsc[rows, lane(j)] = gu * dt + r.gy[rows, lane(j)] * r.cp[6:7, lane(j)]
            out.append(acc[j] + jnp.sum(gz.reshape(8, V, LN), axis=0))
        return tuple(out)

    db = lax.fori_loop(0, T // 64, finish, tuple(jnp.zeros((V, LN), F32) for _ in range(NB)))
    for j in range(NB):
        r.rowsum[5:6, lane(j)] = jnp.sum(db[j], axis=0, keepdims=True)
    r.gx[:, 0 : d.R] = dot(r.ggate[0:T, :], r.wdt[...], 1, 1).astype(BF16)
    acc = jnp.zeros((T, 2 * N), F32)
    for n in range(0, 2 * N, 4):
        row = lax.div(lax.broadcasted_iota(jnp.int32, (4 * LN, 2 * N), 0), LN) + n
        col = lax.broadcasted_iota(jnp.int32, (4 * LN, 2 * N), 1)
        pick = jnp.where(row == col, 1.0, 0.0).astype(BF16)
        acc = acc + dot(r.x_s[:, n * LN : (n + 4) * LN].astype(BF16), pick)
    r.gx[:, d.R : W] = acc.astype(BF16)
    gx_near = net.send(r.gx, r.gxn, ms, core)
    gx_far = chips(r.gx, gx_near, r.gxn, r.gxr)

    step(sum_g, S - 2 - S // 2)
    step(sum_o, S // 2 - S // 4)
    gwdt = dot(r.ggate[0:T, :], r.xd[:, 0 : d.R], 0, 0)

    gxd = chips_total(r.gx, gx_far, r.gxr).astype(BF16)
    step(sum_o, S - 2 - S // 2)
    pad = HG * V
    r.gg[0:pad, :] = jnp.zeros((pad, CL), F32)
    r.gg[pad + T :, :] = jnp.zeros((pad, CL), F32)
    for c in range(0, CL, 256):
        r.gg[pad : pad + T, c : c + 256] = r.gsc[:, c : c + 256] + dot(gxd, r.xp[:, c : c + 256])

    def act(i, acc):
        r0 = pl.multiple_of(i * 64, 64)
        rows = pl.ds(r0, 64)
        shift = pl.ds(pl.multiple_of(r0 + pad, V), 64)
        age = r.rel[shift, :]
        out = []
        for j in range(NB):
            p = r.pre[rows, lane(j)]
            q = sigmoid(p)
            g = r.gg[shift, lane(j)] * q * (1.0 + p * (1.0 - q))
            r.gg[shift, lane(j)] = g
            a = list(acc[j])
            a[4] = a[4] + jnp.sum(g.reshape(8, V, LN), axis=0)
            for k in range(d.K):
                back = d.K - 1 - k
                xs = r.xb[pl.ds(pl.multiple_of(r0 + (HG - back) * V, V), 64), lane(j)]
                t = jnp.where(age >= back, g * xs, 0.0)
                a[k] = a[k] + jnp.sum(t.reshape(8, V, LN), axis=0)
            out.append(tuple(a))
        return tuple(out)

    zero = tuple(tuple(jnp.zeros((V, LN), F32) for _ in range(5)) for _ in range(NB))
    acc = lax.fori_loop(0, T // 64, act, zero)
    for j in range(NB):
        for k in range(5):
            r.rowsum[k : k + 1, lane(j)] = jnp.sum(acc[j][k], axis=0, keepdims=True)

    def gather_taps(i, _):
        r0 = pl.multiple_of(i * 32, 32)
        for j in range(NB):
            acc = jnp.zeros((32, LN), F32)
            for k in range(d.K):
                back = d.K - 1 - k
                src = pl.ds(pl.multiple_of(r0 + back * V, V), 32)
                acc = acc + jnp.where(
                    r.rel[src, :] >= back, r.gg[src, lane(j)] * r.cp[k : k + 1, lane(j)], 0.0
                )
            r.gated[pl.ds(r0, 32), lane(j)] = acc.astype(BF16)
        return 0

    lax.fori_loop(0, d.TE // 32, gather_taps, 0)
    r.ggate[...] = dot(from_scan(d, HG), r.gated[...]).astype(BF16)
    for c in range(0, D, LN):
        both_halves(put_split, "giwx", c, dot(r.normed[:, c : c + LN], r.ggate[...], 0, 0))
    sum_x = sum_pair("giwx", "o_wx", True)
    r.y_s[0:CL, 0:LN] = r.rowsum[...].T
    r.y_s[0:CL, LN : LN + W] = dot(r.inp[...], gxd, 0, 0)
    r.y_s[0:CL, LN + W : 2 * LN] = jnp.zeros((CL, LN - W), F32)
    r.y_s[0:CL, 32 : 32 + d.R] = gwdt
    put(r.small, 0, r.y_s[0:CL, 0 : 2 * LN])
    sum_s = Scatter(net, r.small, r.small_n, r.o_small, orders[1], False)
    for c in range(0, D, 256):
        g = dot(r.ggate[...], r.w[0, c : c + 256, :], 1, 1)
        r.hid[0:T, c : c + 256] = (
            g[0:T] + dot(r.gatn[...], r.w[1, c : c + 256, :], 1, 1)
        ).astype(BF16)
        r.hid[T:, c : c + 256] = g[T:].astype(BF16)
    def gains(i, acc):
        rows = pl.ds(pl.multiple_of(i * 64, 64), 64)
        t = r.hid[rows, :].astype(F32) * r.normed[rows, :].astype(F32)
        return acc + jnp.sum(t.reshape(8, V, D), axis=0)

    gtot = lax.fori_loop(0, d.NAT // 64, gains, jnp.zeros((V, D), F32)) / r.gain[...]
    gtot = jnp.sum(gtot, axis=0, keepdims=True)
    n = D // S
    for s in range(S):
        r.gg8[s] = gtot[:, s * n : (s + 1) * n]
    gns = Rows(net, core, r.hid, r.m_s.at[0, :, pl.ds(0, D)], r.o_gn)
    for k in range(F):
        ps, pf = net.at(-1, k)
        net.send(r.hid.at[pl.ds(T + pf * TAIL, TAIL)], r.o_gnh.at[mf], ps, pf)
    step(sum_x, 2)
    gns.cross()
    step([sum_s], 2)

    i, j = net.pair()

    def gain_copy(k):
        ps, pf = lax.rem(ms + lax.div(k, F), S), lax.rem(mf + lax.rem(k, F), F)
        return net.remote(r.gg8.at[ps], r.o_gain.at[k], i, j, ps, pf)

    def gain_send(k, _):
        gain_copy(k).start()
        return 0

    lax.fori_loop(1, S * F, gain_send, 0)
    net.local(r.gg8.at[ms], r.o_gain.at[0])
    others = r.o_gain.at[pl.ds(1, S * F - 1)]
    gain_all = net.remote(others, others, i, j, *net.at(0, 1))
    step(sum_x + [sum_s])
    gain_all.wait_send()
    gain_all.wait_recv()
    net.drain()
    assert (net.s_used, net.r_used) == semaphores(d), (net.s_used, net.r_used)


def close(d, gn, gnh, outr, hid, cot, gain, wxa, wxb, wga, wgb, outa, outb, small, ggain,
          o_out, o_hid, o_gain, o_in, o_conv, o_cb, o_db, o_sk, o_xp, o_dt, o_al, o_gout):
    F, T, tok, D = d.F, d.T, d.tok, d.D
    W = d.R + 2 * d.N

    def rows_(i, _):
        rows = pl.ds(pl.multiple_of(i * 16, 16), 16)
        h = hid[rows, :].astype(F32)
        g, o = jnp.zeros((16, D), F32), jnp.zeros((16, D), F32)
        for k in range(gn.shape[0]):
            g = g + gn[k, rows, :].astype(F32)
            o = o + outr[k, rows, :].astype(F32)
        late = jnp.zeros((TAIL, D), F32)
        for f in range(F):
            late = late + gnh[f].astype(F32)
        g = g + jnp.where(i == tok // 16 - 1, late, 0.0)
        inv = lax.rsqrt(jnp.mean(h * h, axis=-1, keepdims=True) + EPS)
        g2 = g * gain[...]
        mean = jnp.mean(g2 * h, axis=-1, keepdims=True)
        o_hid[0, rows, :] = cot[rows, :].astype(F32) + inv * g2 - h * (inv * inv * inv) * mean
        o_out[0, rows, :] = (h + o).astype(BF16)
        return 0

    lax.fori_loop(0, tok // 16, rows_, 0)
    for f in range(F):
        at = f * d.CL
        for part in (wxa, wxb, wga, wgb):
            n = part.shape[-1]
            at = d.DI + f * d.CL if part is wga else at
            o_in[:, at : at + n] = part[0, f].astype(F32) + part[1, f].astype(F32)
            at += n
    o_gout[:, : D // 2] = outa[0].astype(F32) + outa[1].astype(F32)
    o_gout[:, D // 2 :] = outb[0].astype(F32) + outb[1].astype(F32)
    sm = jnp.sum(small[...].astype(F32), axis=0)
    first = sm[:, 0:LN].T
    for i, o_row in enumerate((o_cb, o_db, o_sk)):
        o_row[...] = first[4 + i : 5 + i, :]
    o_conv[...] = first[0 : d.K, :]
    o_al[...] = first[V : V + d.N, :]
    o_dt[...] = sm[:, 32 : 32 + d.R]
    o_xp[...] = sm[:, LN : LN + W]
    tot = jnp.sum(ggain[...], axis=0)
    n, k = D // d.S, D // d.S // F
    row = lax.broadcasted_iota(jnp.int32, (n, k), 0) - lax.axis_index("fsdp") * k
    pick = jnp.where(row == lax.broadcasted_iota(jnp.int32, (n, k), 1), 1.0, 0.0)
    one = lax.dot_general(
        tot + jnp.zeros((V, n), F32), pick, (((1,), (0,)), ((), ())),
        precision=lax.Precision.HIGHEST, preferred_element_type=F32,
    )
    o_gain[...] = one[0:1, :]


def semaphores(d):
    far = d.F // 2 - 1
    one = (d.F - 1) + 2 * (2 * far + 1) + d.F + 2 * (2 * far) + 2 + 2 * (6 * far) + 2 * (2 * far + 1) + d.F
    one += 2 * 2 + 1 + d.NB + 1
    return one + 7 * d.S, one + 7 * (d.S - 1) + 17


def vm(*shape, dtype=F32):
    return pltpu.VMEM(shape, dtype)


def per_device(
    d, hidden, cluster_lengths, norm_gain, in_weight, conv_weight, conv_bias, xproj_weight,
    dt_weight, dt_bias, a_log, skip, out_weight, cotangent,
):
    S, F, T, D, CL, N, NB, R = d.S, d.F, d.T, d.D, d.CL, d.N, d.NB, d.R
    ins = dict(
        hidden=hidden[0], lens=cluster_lengths, norm_gain=norm_gain, conv_bias=conv_bias,
        dt_bias=dt_bias, skip=skip, in_weight=in_weight, conv_weight=conv_weight.T,
        xproj_weight=xproj_weight.T, dt_weight=dt_weight.T, a_log=a_log.T, out_weight=out_weight,
        cotangent=cotangent[0],
    )
    DS, CS, W, W2 = D // S, CL // S, R + 2 * N, 2 * LN
    TP = T + 2 * HG * V
    rt = BF16 if CS >= 16 else F32
    half, most = CL // 2, CL // LN * 3 // 4 * LN or CL // 2
    two = lambda name, shape, t: {name + k: (shape, t) for k in "ab"}
    outs = dict(
        o_gn=((F // 2 + 1, d.tok, D), BF16), o_gnh=((F, TAIL, D), BF16),
        outr=((F // 2 + 1, d.tok, D), BF16), gain=((1, D), F32),
        o_wxa=((2, F, DS // F, most), BF16), o_wxb=((2, F, DS // F, CL - most), BF16),
        **two("o_wg", (2, F, DS // F, half), BF16),
        **two("o_out", (2, CS, D // 2), rt), o_small=((2, CS, W2), rt), o_gain=((S * F, 1, DS), F32),
    )
    small_t = T <= 512
    EP = N // d.H * V
    scratch = dict(
        hid=((d.NAT, D), BF16), normed=((d.NAT, D), BF16), big=((d.TE, D), BF16),
        cot=((T, D), BF16), w=((2, D, CL), BF16), ow=((CL, D), BF16),
        xp=((W, CL), BF16), wdt=((R, CL), BF16), cw=((d.K, CL), BF16), al=((N, CL), BF16),
        row_cb=((CL,), BF16), row_db=((CL,), BF16), row_sk=((CL,), BF16), row_g=((D // F,), BF16),
        row_l=((1, d.clusters), jnp.int32), pg=((F, V, D // F), F32), pg_own=((V, D // F), F32), cp=((V, CL), F32), dec=((N, CL), F32), rel=((TP, LN), F32),
        xb=((d.TE, CL), F32), gate=((T, CL), F32), pre=((T, CL), F32), inp=((T, CL), BF16),
        xd=((T, LN), BF16), xdn=((T, LN), BF16), xdr=((F // 2 - 1, T, LN), BF16),
        dtpre=((T, CL), F32), dtd=((T, CL), F32), u=((T, CL), F32), gg=((TP, CL), F32),
        gy=((T, CL), F32), bcb=((T, 2 * N * LN), F32 if small_t else BF16),
        sd=((V, CL), F32), tot=((V, CL), F32), totr=((S - 1, V, CL), F32),
        ends=((2, N * V, CL), F32), epack=((2, NB, EP, LN), BF16), eget=((NB, S - 1, EP, LN), BF16),
        start=((2, N * V, CL), F32), m_s=((NB, T, N * LN), BF16), y_s=((T, CL), F32),
        gsc=((T, CL), F32), x_s=((T, 2 * N * LN), F32 if small_t else BF16),
        gated=((d.TE, CL), BF16), ggate=((d.NAT, CL), BF16), gatn=((T, CL), BF16),
        gx=((T, LN), BF16), gxn=((T, LN), BF16), gxr=((F // 2 - 1, T, LN), BF16), rowsum=((LN, CL), F32),

        small=((S, CS, W2), rt), small_n=((S - 2, CS, W2), rt),
        gg8=((S, 1, DS), F32),
    )
    for name, wide in (("giwg", half), ("giwx", most)):
        for t, n in (("a", wide), ("b", CL - wide)):
            scratch[name + t] = ((S, F, DS // F, n), BF16)
            scratch[name + t + "n"] = ((S - 2, F, DS // F, n), BF16)
    for t in "ab":
        scratch["gow" + t] = ((S, CS, D // 2), rt)
        scratch["gow" + t + "n"] = ((S - 2, CS, D // 2), rt)
    names = list(ins) + list(outs) + list(scratch) + ["ssem", "rsem"]
    sends, gets = semaphores(d)
    res = pl.pallas_call(
        functools.partial(layer, d, names),
        out_shape=[jax.ShapeDtypeStruct(*o) for o in outs.values()],
        in_specs=[pl.BlockSpec(memory_space=pl.ANY)] * len(ins),
        out_specs=[
            pl.BlockSpec(memory_space=pltpu.VMEM if k == "gain" else pl.ANY) for k in outs
        ],
        scratch_shapes=[vm(*s, dtype=t) for s, t in scratch.values()]
        + [pltpu.SemaphoreType.DMA((sends,)), pltpu.SemaphoreType.DMA((gets,))],
        compiler_params=pltpu.CompilerParams(
            collective_id=0, has_side_effects=True, vmem_limit_bytes=65250 * 1024
        ),
    )(*ins.values())
    o = dict(zip(outs, res))
    fin = kernel(
        functools.partial(close, d),
        (o["o_gn"], o["o_gnh"], o["outr"], hidden[0], cotangent[0], o["gain"])
        + tuple(o[k] for k in ("o_wxa", "o_wxb", "o_wga", "o_wgb", "o_outa", "o_outb", "o_small", "o_gain")),
        [((1, d.tok, D), BF16), ((1, d.tok, D), F32), ((1, DS // F), F32), ((DS // F, 2 * d.DI), F32),
         ((d.K, CS), F32), ((1, CS), F32), ((1, CS), F32), ((1, CS), F32), ((CS, W), F32), ((CS, R), F32),
         ((N, CS), F32), ((CS, D), F32)],
    )
    out, g_hid, g_gain, g_in, g_conv, g_cb, g_db, g_sk, g_xp, g_dt, g_al, g_out = fin
    return (
        out, g_hid, g_gain[0], g_in, g_conv.T, g_cb[0], g_xp, g_dt, g_db[0], g_al.T, g_sk[0], g_out,
    )


def solution(mesh):
    S, F = mesh.shape["seq"], mesh.shape["fsdp"]

    def run(*args):
        tok, D = args[0].shape[1] // S, args[0].shape[2]
        d = Dims(
            S, F, tok, D, args[11].shape[0], args[9].shape[1], args[7].shape[1], args[4].shape[1],
            args[1].shape[1],
        )
        return jax.shard_map(
            functools.partial(per_device, d),
            mesh=mesh,
            in_specs=(
                P("fsdp", "seq", None), P("fsdp", None), P("fsdp"), P("fsdp", None),
                P("fsdp", None), P("fsdp"), P("fsdp", None), P("fsdp", None), P("fsdp"),
                P("fsdp", None), P("fsdp"), P("fsdp", None), P("fsdp", "seq", None),
            ),
            out_specs=(
                P("fsdp", "seq", None), P("fsdp", "seq", None), P(("seq", "fsdp")),
                P(("seq", "fsdp"), None), P(("seq", "fsdp"), None), P(("seq", "fsdp")),
                P(("seq", "fsdp"), None), P(("seq", "fsdp"), None), P(("seq", "fsdp")),
                P(("seq", "fsdp"), None), P(("seq", "fsdp")), P(("seq", "fsdp"), None),
            ),
            check_vma=False,
        )(*args)

    return run
```

```python
import functools
import math

import jax
import jax.numpy as jnp
from jax import lax
from jax.experimental import pallas as pl
from jax.experimental.pallas import tpu as pltpu
from jax.sharding import PartitionSpec as P

EPS = 1e-05
V = 8
LN = 128
HG = 4
TAIL = 16
LOG2E = 1.0 / math.log(2.0)
RESET = 1e30
F32 = jnp.float32
TOP, BOT = slice(0, V), slice(V, 2 * V)
BF16 = jnp.bfloat16
MESH = pl.DeviceIdType.MESH


class Dims:
    def __init__(self, S, F, tok, D, DI, N, R, K, clusters):
        self.S, self.F, self.tok, self.D, self.DI = S, F, tok, D, DI
        self.N, self.R, self.K, self.clusters = N, R, K, clusters
        self.H = V // F
        self.Q = tok // self.H
        self.T = F * tok
        self.TE = (self.Q + HG) * V
        self.NAT = F * (tok + TAIL)
        self.CL = DI // F
        self.NB = self.CL // LN


def dot(a, b, ca=1, cb=0):
    return lax.dot_general(a, b, (((ca,), (cb,)), ((), ())), preferred_element_type=F32)


def sigmoid(v):
    return 1.0 / (1.0 + jnp.exp(-v))


def kernel(body, args, outs, scratch=()):
    return pl.pallas_call(
        body,
        out_shape=[jax.ShapeDtypeStruct(s, t) for s, t in outs],
        in_specs=[pl.BlockSpec(memory_space=pltpu.VMEM)] * len(args),
        out_specs=[pl.BlockSpec(memory_space=pltpu.VMEM)] * len(outs),
        scratch_shapes=list(scratch),
        compiler_params=pltpu.CompilerParams(vmem_limit_bytes=60 * 1024 * 1024),
    )(*args)


def lane(j):
    return slice(j * LN, (j + 1) * LN)


def natural_of(d, row, halo):
    q = lax.div(row, V) - halo
    v = lax.rem(row, V)
    f = lax.div(v, d.H)
    p = lax.rem(v, d.H) * d.Q + q
    return jnp.where(p >= 0, f * d.tok + p, d.T + f * TAIL + TAIL + p)


def to_scan(d, halo):
    rows, cols = (d.TE, d.NAT) if halo else (d.T, d.T)
    want = natural_of(d, lax.broadcasted_iota(jnp.int32, (rows, 1), 0), halo)
    have = lax.broadcasted_iota(jnp.int32, (rows, cols), 1)
    return jnp.where(have == want, 1.0, 0.0).astype(BF16)


def from_scan(d, halo):
    rows, cols = (d.NAT, d.TE) if halo else (d.T, d.T)
    want = natural_of(d, lax.broadcasted_iota(jnp.int32, (1, cols), 1), halo)
    have = lax.broadcasted_iota(jnp.int32, (rows, cols), 0)
    return jnp.where(have == want, 1.0, 0.0).astype(BF16)


class Refs:
    pass


class Copy:
    def __init__(self, copy, remote):
        self.copy, self.sent, self.got = copy, not remote, False
        self.remote = remote

    def wait_send(self):
        if not self.sent:
            self.copy.wait_send()
            self.sent = True

    def wait_recv(self):
        if not self.got:
            if self.remote:
                self.copy.wait_recv()
            else:
                self.copy.wait()
            self.got = True

    def wait(self):
        self.wait_send()
        self.wait_recv()


class Batch:
    def __init__(self, net, sends, whole):
        i, j = net.pair()
        self.open = True
        for src, dst, ps, pf in sends:
            net.remote(src, dst, i, j, ps, pf).start()
        self.all = net.remote(whole, whole, i, j, *net.at(0, 1))

    def wait(self):
        if self.open:
            self.all.wait_send()
            self.all.wait_recv()
            self.open = False


class Net:
    def __init__(self, d, ssem, rsem):
        self.d, self.ssem, self.rsem, self.s_used, self.r_used = d, ssem, rsem, 0, 0
        self.ms, self.mf = lax.axis_index("seq"), lax.axis_index("fsdp")
        self.open = []

    def at(self, ds, df):
        return lax.rem(self.ms + ds % self.d.S, self.d.S), lax.rem(self.mf + df % self.d.F, self.d.F)

    def pair(self):
        self.s_used += 1
        self.r_used += 1
        return self.s_used - 1, self.r_used - 1

    def remote(self, src, dst, i, j, ps, pf):
        return pltpu.make_async_remote_copy(
            src, dst, self.ssem.at[i], self.rsem.at[j], {"seq": ps, "fsdp": pf}, device_id_type=MESH
        )

    def start(self, copy, remote):
        copy.start()
        self.open.append(Copy(copy, remote))
        return self.open[-1]

    def send(self, src, dst, ps, pf):
        i, j = self.pair()
        return self.start(self.remote(src, dst, i, j, ps, pf), True)

    def batch(self, sends, whole):
        self.open.append(Batch(self, sends, whole))
        return self.open[-1]

    def local(self, src, dst):
        self.r_used += 1
        return self.start(pltpu.make_async_copy(src, dst, self.rsem.at[self.r_used - 1]), False)

    def drain(self):
        for c in self.open:
            c.wait()


def flip(value, mask):
    bit = 0
    out = value
    while 1 << bit <= mask:
        if mask >> bit & 1:
            out = out + (1 - 2 * lax.rem(lax.div(value, 1 << bit), 2)) * (1 << bit)
        bit += 1
    return out


class Scatter:
    def __init__(self, net, mine, near, out, bits, spread, split=True):
        self.net, self.mine, self.near, self.out = net, mine, near, out
        self.bits, self.spread, self.split = bits, spread, split
        self.tails, self.queue, self.last = [], [], {}
        self.into = net.r_used
        net.r_used += 1
        slot = 0
        self.slots = []
        for level in range(len(bits) - 1):
            sides = self.sides(level)
            self.slots.append({side: slot + i for i, side in enumerate(sides)})
            slot += len(sides)
            self.queue += [(level, side) for side in sides]
        self.copies = {}
        for side in self.sides(0):
            self.push(0, side)
        self.done = 0
        net.open.append(self)

    def sides(self, level):
        masks = [0]
        for bit in reversed(self.bits[level + 1 :]):
            masks = [m | 1 << bit for m in masks] + masks
        return masks

    def push(self, level, side):
        net = self.net
        to = flip(net.ms, 1 << self.bits[level])
        self.copies[level, side] = net.send(
            self.mine.at[flip(to, side)], self.near.at[self.slots[level][side]], to, net.mf
        )

    def step(self, count=1000):
        net = self.net
        for level, side in self.queue[self.done : self.done + count]:
            self.done += 1
            self.copies[level, side].wait()
            at = flip(net.ms, side)
            both = self.mine[at].astype(F32) + self.near[self.slots[level][side]].astype(F32)
            self.mine[at] = both.astype(self.mine.dtype)
            bit = 1 << self.bits[level + 1]
            if level + 2 < len(self.bits):
                if side & bit:
                    self.push(level + 1, side ^ bit)
            else:
                self.finish(at, 1 if side else 0)

    def finish(self, at, side):
        net, d = self.net, self.net.d
        i = net.s_used
        net.s_used += 1
        if self.spread:
            for g in range(1 - side, d.F):
                f = lax.rem(net.mf + g, d.F)
                src = self.mine.at[at, f] if self.split else self.mine.at[at]
                net.remote(src, self.out.at[side, net.mf], i, self.into, at, f).start()
            if not side:
                src = self.mine.at[at, net.mf] if self.split else self.mine.at[at]
                pltpu.make_async_copy(src, self.out.at[0, net.mf], net.rsem.at[self.into]).start()
            sent = self.out.at[side] if side else self.out.at[0, pl.ds(0, d.F - 1)]
            self.tails.append((None, net.remote(sent, sent, i, self.into, *net.at(0, 1))))
        else:
            spot = net.mf * d.S + at
            away = spot != net.ms * d.F + net.mf
            src, dst = self.mine.at[at], self.out.at[side]
            far = net.remote(src, dst, i, self.into, lax.div(spot, d.F), lax.rem(spot, d.F))
            near = pltpu.make_async_copy(src, dst, net.rsem.at[self.into])
            pl.when(away)(far.start)
            pl.when(jnp.logical_not(away))(near.start)
            self.tails.append((away, far))

    def wait(self):
        self.step()
        for away, c in self.tails:
            if away is None:
                c.wait_send()
            else:
                pl.when(away)(c.wait_send)
        net = self.net
        net.remote(self.out, self.out, 0, self.into, *net.at(0, 1)).wait_recv()


class Rows:
    def __init__(self, net, core, src, land, out):
        self.net, self.src, self.land, self.out = net, src, land, out
        d = net.d
        self.rows = lambda f: src.at[pl.ds(f * d.tok, d.tok)]
        self.far = range(1, d.F // 2)
        step = lambda f, k: lax.rem(f + 2 * k, d.F)
        self.to = [step(net.mf, k) for k in self.far]
        self.near = [
            net.send(self.rows(step(core, k)), land.at[pl.ds((k - 1) * d.tok, d.tok)], net.ms, core)
            for k in self.far
        ]
        net.send(self.rows(core), out.at[1], net.ms, core)
        net.local(self.rows(net.mf), out.at[0])

    def cross(self):
        net, d = self.net, self.net.d
        for k, f, c in zip(self.far, self.to, self.near):
            c.wait()

            def add(i, _, k=k, f=f):
                here = pl.ds(pl.multiple_of(f * d.tok + i * 32, 32), 32)
                there = pl.ds(pl.multiple_of((k - 1) * d.tok + i * 32, 32), 32)
                self.src[here, :] = (
                    self.src[here, :].astype(F32) + self.land[there, :].astype(F32)
                ).astype(BF16)
                return 0

            lax.fori_loop(0, d.tok // 32, add, 0)
            net.send(self.rows(f), self.out.at[1 + k], net.ms, f)


def layer(d, names, *refs):
    r = Refs()
    for name, ref in zip(names, refs):
        setattr(r, name, ref)
    S, F, CL, T, N, Q, NB, D, tok, H = d.S, d.F, d.CL, d.T, d.N, d.Q, d.NB, d.D, d.tok, d.H
    DF = D // F
    net = Net(d, r.ssem, r.rsem)
    ms, mf = net.ms, net.mf
    core = mf + 1 - 2 * lax.rem(mf, 2)
    greet = [(i, k) for i in range(S) for k in range(F) if (i, k) != (0, 0)]
    bar = pltpu.get_barrier_semaphore()
    for ds, df in greet:
        ps, pf = net.at(-ds, -df)
        pl.semaphore_signal(bar, inc=1, device_id={"seq": ps, "fsdp": pf}, device_id_type=MESH)

    own = [
        net.local(r.hidden, r.hid.at[pl.ds(mf * tok, tok)]),
        net.local(r.norm_gain, r.row_g),
        net.local(r.in_weight.at[:, pl.ds(pl.multiple_of(mf * CL, LN), CL)], r.w.at[0, pl.ds(mf * DF, DF)]),
        net.local(
            r.in_weight.at[:, pl.ds(pl.multiple_of(d.DI + mf * CL, LN), CL)],
            r.w.at[1, pl.ds(mf * DF, DF)],
        ),
        net.local(r.cotangent, r.cot.at[pl.ds(mf * tok, tok)]),
        net.local(r.out_weight, r.ow),
        net.local(r.xproj_weight, r.xp),
        net.local(r.dt_weight, r.wdt),
        net.local(r.conv_weight, r.cw),
        net.local(r.a_log, r.al),
        net.local(r.lens, r.row_l),
        net.local(r.conv_bias, r.row_cb),
        net.local(r.dt_bias, r.row_db),
        net.local(r.skip, r.row_sk),
    ]
    pl.semaphore_wait(bar, len(greet))

    rows_of = lambda ref, f, n: ref.at[pl.ds(f * n, n)]
    same_core = [lax.rem(mf + 2 * k, F) for k in range(1, F // 2)]
    other_chip = [(lax.rem(mf + 2 * k, F), lax.rem(core + 2 * k, F)) for k in range(1, F // 2)]

    for i in (1, 10):
        own[i].wait()
    as_row = lambda ref: ref[...].astype(F32).reshape(1, ref.shape[-1])
    r.pg_own[0:1, :] = as_row(r.row_g)
    r.pg_own[1:2, 0 : d.clusters] = as_row(r.row_l)
    r.pg[mf] = r.pg_own[...]

    def spread_rows(src, dst):
        direct = [net.send(src, rows_of(dst, mf, tok), ms, f) for f in same_core]
        beside = [net.send(src, rows_of(dst, mf, tok), ms, core)]
        return direct, beside

    def relay_rows(dst, direct, beside):
        for k, c in enumerate(direct):
            c.wait()
            f = lax.rem(mf + F - 2 * (k + 1), F)
            beside.append(net.send(rows_of(dst, f, tok), rows_of(dst, f, tok), ms, core))

    def w_slice(g, f):
        return r.in_weight.at[:, pl.ds(pl.multiple_of(g * d.DI + f * CL, LN), CL)]

    quart, ring = lax.rem(ms, 4), ms - lax.rem(ms, 4)
    QF = DF // 4

    def w_far(g):
        out = []
        for pair in other_chip:
            for f in pair:
                src = r.in_weight.at[
                    pl.ds(quart * QF, QF), pl.ds(pl.multiple_of(g * d.DI + f * CL, LN), CL)
                ]
                out.append(net.send(src, r.w.at[g, pl.ds(mf * DF + quart * QF, QF)], ms, f))
        return out

    def w_relay(g, far):
        out = []
        i = 0
        for k in range(1, F // 2):
            for flip in (0, 1):
                far[i].wait_recv()
                i += 1
                f0 = lax.rem(mf + F - 2 * k, F)
                if flip:
                    f0 = f0 + 1 - 2 * lax.rem(f0, 2)
                place = r.w.at[g, pl.ds(f0 * DF + quart * QF, QF)]
                for t in (1, 2, 3):
                    out.append(net.send(place, place, ring + lax.rem(quart + t, 4), mf))
        return out

    wx_far = w_far(0)
    pgs = [net.send(r.pg_own, r.pg.at[mf], *net.at(0, k)) for k in range(1, F)]
    w_beside = [net.send(w_slice(g, core), r.w.at[g, pl.ds(mf * DF, DF)], ms, core) for g in (0, 1)]
    for c in wx_far:
        c.wait_send()
    h_direct, h_beside = spread_rows(r.hidden, r.hid)
    halo = [
        net.send(
            r.hidden.at[pl.ds(tok - TAIL, TAIL)],
            r.hid.at[pl.ds(T + mf * TAIL, TAIL)],
            *net.at(1, k),
        )
        for k in range(F)
    ]
    wx_near = w_relay(0, wx_far)
    for c in pgs + own[:1]:
        c.wait()
    for f in range(F):
        r.gain[0:1, f * DF : (f + 1) * DF] = r.pg[f, 0:1, :]
    sub = lax.broadcasted_iota(jnp.int32, (V, LN), 0)
    hidx = lax.rem(sub, H)
    stream = lax.div(sub, H)
    offs, run = [], jnp.zeros((V, LN), F32)
    for j in range(d.clusters - 1):
        for f in range(F):
            run = run + jnp.where(stream == f, r.pg[f, 1:2, j : j + 1], 0.0)
        offs.append(run)
    base = ms * tok + hidx * Q
    r.rel[0 : HG * V, :] = jnp.zeros((HG * V, LN), F32)
    r.rel[HG * V + T :, :] = jnp.zeros((HG * V, LN), F32)

    def mark(q, _):
        pos = (base + q).astype(F32)
        last = jnp.zeros((V, LN), F32)
        for o in offs:
            last = jnp.maximum(last, jnp.where(o <= pos, o, 0.0))
        r.rel[pl.ds(pl.multiple_of((q + HG) * V, V), V), :] = jnp.where(pos == 0.0, 0.5, pos - last)
        return 0

    lax.fori_loop(0, Q, mark, 0)
    for c in own[8:]:
        c.wait()
    r.cp[0 : d.K, :] = r.cw[...].astype(F32)
    for i, ref in enumerate((r.row_cb, r.row_db, r.row_sk)):
        r.cp[4 + i : 5 + i, :] = as_row(ref)
    r.dec[...] = -LOG2E * jnp.exp(r.al[...].astype(F32))
    for c in h_direct:
        c.wait_send()
    c_direct, c_beside = spread_rows(r.cotangent, r.cot)
    wg_far = w_far(1)
    for k, c in enumerate(h_direct):
        c.wait_recv()
        f = lax.rem(mf + F - 2 * (k + 1), F)
        h_beside.append(net.send(rows_of(r.hid, f, tok), rows_of(r.hid, f, tok), ms, core))
    perm = to_scan(d, HG)

    def rms(first, count):
        def body(i, _):
            rows = pl.ds(pl.multiple_of(first + i * 64, 64), 64)
            h = r.hid[rows, :].astype(F32)
            inv = lax.rsqrt(jnp.mean(h * h, axis=-1, keepdims=True) + EPS)
            r.normed[rows, :] = (h * inv * r.gain[...]).astype(BF16)
            return 0

        lax.fori_loop(0, count // 64, body, 0)

    for k in range(F // 2):
        rms(lax.rem(mf + F - 2 * k, F) * tok, tok)
    for k, c in enumerate(h_beside):
        c.wait()
        rms(lax.rem(core + F - 2 * k, F) * tok, tok)
    for c in halo:
        c.wait()
    rms(T, F * TAIL)
    for c in range(0, D, 256):
        r.big[:, c : c + 256] = dot(perm, r.normed[:, c : c + 256]).astype(BF16)
    own[2].wait()
    w_beside[0].wait()
    for c in wx_near:
        c.wait()
    for c in range(0, CL, 256):
        r.xb[:, c : c + 256] = (
            dot(r.big[:, :], r.w[0, :, c : c + 256]).astype(BF16).astype(F32)
        )

    def conv(i, _):
        r0 = pl.multiple_of(i * 64, 64)
        rows = pl.ds(r0, 64)
        age = r.rel[pl.ds(pl.multiple_of(r0 + HG * V, V), 64), :]
        for j in range(NB):
            acc = jnp.zeros((64, LN), F32) + r.cp[4:5, lane(j)]
            for k in range(d.K):
                back = d.K - 1 - k
                xs = r.xb[pl.ds(pl.multiple_of(r0 + (HG - back) * V, V), 64), lane(j)]
                acc = acc + jnp.where(age >= back, xs * r.cp[k : k + 1, lane(j)], 0.0)
            r.pre[rows, lane(j)] = acc
            r.inp[rows, lane(j)] = (acc * sigmoid(acc)).astype(BF16)
        return 0

    own[6].wait()
    W = d.R + 2 * N
    bands = [pl.ds(0, T // 2), pl.ds(T // 2, T // 2)]
    beside = lambda src, dst, band: net.send(src.at[band], dst.at[band], ms, core)
    xd_near = []
    for i, band in enumerate(bands):
        lax.fori_loop(i * T // 128, (i + 1) * T // 128, conv, 0)
        r.xd[band, 0:W] = dot(r.inp[band, :], r.xp[...], 1, 1).astype(BF16)
        if i == 0:
            xd_near.append(beside(r.xd, r.xdn, band))
    xd_near.append(beside(r.xd, r.xdn, bands[1]))

    def chips(src, near_copy, near, far, band):
        near_copy.wait()
        rows = src.at[band]
        rows[...] = (rows[...].astype(F32) + near[band, :].astype(F32)).astype(BF16)
        return net.batch(
            [(rows, far.at[k - 1, band], *net.at(0, 2 * k)) for k in range(1, F // 2)],
            far.at[:, band],
        )

    def chips_total(src, batches, far):
        for c in batches:
            c.wait()
        tot = src[:, 0:W].astype(F32)
        for k in range(F // 2 - 1):
            tot = tot + far[k, :, 0:W].astype(F32)
        return tot

    xd_far = [chips(r.xd, c, r.xdn, r.xdr, band) for c, band in zip(xd_near, bands)]
    relay_rows(r.cot, c_direct, c_beside)
    wg_near = w_relay(1, wg_far)
    perm = to_scan(d, 0)
    for c in [own[4], own[5]] + c_beside:
        c.wait()
    for c in range(0, D, 256):
        r.cot[:, c : c + 256] = dot(perm, r.cot[:, c : c + 256]).astype(BF16)
    for c in range(0, CL, 256):
        r.gg[0:T, c : c + 256] = dot(r.cot[...], r.ow[c : c + 256, :], 1, 1)
    xd = chips_total(r.xd, xd_far, r.xdr)
    own[7].wait()
    low = xd[:, : d.R].astype(BF16)
    r.xd[:, 0 : d.R] = low
    for c in range(0, CL, 256):
        r.dtpre[:, c : c + 256] = dot(low, r.wdt[:, c : c + 256])

    def steps(i, acc):
        rows = pl.ds(pl.multiple_of(i * 64, 64), 64)
        age = r.rel[pl.ds(pl.multiple_of(i * 64 + HG * V, V), 64), :]
        out = []
        for j in range(NB):
            z = r.dtpre[rows, lane(j)] + r.cp[5:6, lane(j)]
            dt = jnp.maximum(z, 0.0) + jnp.log1p(jnp.exp(-jnp.abs(z)))
            r.dtpre[rows, lane(j)] = z
            e = jnp.where(age == 0.0, RESET, dt)
            r.dtd[rows, lane(j)] = e
            r.u[rows, lane(j)] = dt * r.inp[rows, lane(j)].astype(F32)
            out.append(acc[j] + jnp.sum(e.reshape(8, V, LN), axis=0))
        return tuple(out)

    sums = lax.fori_loop(0, T // 64, steps, tuple(jnp.zeros((V, LN), F32) for _ in range(NB)))
    for j in range(NB):
        whole, t = sums[j], 1
        while t < H:
            low_half = lax.rem(lax.div(hidx, t), 2) == 0
            whole = whole + jnp.where(low_half, pltpu.roll(whole, V - t, 0), pltpu.roll(whole, t, 0))
            t *= 2
        r.sd[0:V, lane(j)] = sums[j]
        r.tot[:, lane(j)] = whole
    tots = net.batch([(r.tot, r.totr.at[k - 1], *net.at(k, 0)) for k in range(1, S)], r.totr)
    bc = xd[:, d.R : W]
    hi = bc.astype(BF16)
    rest = (bc - hi.astype(F32)).astype(BF16)
    both = jnp.concatenate([hi, rest], axis=1)
    for n in range(0, 2 * N, 4):
        row = lax.rem(lax.broadcasted_iota(jnp.int32, (4 * N, 4 * LN), 0), 2 * N)
        col = lax.div(lax.broadcasted_iota(jnp.int32, (4 * N, 4 * LN), 1), LN) + n
        pick = jnp.where(row == col, 1.0, 0.0).astype(BF16)
        r.bcb[:, n * LN : (n + 4) * LN] = dot(both, pick).astype(r.bcb.dtype)

    half = N // 2
    row_n = lambda n: slice(n * V, (n + 1) * V)
    dec_of = lambda n, j: jnp.broadcast_to(r.dec[n : n + 1, lane(j)], (V, LN))

    def state_scan(j):
        dn = [dec_of(n, j) for n in range(N)]

        def ahead(q, hs):
            hs = list(hs)
            rows = pl.ds(pl.multiple_of(q * 2 * V, 2 * V), 2 * V)
            t, w = r.dtd[rows, lane(j)], r.u[rows, lane(j)]
            for n in range(N):
                b = r.bcb[rows, lane(n)].astype(F32)
                for p in (TOP, BOT):
                    hs[n] = jnp.exp2(t[p] * dn[n]) * hs[n] + w[p] * b[p]
            return tuple(hs)

        hs = lax.fori_loop(0, Q // 2, ahead, tuple(jnp.zeros((V, LN), F32) for _ in range(N)))
        for n in range(N):
            r.ends[0, row_n(n), lane(j)] = hs[n]

    def adjoint_scan(j):
        dn = [dec_of(n, j) for n in range(N)]

        def behind(q, gs):
            gs = list(gs)
            rows = pl.ds(pl.multiple_of((Q - 2 - 2 * q) * V, 2 * V), 2 * V)
            t, g0 = r.dtd[rows, lane(j)], r.gy[rows, lane(j)]
            for n in range(N):
                c = r.bcb[rows, lane(N + n)].astype(F32)
                for p in (BOT, TOP):
                    gs[n] = jnp.exp2(t[p] * dn[n]) * (gs[n] + g0[p] * c[p])
            return tuple(gs)

        gs = lax.fori_loop(0, Q // 2, behind, tuple(jnp.zeros((V, LN), F32) for _ in range(N)))
        for n in range(N):
            r.ends[1, row_n(n), lane(j)] = gs[n]

    def piece_ends(j, way):
        one = r.sd[0:V, lane(j)]
        tiles = []
        for n0 in range(0, N, H):
            a = jnp.zeros((V, LN), F32)
            for t in range(H):
                fac = jnp.exp2(one * dec_of(n0 + t, j))
                e = r.ends[way, row_n(n0 + t), lane(j)]
                x = e
                for h in range(1, H):
                    at = H - 1 - h if way else h
                    x = jnp.where(hidx == at, fac * pltpu.roll(x, V - 1 if way else 1, 0) + e, x)
                a = jnp.where(hidx == t, turn(x, t if way else t - (H - 1)), a)
            tiles.append(a)
        for i in range(0, len(tiles), 2):
            band = slice(i * V, (i + 2) * V)
            r.epack[way, j, band, :] = jnp.concatenate(tiles[i : i + 2], axis=0).astype(BF16)
        for k in range(1, S):
            ps, pf = net.at(k, 0)
            copy = net.remote(r.epack.at[way, j], r.eget.at[j, k - 1], *state_sems[j], ps, pf)
            pl.when(ps < ms if way else ps > ms)(copy.start)

    def turn(x, by):
        return x if by % V == 0 else pltpu.roll(x, by % V, 0)

    def begin(j, copies):
        copies.wait_send()
        copies.wait_recv()
        tiles = N // H
        dn = []
        for i in range(tiles):
            x = dec_of(i * H, j)
            for t in range(1, H):
                x = jnp.where(hidx == t, dec_of(i * H + t, j), x)
            dn.append(x)

        def join(p, acc):
            slot = lax.rem(ms + S - p, S) - 1
            tot = r.totr[slot, :, lane(j)]
            e = r.eget[j, slot].astype(F32)
            return tuple(jnp.exp2(tot * dn[i]) * acc[i] + e[row_n(i)] for i in range(tiles))

        zero = tuple(jnp.zeros((V, LN), F32) for _ in range(tiles))
        fw = lax.fori_loop(0, ms, join, zero)
        bw = lax.fori_loop(0, S - 1 - ms, lambda i, acc: join(S - 1 - i, acc), zero)
        one = r.sd[0:V, lane(j)]
        for i in range(tiles):
            for t in range(H):
                n = i * H + t
                fac = jnp.exp2(one * dec_of(n, j))
                x, y = turn(fw[i], -t), turn(bw[i], H - 1 - t)
                for h in range(1, H):
                    xn = pltpu.roll(fac * x + r.ends[0, row_n(n), lane(j)], 1, 0)
                    yn = pltpu.roll(fac * y + r.ends[1, row_n(n), lane(j)], V - 1, 0)
                    x = jnp.where(hidx == h, xn, x)
                    y = jnp.where(hidx == H - 1 - h, yn, y)
                r.start[0, row_n(n), lane(j)] = x
                r.start[1, row_n(n), lane(j)] = y

    def forward(j):
        dn = [dec_of(n, j) for n in range(N)]

        def ahead(q, hs):
            hs = list(hs)
            rows = pl.ds(pl.multiple_of(q * 2 * V, 2 * V), 2 * V)
            t, w = r.dtd[rows, lane(j)], r.u[rows, lane(j)]
            y = [jnp.zeros((V, LN), F32), jnp.zeros((V, LN), F32)]
            for n in range(N):
                b = r.bcb[rows, lane(n)].astype(F32)
                c = r.bcb[rows, lane(N + n)].astype(F32)
                keep = []
                for k, p in enumerate((TOP, BOT)):
                    m = jnp.exp2(t[p] * dn[n]) * hs[n]
                    hs[n] = m + w[p] * b[p]
                    y[k] = y[k] + c[p] * hs[n]
                    keep.append(m)
                r.m_s[j, rows, lane(n)] = jnp.concatenate(keep, axis=0).astype(BF16)
            r.y_s[rows, lane(j)] = jnp.concatenate(y, axis=0)
            return tuple(hs)

        lax.fori_loop(0, Q // 2, ahead, tuple(r.start[0, row_n(n), lane(j)] for n in range(N)))

    def backward(j):
        for n0 in range(0, N, half):
            dn = [dec_of(n, j) for n in range(n0, n0 + half)]

            def behind(i, carry, n0=n0, dn=dn):
                gs, gd = list(carry[0]), list(carry[1])
                rows = pl.ds(pl.multiple_of((Q - 2 - 2 * i) * V, 2 * V), 2 * V)
                t, w, g0 = r.dtd[rows, lane(j)], r.u[rows, lane(j)], r.gy[rows, lane(j)]
                t0 = jnp.where(t == RESET, 0.0, t)
                gu = [jnp.zeros((V, LN), F32), jnp.zeros((V, LN), F32)]
                gt = [jnp.zeros((V, LN), F32), jnp.zeros((V, LN), F32)]
                for i in range(half):
                    n = n0 + i
                    b = r.bcb[rows, lane(n)].astype(F32)
                    c = r.bcb[rows, lane(N + n)].astype(F32)
                    m = r.m_s[j, rows, lane(n)].astype(F32)
                    pc = g0 * (m + w * b)
                    pb = [None, None]
                    gc = g0 * c
                    for k, p in ((1, BOT), (0, TOP)):
                        g = gs[i] + gc[p]
                        pb[k] = g * w[p]
                        gu[k] = gu[k] + g * b[p]
                        x = g * m[p]
                        gt[k] = gt[k] + x * dn[i]
                        gd[i] = gd[i] + x * t0[p]
                        gs[i] = jnp.exp2(t[p] * dn[i]) * g
                    pb = jnp.concatenate(pb, axis=0)
                    if j > 0:
                        pb = pb + r.x_s[rows, lane(n)].astype(F32)
                        pc = pc + r.x_s[rows, lane(N + n)].astype(F32)
                    r.x_s[rows, lane(n)] = pb.astype(r.x_s.dtype)
                    r.x_s[rows, lane(N + n)] = pc.astype(r.x_s.dtype)
                gu, gt = jnp.concatenate(gu, axis=0), jnp.concatenate(gt, axis=0)
                if n0 > 0:
                    gu = gu + r.gsc[rows, lane(j)]
                    gt = gt + r.y_s[rows, lane(j)]
                r.gsc[rows, lane(j)] = gu
                r.y_s[rows, lane(j)] = gt
                return tuple(gs), tuple(gd)

            zero = tuple(jnp.zeros((V, LN), F32) for _ in range(half))
            first = tuple(r.start[1, row_n(n), lane(j)] for n in range(n0, n0 + half))
            _, gd = lax.fori_loop(0, Q // 2, behind, (first, zero))
            for i in range(half):
                dec = r.dec[n0 + i : n0 + i + 1, lane(j)] * (1.0 / LOG2E)
                r.rowsum[8 + n0 + i : 9 + n0 + i, lane(j)] = (
                    jnp.sum(gd[i], axis=0, keepdims=True) * dec
                )

    def gating(j):
        def body(i, sk):
            rows = pl.ds(pl.multiple_of(i * 64, 64), 64)
            x = r.inp[rows, lane(j)].astype(F32)
            mixed = r.y_s[rows, lane(j)] + r.cp[6:7, lane(j)] * x
            g = r.gate[rows, lane(j)]
            s = sigmoid(g)
            r.gated[rows, lane(j)] = (mixed * (g * s)).astype(BF16)
            r.ggate[rows, lane(j)] = (
                r.gg[rows, lane(j)] * mixed * s * (1.0 + g * (1.0 - s))
            ).astype(BF16)
            p = r.gy[rows, lane(j)] * x
            return sk + jnp.sum(p.reshape(8, V, LN), axis=0)

        sk = lax.fori_loop(0, T // 64, body, jnp.zeros((V, LN), F32))
        r.rowsum[6:7, lane(j)] = jnp.sum(sk, axis=0, keepdims=True)

    def put(dst, first, res):
        n = dst.shape[1]
        for t in range(res.shape[0] // n):
            dst[first // n + t] = res[t * n : (t + 1) * n].astype(dst.dtype)

    def put_split(dst, first, res):
        n = dst.shape[2]
        for t in range(res.shape[0] // n):
            s, f = divmod(first // n + t, F)
            dst[s, f] = res[t * n : (t + 1) * n].astype(dst.dtype)

    levels = list(range(S.bit_length() - 1))
    orders = (levels, [1, 0] + levels[2:])

    def start_sum(name, out, t, spread):
        parts = getattr(r, name + t), getattr(r, name + t + "n"), getattr(r, out + t)
        return Scatter(net, *parts, orders["ab".index(t)], spread)

    def sum_pair(name, out, spread):
        return [start_sum(name, out, t, spread) for t in "ab"]

    def both_halves(putter, name, first, res):
        n = getattr(r, name + "a").shape[-1]
        putter(getattr(r, name + "a"), first, res[:, :n])
        putter(getattr(r, name + "b"), first, res[:, n:])

    def step(sums, count=S - 2):
        for _ in range(count):
            for one in sums:
                one.step(1)

    back0 = from_scan(d, 0)
    cut = r.giwga.shape[-1]

    def gate_grads(t, cols):
        r.gatn[:, cols] = dot(back0, r.ggate[0:T, cols]).astype(BF16)
        for c in range(0, D, 256):
            res = dot(r.normed[0:T, c : c + 256], r.gatn[:, cols], 0, 0)
            put_split(getattr(r, "giwg" + t), c, res)
        return start_sum("giwg", "o_wg", t, True)

    r.rowsum[...] = jnp.zeros_like(r.rowsum)
    state_sems = [net.pair() for _ in range(NB)]
    states = [
        net.remote(r.eget.at[j], r.eget.at[j], *state_sems[j], *net.at(0, 1)) for j in range(NB)
    ]
    for j in range(NB):
        state_scan(j)
        piece_ends(j, 0)
    for c in [own[3], w_beside[1]] + wg_near:
        c.wait()
    for c in range(0, CL, 256):
        r.gate[:, c : c + 256] = dot(r.big[HG * V :, :], r.w[1, :, c : c + 256])

    def gys(i, _):
        rows = pl.ds(pl.multiple_of(i * 64, 64), 64)
        for j in range(NB):
            g = r.gate[rows, lane(j)]
            r.gy[rows, lane(j)] = r.gg[rows, lane(j)] * (g * sigmoid(g))
        return 0

    lax.fori_loop(0, T // 64, gys, 0)
    for j in range(NB):
        adjoint_scan(j)
        piece_ends(j, 1)
    tots.wait()
    for j in range(NB):
        begin(j, states[j])
        forward(j)
        gating(j)
        if (j + 1) * LN == cut:
            sum_g = [gate_grads("a", slice(0, cut))]
    level = S // 2

    sum_g.append(gate_grads("b", slice(cut, CL)))
    for c in range(0, CL, 256):
        both_halves(put, "gow", c, dot(r.gated[0:T, c : c + 256], r.cot[...], 0, 0))
    r.gated[0:T, :] = dot(back0, r.gated[0:T, :]).astype(BF16)
    for c in range(0, D, 256):
        r.cot[:, c : c + 256] = dot(r.gated[0:T, :], r.ow[:, c : c + 256]).astype(BF16)
    outs = Rows(net, core, r.cot, r.hid, r.outr)
    for j in range(NB):
        backward(j)
        if j == 0:
            outs.cross()
            sum_o = sum_pair("gow", "o_out", False)
        if j == 1:
            step(sum_g, level)
    step(sum_g, S - 2 - level)
    step(sum_o, level)
    def finish(i, acc):
        rows = pl.ds(pl.multiple_of(i * 64, 64), 64)
        out = []
        for j in range(NB):
            x = r.inp[rows, lane(j)].astype(F32)
            z = r.dtpre[rows, lane(j)]
            gu = r.gsc[rows, lane(j)]
            gt = r.y_s[rows, lane(j)] * (1.0 / LOG2E) + gu * x
            e = jnp.exp(-jnp.abs(z))
            dt = jnp.maximum(z, 0.0) + jnp.log1p(e)
            gz = gt * (jnp.where(z >= 0.0, 1.0, e) / (1.0 + e))
            r.ggate[rows, lane(j)] = gz.astype(BF16)
            r.gsc[rows, lane(j)] = gu * dt + r.gy[rows, lane(j)] * r.cp[6:7, lane(j)]
            out.append(acc[j] + jnp.sum(gz.reshape(8, V, LN), axis=0))
        return tuple(out)

    db = lax.fori_loop(0, T // 64, finish, tuple(jnp.zeros((V, LN), F32) for _ in range(NB)))
    for j in range(NB):
        r.rowsum[5:6, lane(j)] = jnp.sum(db[j], axis=0, keepdims=True)
    gx_near = []
    for band in bands:
        r.gx[band, 0 : d.R] = dot(r.ggate[band, :], r.wdt[...], 1, 1).astype(BF16)
        acc = jnp.zeros((T // 2, 2 * N), F32)
        for n in range(0, 2 * N, 4):
            row = lax.div(lax.broadcasted_iota(jnp.int32, (4 * LN, 2 * N), 0), LN) + n
            col = lax.broadcasted_iota(jnp.int32, (4 * LN, 2 * N), 1)
            pick = jnp.where(row == col, 1.0, 0.0).astype(BF16)
            acc = acc + dot(r.x_s[band, n * LN : (n + 4) * LN].astype(BF16), pick)
        r.gx[band, d.R : W] = acc.astype(BF16)
        gx_near.append(beside(r.gx, r.gxn, band))
    gx_far = [chips(r.gx, c, r.gxn, r.gxr, band) for c, band in zip(gx_near, bands)]
    gwdt = dot(r.ggate[0:T, :], r.xd[:, 0 : d.R], 0, 0)

    gxd = chips_total(r.gx, gx_far, r.gxr).astype(BF16)
    step(sum_o, S - 2 - level)
    pad = HG * V
    r.gg[0:pad, :] = jnp.zeros((pad, CL), F32)
    r.gg[pad + T :, :] = jnp.zeros((pad, CL), F32)
    for c in range(0, CL, 256):
        r.gg[pad : pad + T, c : c + 256] = r.gsc[:, c : c + 256] + dot(gxd, r.xp[:, c : c + 256])

    def act(i, acc):
        r0 = pl.multiple_of(i * 64, 64)
        rows = pl.ds(r0, 64)
        shift = pl.ds(pl.multiple_of(r0 + pad, V), 64)
        age = r.rel[shift, :]
        out = []
        for j in range(NB):
            p = r.pre[rows, lane(j)]
            q = sigmoid(p)
            g = r.gg[shift, lane(j)] * q * (1.0 + p * (1.0 - q))
            r.gg[shift, lane(j)] = g
            a = list(acc[j])
            a[4] = a[4] + jnp.sum(g.reshape(8, V, LN), axis=0)
            for k in range(d.K):
                back = d.K - 1 - k
                xs = r.xb[pl.ds(pl.multiple_of(r0 + (HG - back) * V, V), 64), lane(j)]
                t = jnp.where(age >= back, g * xs, 0.0)
                a[k] = a[k] + jnp.sum(t.reshape(8, V, LN), axis=0)
            out.append(tuple(a))
        return tuple(out)

    zero = tuple(tuple(jnp.zeros((V, LN), F32) for _ in range(5)) for _ in range(NB))
    acc = lax.fori_loop(0, T // 64, act, zero)
    for j in range(NB):
        for k in range(5):
            r.rowsum[k : k + 1, lane(j)] = jnp.sum(acc[j][k], axis=0, keepdims=True)

    def gather_taps(i, _):
        r0 = pl.multiple_of(i * 32, 32)
        for j in range(NB):
            acc = jnp.zeros((32, LN), F32)
            for k in range(d.K):
                back = d.K - 1 - k
                src = pl.ds(pl.multiple_of(r0 + back * V, V), 32)
                acc = acc + jnp.where(
                    r.rel[src, :] >= back, r.gg[src, lane(j)] * r.cp[k : k + 1, lane(j)], 0.0
                )
            r.gated[pl.ds(r0, 32), lane(j)] = acc.astype(BF16)
        return 0

    lax.fori_loop(0, d.TE // 32, gather_taps, 0)
    r.ggate[...] = dot(from_scan(d, HG), r.gated[...]).astype(BF16)
    sum_x, first = [], 0
    for t in "ab":
        part = getattr(r, "giwx" + t)
        cols = slice(first, first + part.shape[-1])
        first = cols.stop
        for c in range(0, D, 256):
            put_split(part, c, dot(r.normed[:, c : c + 256], r.ggate[:, cols], 0, 0))
        sum_x.append(start_sum("giwx", "o_wx", t, True))
    r.y_s[0:CL, 0:LN] = r.rowsum[...].T
    r.y_s[0:CL, LN : LN + W] = dot(r.inp[...], gxd, 0, 0)
    r.y_s[0:CL, LN + W : 2 * LN] = jnp.zeros((CL, LN - W), F32)
    r.y_s[0:CL, 32 : 32 + d.R] = gwdt
    put(r.small, 0, r.y_s[0:CL, 0 : 2 * LN])
    sum_s = Scatter(net, r.small, r.small_n, r.o_small, orders[1], False)
    for c in range(0, D, 256):
        g = dot(r.ggate[...], r.w[0, c : c + 256, :], 1, 1)
        r.hid[0:T, c : c + 256] = (
            g[0:T] + dot(r.gatn[...], r.w[1, c : c + 256, :], 1, 1)
        ).astype(BF16)
        r.hid[T:, c : c + 256] = g[T:].astype(BF16)
    def gains(i, acc):
        rows = pl.ds(pl.multiple_of(i * 64, 64), 64)
        t = r.hid[rows, :].astype(F32) * r.normed[rows, :].astype(F32)
        return acc + jnp.sum(t.reshape(8, V, D), axis=0)

    gtot = lax.fori_loop(0, d.NAT // 64, gains, jnp.zeros((V, D), F32)) / r.gain[...]
    gtot = jnp.sum(gtot, axis=0, keepdims=True)
    n = D // S
    for s in range(S):
        r.gg8[s] = gtot[:, s * n : (s + 1) * n]
    gns = Rows(net, core, r.hid, r.m_s.at[0, :, pl.ds(0, D)], r.o_gn)
    for k in range(F):
        ps, pf = net.at(-1, k)
        net.send(r.hid.at[pl.ds(T + pf * TAIL, TAIL)], r.o_gnh.at[mf], ps, pf)
    step(sum_x, 2)
    gns.cross()
    step([sum_s], 2)

    i, j = net.pair()

    def gain_copy(k):
        ps, pf = lax.rem(ms + lax.div(k, F), S), lax.rem(mf + lax.rem(k, F), F)
        return net.remote(r.gg8.at[ps], r.o_gain.at[k], i, j, ps, pf)

    def gain_send(k, _):
        gain_copy(k).start()
        return 0

    lax.fori_loop(1, S * F, gain_send, 0)
    net.local(r.gg8.at[ms], r.o_gain.at[0])
    others = r.o_gain.at[pl.ds(1, S * F - 1)]
    gain_all = net.remote(others, others, i, j, *net.at(0, 1))
    step(sum_x + [sum_s])
    gain_all.wait_send()
    gain_all.wait_recv()
    net.drain()
    assert (net.s_used, net.r_used) == semaphores(d), (net.s_used, net.r_used)


def close(d, gn, gnh, outr, hid, cot, gain, wxa, wxb, wga, wgb, outa, outb, small, ggain,
          o_out, o_hid, o_gain, o_in, o_conv, o_cb, o_db, o_sk, o_xp, o_dt, o_al, o_gout):
    F, T, tok, D = d.F, d.T, d.tok, d.D
    W = d.R + 2 * d.N

    def rows_(i, _):
        rows = pl.ds(pl.multiple_of(i * 16, 16), 16)
        h = hid[rows, :].astype(F32)
        g, o = jnp.zeros((16, D), F32), jnp.zeros((16, D), F32)
        for k in range(gn.shape[0]):
            g = g + gn[k, rows, :].astype(F32)
            o = o + outr[k, rows, :].astype(F32)
        late = jnp.zeros((TAIL, D), F32)
        for f in range(F):
            late = late + gnh[f].astype(F32)
        g = g + jnp.where(i == tok // 16 - 1, late, 0.0)
        inv = lax.rsqrt(jnp.mean(h * h, axis=-1, keepdims=True) + EPS)
        g2 = g * gain[...]
        mean = jnp.mean(g2 * h, axis=-1, keepdims=True)
        o_hid[0, rows, :] = cot[rows, :].astype(F32) + inv * g2 - h * (inv * inv * inv) * mean
        o_out[0, rows, :] = (h + o).astype(BF16)
        return 0

    lax.fori_loop(0, tok // 16, rows_, 0)
    for f in range(F):
        at = f * d.CL
        for part in (wxa, wxb, wga, wgb):
            n = part.shape[-1]
            at = d.DI + f * d.CL if part is wga else at
            o_in[:, at : at + n] = part[0, f].astype(F32) + part[1, f].astype(F32)
            at += n
    o_gout[:, : D // 2] = outa[0].astype(F32) + outa[1].astype(F32)
    o_gout[:, D // 2 :] = outb[0].astype(F32) + outb[1].astype(F32)
    sm = jnp.sum(small[...].astype(F32), axis=0)
    first = sm[:, 0:LN].T
    for i, o_row in enumerate((o_cb, o_db, o_sk)):
        o_row[...] = first[4 + i : 5 + i, :]
    o_conv[...] = first[0 : d.K, :]
    o_al[...] = first[V : V + d.N, :]
    o_dt[...] = sm[:, 32 : 32 + d.R]
    o_xp[...] = sm[:, LN : LN + W]
    tot = jnp.sum(ggain[...], axis=0)
    n, k = D // d.S, D // d.S // F
    row = lax.broadcasted_iota(jnp.int32, (n, k), 0) - lax.axis_index("fsdp") * k
    pick = jnp.where(row == lax.broadcasted_iota(jnp.int32, (n, k), 1), 1.0, 0.0)
    one = lax.dot_general(
        tot + jnp.zeros((V, n), F32), pick, (((1,), (0,)), ((), ())),
        precision=lax.Precision.HIGHEST, preferred_element_type=F32,
    )
    o_gain[...] = one[0:1, :]


def semaphores(d):
    far = d.F // 2 - 1
    one = (d.F - 1) + 2 * (2 * far + 1) + d.F + 2 * (2 * far) + 2 + 2 * (6 * far) + 2 * (2 * far + 1) + d.F
    one += 2 * 4 + 1 + d.NB + 1
    return one + 7 * d.S, one + 7 * (d.S - 1) + 17


def vm(*shape, dtype=F32):
    return pltpu.VMEM(shape, dtype)


def per_device(
    d, hidden, cluster_lengths, norm_gain, in_weight, conv_weight, conv_bias, xproj_weight,
    dt_weight, dt_bias, a_log, skip, out_weight, cotangent,
):
    S, F, T, D, CL, N, NB, R = d.S, d.F, d.T, d.D, d.CL, d.N, d.NB, d.R
    ins = dict(
        hidden=hidden[0], lens=cluster_lengths, norm_gain=norm_gain, conv_bias=conv_bias,
        dt_bias=dt_bias, skip=skip, in_weight=in_weight, conv_weight=conv_weight.T,
        xproj_weight=xproj_weight.T, dt_weight=dt_weight.T, a_log=a_log.T, out_weight=out_weight,
        cotangent=cotangent[0],
    )
    DS, CS, W, W2 = D // S, CL // S, R + 2 * N, 2 * LN
    TP = T + 2 * HG * V
    rt = BF16 if CS >= 16 else F32
    half, most = CL // 2, CL // LN * 3 // 4 * LN or CL // 2
    two = lambda name, shape, t: {name + k: (shape, t) for k in "ab"}
    outs = dict(
        o_gn=((F // 2 + 1, d.tok, D), BF16), o_gnh=((F, TAIL, D), BF16),
        outr=((F // 2 + 1, d.tok, D), BF16), gain=((1, D), F32),
        o_wxa=((2, F, DS // F, most), BF16), o_wxb=((2, F, DS // F, CL - most), BF16),
        **two("o_wg", (2, F, DS // F, half), BF16),
        **two("o_out", (2, CS, D // 2), rt), o_small=((2, CS, W2), rt), o_gain=((S * F, 1, DS), F32),
    )
    small_t = T <= 512
    EP = N // d.H * V
    scratch = dict(
        hid=((d.NAT, D), BF16), normed=((d.NAT, D), BF16), big=((d.TE, D), BF16),
        cot=((T, D), BF16), w=((2, D, CL), BF16), ow=((CL, D), BF16),
        xp=((W, CL), BF16), wdt=((R, CL), BF16), cw=((d.K, CL), BF16), al=((N, CL), BF16),
        row_cb=((CL,), BF16), row_db=((CL,), BF16), row_sk=((CL,), BF16), row_g=((D // F,), BF16),
        row_l=((1, d.clusters), jnp.int32), pg=((F, V, D // F), F32), pg_own=((V, D // F), F32), cp=((V, CL), F32), dec=((N, CL), F32), rel=((TP, LN), F32),
        xb=((d.TE, CL), F32), gate=((T, CL), F32), pre=((T, CL), F32), inp=((T, CL), BF16),
        xd=((T, LN), BF16), xdn=((T, LN), BF16), xdr=((F // 2 - 1, T, LN), BF16),
        dtpre=((T, CL), F32), dtd=((T, CL), F32), u=((T, CL), F32), gg=((TP, CL), F32),
        gy=((T, CL), F32), bcb=((T, 2 * N * LN), F32 if small_t else BF16),
        sd=((V, CL), F32), tot=((V, CL), F32), totr=((S - 1, V, CL), F32),
        ends=((2, N * V, CL), F32), epack=((2, NB, EP, LN), BF16), eget=((NB, S - 1, EP, LN), BF16),
        start=((2, N * V, CL), F32), m_s=((NB, T, N * LN), BF16), y_s=((T, CL), F32),
        gsc=((T, CL), F32), x_s=((T, 2 * N * LN), F32 if small_t else BF16),
        gated=((d.TE, CL), BF16), ggate=((d.NAT, CL), BF16), gatn=((T, CL), BF16),
        gx=((T, LN), BF16), gxn=((T, LN), BF16), gxr=((F // 2 - 1, T, LN), BF16), rowsum=((LN, CL), F32),

        small=((S, CS, W2), rt), small_n=((S - 2, CS, W2), rt),
        gg8=((S, 1, DS), F32),
    )
    for name, wide in (("giwg", half), ("giwx", most)):
        for t, n in (("a", wide), ("b", CL - wide)):
            scratch[name + t] = ((S, F, DS // F, n), BF16)
            scratch[name + t + "n"] = ((S - 2, F, DS // F, n), BF16)
    for t in "ab":
        scratch["gow" + t] = ((S, CS, D // 2), rt)
        scratch["gow" + t + "n"] = ((S - 2, CS, D // 2), rt)
    names = list(ins) + list(outs) + list(scratch) + ["ssem", "rsem"]
    sends, gets = semaphores(d)
    res = pl.pallas_call(
        functools.partial(layer, d, names),
        out_shape=[jax.ShapeDtypeStruct(*o) for o in outs.values()],
        in_specs=[pl.BlockSpec(memory_space=pl.ANY)] * len(ins),
        out_specs=[
            pl.BlockSpec(memory_space=pltpu.VMEM if k == "gain" else pl.ANY) for k in outs
        ],
        scratch_shapes=[vm(*s, dtype=t) for s, t in scratch.values()]
        + [pltpu.SemaphoreType.DMA((sends,)), pltpu.SemaphoreType.DMA((gets,))],
        compiler_params=pltpu.CompilerParams(
            collective_id=0, has_side_effects=True, vmem_limit_bytes=65250 * 1024
        ),
    )(*ins.values())
    o = dict(zip(outs, res))
    fin = kernel(
        functools.partial(close, d),
        (o["o_gn"], o["o_gnh"], o["outr"], hidden[0], cotangent[0], o["gain"])
        + tuple(o[k] for k in ("o_wxa", "o_wxb", "o_wga", "o_wgb", "o_outa", "o_outb", "o_small", "o_gain")),
        [((1, d.tok, D), BF16), ((1, d.tok, D), F32), ((1, DS // F), F32), ((DS // F, 2 * d.DI), F32),
         ((d.K, CS), F32), ((1, CS), F32), ((1, CS), F32), ((1, CS), F32), ((CS, W), F32), ((CS, R), F32),
         ((N, CS), F32), ((CS, D), F32)],
    )
    out, g_hid, g_gain, g_in, g_conv, g_cb, g_db, g_sk, g_xp, g_dt, g_al, g_out = fin
    return (
        out, g_hid, g_gain[0], g_in, g_conv.T, g_cb[0], g_xp, g_dt, g_db[0], g_al.T, g_sk[0], g_out,
    )


def solution(mesh):
    S, F = mesh.shape["seq"], mesh.shape["fsdp"]

    def run(*args):
        tok, D = args[0].shape[1] // S, args[0].shape[2]
        d = Dims(
            S, F, tok, D, args[11].shape[0], args[9].shape[1], args[7].shape[1], args[4].shape[1],
            args[1].shape[1],
        )
        return jax.shard_map(
            functools.partial(per_device, d),
            mesh=mesh,
            in_specs=(
                P("fsdp", "seq", None), P("fsdp", None), P("fsdp"), P("fsdp", None),
                P("fsdp", None), P("fsdp"), P("fsdp", None), P("fsdp", None), P("fsdp"),
                P("fsdp", None), P("fsdp"), P("fsdp", None), P("fsdp", "seq", None),
            ),
            out_specs=(
                P("fsdp", "seq", None), P("fsdp", "seq", None), P(("seq", "fsdp")),
                P(("seq", "fsdp"), None), P(("seq", "fsdp"), None), P(("seq", "fsdp")),
                P(("seq", "fsdp"), None), P(("seq", "fsdp"), None), P(("seq", "fsdp")),
                P(("seq", "fsdp"), None), P(("seq", "fsdp")), P(("seq", "fsdp"), None),
            ),
            check_vma=False,
        )(*args)

    return run
```

```python
import functools
import math

import jax
import jax.numpy as jnp
from jax import lax
from jax.experimental import pallas as pl
from jax.experimental.pallas import tpu as pltpu
from jax.sharding import PartitionSpec as P

EPS = 1e-05
V = 8
LN = 128
HG = 4
TAIL = 16
LOG2E = 1.0 / math.log(2.0)
RESET = 1e30
F32 = jnp.float32
TOP, BOT = slice(0, V), slice(V, 2 * V)
BF16 = jnp.bfloat16
MESH = pl.DeviceIdType.MESH


class Dims:
    def __init__(self, S, F, tok, D, DI, N, R, K, clusters):
        self.S, self.F, self.tok, self.D, self.DI = S, F, tok, D, DI
        self.N, self.R, self.K, self.clusters = N, R, K, clusters
        self.H = V // F
        self.Q = tok // self.H
        self.T = F * tok
        self.TE = (self.Q + HG) * V
        self.NAT = F * (tok + TAIL)
        self.CL = DI // F
        self.NB = self.CL // LN


def dot(a, b, ca=1, cb=0):
    return lax.dot_general(a, b, (((ca,), (cb,)), ((), ())), preferred_element_type=F32)


def sigmoid(v):
    return 1.0 / (1.0 + jnp.exp(-v))


def kernel(body, args, outs, scratch=()):
    return pl.pallas_call(
        body,
        out_shape=[jax.ShapeDtypeStruct(s, t) for s, t in outs],
        in_specs=[pl.BlockSpec(memory_space=pltpu.VMEM)] * len(args),
        out_specs=[pl.BlockSpec(memory_space=pltpu.VMEM)] * len(outs),
        scratch_shapes=list(scratch),
        compiler_params=pltpu.CompilerParams(vmem_limit_bytes=60 * 1024 * 1024),
    )(*args)


def lane(j):
    return slice(j * LN, (j + 1) * LN)


def natural_of(d, row, halo):
    q = lax.div(row, V) - halo
    v = lax.rem(row, V)
    f = lax.div(v, d.H)
    p = lax.rem(v, d.H) * d.Q + q
    return jnp.where(p >= 0, f * d.tok + p, d.T + f * TAIL + TAIL + p)


def to_scan(d, halo):
    rows, cols = (d.TE, d.NAT) if halo else (d.T, d.T)
    want = natural_of(d, lax.broadcasted_iota(jnp.int32, (rows, 1), 0), halo)
    have = lax.broadcasted_iota(jnp.int32, (rows, cols), 1)
    return jnp.where(have == want, 1.0, 0.0).astype(BF16)


def from_scan(d, halo):
    rows, cols = (d.NAT, d.TE) if halo else (d.T, d.T)
    want = natural_of(d, lax.broadcasted_iota(jnp.int32, (1, cols), 1), halo)
    have = lax.broadcasted_iota(jnp.int32, (rows, cols), 0)
    return jnp.where(have == want, 1.0, 0.0).astype(BF16)


class Refs:
    pass


class Copy:
    def __init__(self, copy, remote):
        self.copy, self.sent, self.got = copy, not remote, False
        self.remote = remote

    def wait_send(self):
        if not self.sent:
            self.copy.wait_send()
            self.sent = True

    def wait_recv(self):
        if not self.got:
            if self.remote:
                self.copy.wait_recv()
            else:
                self.copy.wait()
            self.got = True

    def wait(self):
        self.wait_send()
        self.wait_recv()


class Batch:
    def __init__(self, net, sends, whole):
        i, j = net.pair()
        self.open = True
        for src, dst, ps, pf in sends:
            net.remote(src, dst, i, j, ps, pf).start()
        self.all = net.remote(whole, whole, i, j, *net.at(0, 1))

    def wait(self):
        if self.open:
            self.all.wait_send()
            self.all.wait_recv()
            self.open = False


class Net:
    def __init__(self, d, ssem, rsem):
        self.d, self.ssem, self.rsem, self.s_used, self.r_used = d, ssem, rsem, 0, 0
        self.ms, self.mf = lax.axis_index("seq"), lax.axis_index("fsdp")
        self.open = []

    def at(self, ds, df):
        return lax.rem(self.ms + ds % self.d.S, self.d.S), lax.rem(self.mf + df % self.d.F, self.d.F)

    def pair(self):
        self.s_used += 1
        self.r_used += 1
        return self.s_used - 1, self.r_used - 1

    def remote(self, src, dst, i, j, ps, pf):
        return pltpu.make_async_remote_copy(
            src, dst, self.ssem.at[i], self.rsem.at[j], {"seq": ps, "fsdp": pf}, device_id_type=MESH
        )

    def start(self, copy, remote):
        copy.start()
        self.open.append(Copy(copy, remote))
        return self.open[-1]

    def send(self, src, dst, ps, pf):
        i, j = self.pair()
        return self.start(self.remote(src, dst, i, j, ps, pf), True)

    def batch(self, sends, whole):
        self.open.append(Batch(self, sends, whole))
        return self.open[-1]

    def local(self, src, dst):
        self.r_used += 1
        return self.start(pltpu.make_async_copy(src, dst, self.rsem.at[self.r_used - 1]), False)

    def drain(self):
        for c in self.open:
            c.wait()


def flip(value, mask):
    bit = 0
    out = value
    while 1 << bit <= mask:
        if mask >> bit & 1:
            out = out + (1 - 2 * lax.rem(lax.div(value, 1 << bit), 2)) * (1 << bit)
        bit += 1
    return out


class Scatter:
    def __init__(self, net, mine, near, out, bits, spread, split=True):
        self.net, self.mine, self.near, self.out = net, mine, near, out
        self.bits, self.spread, self.split = bits, spread, split
        self.tails, self.queue, self.last = [], [], {}
        self.into = net.r_used
        net.r_used += 1
        slot = 0
        self.slots = []
        for level in range(len(bits) - 1):
            sides = self.sides(level)
            self.slots.append({side: slot + i for i, side in enumerate(sides)})
            slot += len(sides)
            self.queue += [(level, side) for side in sides]
        self.copies = {}
        for side in self.sides(0):
            self.push(0, side)
        self.done = 0
        net.open.append(self)

    def sides(self, level):
        masks = [0]
        for bit in reversed(self.bits[level + 1 :]):
            masks = [m | 1 << bit for m in masks] + masks
        return masks

    def push(self, level, side):
        net = self.net
        to = flip(net.ms, 1 << self.bits[level])
        self.copies[level, side] = net.send(
            self.mine.at[flip(to, side)], self.near.at[self.slots[level][side]], to, net.mf
        )

    def step(self, count=1000):
        net = self.net
        for level, side in self.queue[self.done : self.done + count]:
            self.done += 1
            self.copies[level, side].wait()
            at = flip(net.ms, side)
            both = self.mine[at].astype(F32) + self.near[self.slots[level][side]].astype(F32)
            self.mine[at] = both.astype(self.mine.dtype)
            bit = 1 << self.bits[level + 1]
            if level + 2 < len(self.bits):
                if side & bit:
                    self.push(level + 1, side ^ bit)
            else:
                self.finish(at, 1 if side else 0)

    def finish(self, at, side):
        net, d = self.net, self.net.d
        i = net.s_used
        net.s_used += 1
        if self.spread:
            for g in range(1 - side, d.F):
                f = lax.rem(net.mf + g, d.F)
                src = self.mine.at[at, f] if self.split else self.mine.at[at]
                net.remote(src, self.out.at[side, net.mf], i, self.into, at, f).start()
            if not side:
                src = self.mine.at[at, net.mf] if self.split else self.mine.at[at]
                pltpu.make_async_copy(src, self.out.at[0, net.mf], net.rsem.at[self.into]).start()
            sent = self.out.at[side] if side else self.out.at[0, pl.ds(0, d.F - 1)]
            self.tails.append((None, net.remote(sent, sent, i, self.into, *net.at(0, 1))))
        else:
            spot = net.mf * d.S + at
            away = spot != net.ms * d.F + net.mf
            src, dst = self.mine.at[at], self.out.at[side]
            far = net.remote(src, dst, i, self.into, lax.div(spot, d.F), lax.rem(spot, d.F))
            near = pltpu.make_async_copy(src, dst, net.rsem.at[self.into])
            pl.when(away)(far.start)
            pl.when(jnp.logical_not(away))(near.start)
            self.tails.append((away, far))

    def wait(self):
        self.step()
        for away, c in self.tails:
            if away is None:
                c.wait_send()
            else:
                pl.when(away)(c.wait_send)
        net = self.net
        net.remote(self.out, self.out, 0, self.into, *net.at(0, 1)).wait_recv()


class Rows:
    def __init__(self, net, core, src, land, out):
        self.net, self.src, self.land, self.out = net, src, land, out
        d = net.d
        self.rows = lambda f: src.at[pl.ds(f * d.tok, d.tok)]
        self.far = range(1, d.F // 2)
        step = lambda f, k: lax.rem(f + 2 * k, d.F)
        self.to = [step(net.mf, k) for k in self.far]
        self.near = [
            net.send(self.rows(step(core, k)), land.at[pl.ds((k - 1) * d.tok, d.tok)], net.ms, core)
            for k in self.far
        ]
        net.send(self.rows(core), out.at[1], net.ms, core)
        net.local(self.rows(net.mf), out.at[0])

    def cross(self):
        net, d = self.net, self.net.d
        for k, f, c in zip(self.far, self.to, self.near):
            c.wait()

            def add(i, _, k=k, f=f):
                here = pl.ds(pl.multiple_of(f * d.tok + i * 32, 32), 32)
                there = pl.ds(pl.multiple_of((k - 1) * d.tok + i * 32, 32), 32)
                self.src[here, :] = (
                    self.src[here, :].astype(F32) + self.land[there, :].astype(F32)
                ).astype(BF16)
                return 0

            lax.fori_loop(0, d.tok // 32, add, 0)
            net.send(self.rows(f), self.out.at[1 + k], net.ms, f)


def layer(d, names, *refs):
    r = Refs()
    for name, ref in zip(names, refs):
        setattr(r, name, ref)
    S, F, CL, T, N, Q, NB, D, tok, H = d.S, d.F, d.CL, d.T, d.N, d.Q, d.NB, d.D, d.tok, d.H
    DF = D // F
    net = Net(d, r.ssem, r.rsem)
    ms, mf = net.ms, net.mf
    core = mf + 1 - 2 * lax.rem(mf, 2)
    greet = [(i, k) for i in range(S) for k in range(F) if (i, k) != (0, 0)]
    bar = pltpu.get_barrier_semaphore()
    for ds, df in greet:
        ps, pf = net.at(-ds, -df)
        pl.semaphore_signal(bar, inc=1, device_id={"seq": ps, "fsdp": pf}, device_id_type=MESH)

    own = [
        net.local(r.hidden, r.hid.at[pl.ds(mf * tok, tok)]),
        net.local(r.norm_gain, r.row_g),
        net.local(r.in_weight.at[:, pl.ds(pl.multiple_of(mf * CL, LN), CL)], r.w.at[0, pl.ds(mf * DF, DF)]),
        net.local(
            r.in_weight.at[:, pl.ds(pl.multiple_of(d.DI + mf * CL, LN), CL)],
            r.w.at[1, pl.ds(mf * DF, DF)],
        ),
        net.local(r.cotangent, r.cot.at[pl.ds(mf * tok, tok)]),
        net.local(r.out_weight, r.ow),
        net.local(r.xproj_weight, r.xp),
        net.local(r.dt_weight, r.wdt),
        net.local(r.conv_weight, r.cw),
        net.local(r.a_log, r.al),
        net.local(r.lens, r.row_l),
        net.local(r.conv_bias, r.row_cb),
        net.local(r.dt_bias, r.row_db),
        net.local(r.skip, r.row_sk),
    ]
    pl.semaphore_wait(bar, len(greet))

    rows_of = lambda ref, f, n: ref.at[pl.ds(f * n, n)]
    same_core = [lax.rem(mf + 2 * k, F) for k in range(1, F // 2)]
    other_chip = [(lax.rem(mf + 2 * k, F), lax.rem(core + 2 * k, F)) for k in range(1, F // 2)]

    for i in (1, 10):
        own[i].wait()
    as_row = lambda ref: ref[...].astype(F32).reshape(1, ref.shape[-1])
    r.pg_own[0:1, :] = as_row(r.row_g)
    r.pg_own[1:2, 0 : d.clusters] = as_row(r.row_l)
    r.pg[mf] = r.pg_own[...]

    def spread_rows(src, dst):
        direct = [net.send(src, rows_of(dst, mf, tok), ms, f) for f in same_core]
        beside = [net.send(src, rows_of(dst, mf, tok), ms, core)]
        return direct, beside

    def relay_rows(dst, direct, beside):
        for k, c in enumerate(direct):
            c.wait()
            f = lax.rem(mf + F - 2 * (k + 1), F)
            beside.append(net.send(rows_of(dst, f, tok), rows_of(dst, f, tok), ms, core))

    def w_slice(g, f):
        return r.in_weight.at[:, pl.ds(pl.multiple_of(g * d.DI + f * CL, LN), CL)]

    quart, ring = lax.rem(ms, 4), ms - lax.rem(ms, 4)
    QF = DF // 4

    def w_far(g):
        out = []
        for pair in other_chip:
            for f in pair:
                src = r.in_weight.at[
                    pl.ds(quart * QF, QF), pl.ds(pl.multiple_of(g * d.DI + f * CL, LN), CL)
                ]
                out.append(net.send(src, r.w.at[g, pl.ds(mf * DF + quart * QF, QF)], ms, f))
        return out

    def w_relay(g, far):
        out = []
        i = 0
        for k in range(1, F // 2):
            for flip in (0, 1):
                far[i].wait_recv()
                i += 1
                f0 = lax.rem(mf + F - 2 * k, F)
                if flip:
                    f0 = f0 + 1 - 2 * lax.rem(f0, 2)
                place = r.w.at[g, pl.ds(f0 * DF + quart * QF, QF)]
                for t in (1, 2, 3):
                    out.append(net.send(place, place, ring + lax.rem(quart + t, 4), mf))
        return out

    wx_far = w_far(0)
    pgs = [net.send(r.pg_own, r.pg.at[mf], *net.at(0, k)) for k in range(1, F)]
    w_beside = [net.send(w_slice(g, core), r.w.at[g, pl.ds(mf * DF, DF)], ms, core) for g in (0, 1)]
    for c in wx_far:
        c.wait_send()
    h_direct, h_beside = spread_rows(r.hidden, r.hid)
    halo = [
        net.send(
            r.hidden.at[pl.ds(tok - TAIL, TAIL)],
            r.hid.at[pl.ds(T + mf * TAIL, TAIL)],
            *net.at(1, k),
        )
        for k in range(F)
    ]
    wx_near = w_relay(0, wx_far)
    for c in pgs + own[:1]:
        c.wait()
    for f in range(F):
        r.gain[0:1, f * DF : (f + 1) * DF] = r.pg[f, 0:1, :]
    sub = lax.broadcasted_iota(jnp.int32, (V, LN), 0)
    hidx = lax.rem(sub, H)
    stream = lax.div(sub, H)
    offs, run = [], jnp.zeros((V, LN), F32)
    for j in range(d.clusters - 1):
        for f in range(F):
            run = run + jnp.where(stream == f, r.pg[f, 1:2, j : j + 1], 0.0)
        offs.append(run)
    base = ms * tok + hidx * Q
    r.rel[0 : HG * V, :] = jnp.zeros((HG * V, LN), F32)
    r.rel[HG * V + T :, :] = jnp.zeros((HG * V, LN), F32)

    def mark(q, _):
        pos = (base + q).astype(F32)
        last = jnp.zeros((V, LN), F32)
        for o in offs:
            last = jnp.maximum(last, jnp.where(o <= pos, o, 0.0))
        r.rel[pl.ds(pl.multiple_of((q + HG) * V, V), V), :] = jnp.where(pos == 0.0, 0.5, pos - last)
        return 0

    lax.fori_loop(0, Q, mark, 0)
    for c in own[8:]:
        c.wait()
    r.cp[0 : d.K, :] = r.cw[...].astype(F32)
    for i, ref in enumerate((r.row_cb, r.row_db, r.row_sk)):
        r.cp[4 + i : 5 + i, :] = as_row(ref)
    r.dec[...] = -LOG2E * jnp.exp(r.al[...].astype(F32))
    for c in h_direct:
        c.wait_send()
    c_direct, c_beside = spread_rows(r.cotangent, r.cot)
    wg_far = w_far(1)
    for k, c in enumerate(h_direct):
        c.wait_recv()
        f = lax.rem(mf + F - 2 * (k + 1), F)
        h_beside.append(net.send(rows_of(r.hid, f, tok), rows_of(r.hid, f, tok), ms, core))
    perm = to_scan(d, HG)

    def rms(first, count):
        def body(i, _):
            rows = pl.ds(pl.multiple_of(first + i * 64, 64), 64)
            h = r.hid[rows, :].astype(F32)
            inv = lax.rsqrt(jnp.mean(h * h, axis=-1, keepdims=True) + EPS)
            r.normed[rows, :] = (h * inv * r.gain[...]).astype(BF16)
            return 0

        lax.fori_loop(0, count // 64, body, 0)

    for k in range(F // 2):
        rms(lax.rem(mf + F - 2 * k, F) * tok, tok)
    for k, c in enumerate(h_beside):
        c.wait()
        rms(lax.rem(core + F - 2 * k, F) * tok, tok)
    for c in halo:
        c.wait()
    rms(T, F * TAIL)
    for c in range(0, D, 256):
        r.big[:, c : c + 256] = dot(perm, r.normed[:, c : c + 256]).astype(BF16)
    own[2].wait()
    w_beside[0].wait()
    for c in wx_near:
        c.wait()
    for c in range(0, CL, 256):
        r.xb[:, c : c + 256] = (
            dot(r.big[:, :], r.w[0, :, c : c + 256]).astype(BF16).astype(F32)
        )

    def conv(i, _):
        r0 = pl.multiple_of(i * 64, 64)
        rows = pl.ds(r0, 64)
        age = r.rel[pl.ds(pl.multiple_of(r0 + HG * V, V), 64), :]
        for j in range(NB):
            acc = jnp.zeros((64, LN), F32) + r.cp[4:5, lane(j)]
            for k in range(d.K):
                back = d.K - 1 - k
                xs = r.xb[pl.ds(pl.multiple_of(r0 + (HG - back) * V, V), 64), lane(j)]
                acc = acc + jnp.where(age >= back, xs * r.cp[k : k + 1, lane(j)], 0.0)
            r.pre[rows, lane(j)] = acc
            r.inp[rows, lane(j)] = (acc * sigmoid(acc)).astype(BF16)
        return 0

    own[6].wait()
    W = d.R + 2 * N
    bands = [pl.ds(0, T // 2), pl.ds(T // 2, T // 2)]
    beside = lambda src, dst, band: net.send(src.at[band], dst.at[band], ms, core)
    xd_near = []
    for i, band in enumerate(bands):
        lax.fori_loop(i * T // 128, (i + 1) * T // 128, conv, 0)
        r.xd[band, 0:W] = dot(r.inp[band, :], r.xp[...], 1, 1).astype(BF16)
        if i == 0:
            xd_near.append(beside(r.xd, r.xdn, band))
    xd_near.append(beside(r.xd, r.xdn, bands[1]))

    def chips(src, near_copy, near, far, band):
        near_copy.wait()
        rows = src.at[band]
        rows[...] = (rows[...].astype(F32) + near[band, :].astype(F32)).astype(BF16)
        return net.batch(
            [(rows, far.at[k - 1, band], *net.at(0, 2 * k)) for k in range(1, F // 2)],
            far.at[:, band],
        )

    def chips_total(src, batches, far):
        for c in batches:
            c.wait()
        tot = src[:, 0:W].astype(F32)
        for k in range(F // 2 - 1):
            tot = tot + far[k, :, 0:W].astype(F32)
        return tot

    xd_far = [chips(r.xd, c, r.xdn, r.xdr, band) for c, band in zip(xd_near, bands)]
    relay_rows(r.cot, c_direct, c_beside)
    wg_near = w_relay(1, wg_far)
    perm = to_scan(d, 0)
    for c in [own[4], own[5]] + c_beside:
        c.wait()
    for c in range(0, D, 256):
        r.cot[:, c : c + 256] = dot(perm, r.cot[:, c : c + 256]).astype(BF16)
    for c in range(0, CL, 256):
        r.gg[0:T, c : c + 256] = dot(r.cot[...], r.ow[c : c + 256, :], 1, 1)
    xd = chips_total(r.xd, xd_far, r.xdr)
    own[7].wait()
    low = xd[:, : d.R].astype(BF16)
    r.xd[:, 0 : d.R] = low
    for c in range(0, CL, 256):
        r.dtpre[:, c : c + 256] = dot(low, r.wdt[:, c : c + 256])

    def steps(i, acc):
        rows = pl.ds(pl.multiple_of(i * 64, 64), 64)
        age = r.rel[pl.ds(pl.multiple_of(i * 64 + HG * V, V), 64), :]
        out = []
        for j in range(NB):
            z = r.dtpre[rows, lane(j)] + r.cp[5:6, lane(j)]
            dt = jnp.maximum(z, 0.0) + jnp.log1p(jnp.exp(-jnp.abs(z)))
            r.dtpre[rows, lane(j)] = z
            e = jnp.where(age == 0.0, RESET, dt)
            r.dtd[rows, lane(j)] = e
            r.u[rows, lane(j)] = dt * r.inp[rows, lane(j)].astype(F32)
            out.append(acc[j] + jnp.sum(e.reshape(8, V, LN), axis=0))
        return tuple(out)

    sums = lax.fori_loop(0, T // 64, steps, tuple(jnp.zeros((V, LN), F32) for _ in range(NB)))
    for j in range(NB):
        whole, t = sums[j], 1
        while t < H:
            low_half = lax.rem(lax.div(hidx, t), 2) == 0
            whole = whole + jnp.where(low_half, pltpu.roll(whole, V - t, 0), pltpu.roll(whole, t, 0))
            t *= 2
        r.sd[0:V, lane(j)] = sums[j]
        r.tot[:, lane(j)] = whole
    tots = net.batch([(r.tot, r.totr.at[k - 1], *net.at(k, 0)) for k in range(1, S)], r.totr)
    bc = xd[:, d.R : W]
    hi = bc.astype(BF16)
    rest = (bc - hi.astype(F32)).astype(BF16)
    both = jnp.concatenate([hi, rest], axis=1)
    for n in range(0, 2 * N, 4):
        row = lax.rem(lax.broadcasted_iota(jnp.int32, (4 * N, 4 * LN), 0), 2 * N)
        col = lax.div(lax.broadcasted_iota(jnp.int32, (4 * N, 4 * LN), 1), LN) + n
        pick = jnp.where(row == col, 1.0, 0.0).astype(BF16)
        r.bcb[:, n * LN : (n + 4) * LN] = dot(both, pick).astype(r.bcb.dtype)

    half = N // 2
    row_n = lambda n: slice(n * V, (n + 1) * V)
    dec_of = lambda n, j: jnp.broadcast_to(r.dec[n : n + 1, lane(j)], (V, LN))

    def state_scan(j):
        dn = [dec_of(n, j) for n in range(N)]

        def ahead(q, hs):
            hs = list(hs)
            rows = pl.ds(pl.multiple_of(q * 2 * V, 2 * V), 2 * V)
            t, w = r.dtd[rows, lane(j)], r.u[rows, lane(j)]
            for n in range(N):
                b = r.bcb[rows, lane(n)].astype(F32)
                for p in (TOP, BOT):
                    hs[n] = jnp.exp2(t[p] * dn[n]) * hs[n] + w[p] * b[p]
            return tuple(hs)

        hs = lax.fori_loop(0, Q // 2, ahead, tuple(jnp.zeros((V, LN), F32) for _ in range(N)))
        for n in range(N):
            r.ends[0, row_n(n), lane(j)] = hs[n]

    def adjoint_scan(j):
        dn = [dec_of(n, j) for n in range(N)]

        def behind(q, gs):
            gs = list(gs)
            rows = pl.ds(pl.multiple_of((Q - 2 - 2 * q) * V, 2 * V), 2 * V)
            t, g0 = r.dtd[rows, lane(j)], r.gy[rows, lane(j)]
            for n in range(N):
                c = r.bcb[rows, lane(N + n)].astype(F32)
                for p in (BOT, TOP):
                    gs[n] = jnp.exp2(t[p] * dn[n]) * (gs[n] + g0[p] * c[p])
            return tuple(gs)

        gs = lax.fori_loop(0, Q // 2, behind, tuple(jnp.zeros((V, LN), F32) for _ in range(N)))
        for n in range(N):
            r.ends[1, row_n(n), lane(j)] = gs[n]

    def piece_ends(j, way):
        one = r.sd[0:V, lane(j)]
        tiles = []
        for n0 in range(0, N, H):
            a = jnp.zeros((V, LN), F32)
            for t in range(H):
                fac = jnp.exp2(one * dec_of(n0 + t, j))
                e = r.ends[way, row_n(n0 + t), lane(j)]
                x = e
                for h in range(1, H):
                    at = H - 1 - h if way else h
                    x = jnp.where(hidx == at, fac * pltpu.roll(x, V - 1 if way else 1, 0) + e, x)
                a = jnp.where(hidx == t, turn(x, t if way else t - (H - 1)), a)
            tiles.append(a)
        for i in range(0, len(tiles), 2):
            band = slice(i * V, (i + 2) * V)
            r.epack[way, j, band, :] = jnp.concatenate(tiles[i : i + 2], axis=0).astype(BF16)
        for k in range(1, S):
            ps, pf = net.at(k, 0)
            copy = net.remote(r.epack.at[way, j], r.eget.at[j, k - 1], *state_sems[j], ps, pf)
            pl.when(ps < ms if way else ps > ms)(copy.start)

    def turn(x, by):
        return x if by % V == 0 else pltpu.roll(x, by % V, 0)

    def begin(j, copies):
        copies.wait_send()
        copies.wait_recv()
        tiles = N // H
        dn = []
        for i in range(tiles):
            x = dec_of(i * H, j)
            for t in range(1, H):
                x = jnp.where(hidx == t, dec_of(i * H + t, j), x)
            dn.append(x)

        def join(p, acc):
            slot = lax.rem(ms + S - p, S) - 1
            tot = r.totr[slot, :, lane(j)]
            e = r.eget[j, slot].astype(F32)
            return tuple(jnp.exp2(tot * dn[i]) * acc[i] + e[row_n(i)] for i in range(tiles))

        zero = tuple(jnp.zeros((V, LN), F32) for _ in range(tiles))
        fw = lax.fori_loop(0, ms, join, zero)
        bw = lax.fori_loop(0, S - 1 - ms, lambda i, acc: join(S - 1 - i, acc), zero)
        one = r.sd[0:V, lane(j)]
        for i in range(tiles):
            for t in range(H):
                n = i * H + t
                fac = jnp.exp2(one * dec_of(n, j))
                x, y = turn(fw[i], -t), turn(bw[i], H - 1 - t)
                for h in range(1, H):
                    xn = pltpu.roll(fac * x + r.ends[0, row_n(n), lane(j)], 1, 0)
                    yn = pltpu.roll(fac * y + r.ends[1, row_n(n), lane(j)], V - 1, 0)
                    x = jnp.where(hidx == h, xn, x)
                    y = jnp.where(hidx == H - 1 - h, yn, y)
                r.start[0, row_n(n), lane(j)] = x
                r.start[1, row_n(n), lane(j)] = y

    def forward(j):
        dn = [dec_of(n, j) for n in range(N)]

        def ahead(q, hs):
            hs = list(hs)
            rows = pl.ds(pl.multiple_of(q * 2 * V, 2 * V), 2 * V)
            t, w = r.dtd[rows, lane(j)], r.u[rows, lane(j)]
            y = [jnp.zeros((V, LN), F32), jnp.zeros((V, LN), F32)]
            for n in range(N):
                b = r.bcb[rows, lane(n)].astype(F32)
                c = r.bcb[rows, lane(N + n)].astype(F32)
                keep = []
                for k, p in enumerate((TOP, BOT)):
                    m = jnp.exp2(t[p] * dn[n]) * hs[n]
                    hs[n] = m + w[p] * b[p]
                    y[k] = y[k] + c[p] * hs[n]
                    keep.append(m)
                r.m_s[j, rows, lane(n)] = jnp.concatenate(keep, axis=0).astype(BF16)
            r.y_s[rows, lane(j)] = jnp.concatenate(y, axis=0)
            return tuple(hs)

        lax.fori_loop(0, Q // 2, ahead, tuple(r.start[0, row_n(n), lane(j)] for n in range(N)))

    def backward(j):
        for n0 in range(0, N, half):
            dn = [dec_of(n, j) for n in range(n0, n0 + half)]

            def behind(i, carry, n0=n0, dn=dn):
                gs, gd = list(carry[0]), list(carry[1])
                rows = pl.ds(pl.multiple_of((Q - 2 - 2 * i) * V, 2 * V), 2 * V)
                t, w, g0 = r.dtd[rows, lane(j)], r.u[rows, lane(j)], r.gy[rows, lane(j)]
                t0 = jnp.where(t == RESET, 0.0, t)
                gu = [jnp.zeros((V, LN), F32), jnp.zeros((V, LN), F32)]
                gt = [jnp.zeros((V, LN), F32), jnp.zeros((V, LN), F32)]
                for i in range(half):
                    n = n0 + i
                    b = r.bcb[rows, lane(n)].astype(F32)
                    c = r.bcb[rows, lane(N + n)].astype(F32)
                    m = r.m_s[j, rows, lane(n)].astype(F32)
                    pc = g0 * (m + w * b)
                    pb = [None, None]
                    gc = g0 * c
                    for k, p in ((1, BOT), (0, TOP)):
                        g = gs[i] + gc[p]
                        pb[k] = g * w[p]
                        gu[k] = gu[k] + g * b[p]
                        x = g * m[p]
                        gt[k] = gt[k] + x * dn[i]
                        gd[i] = gd[i] + x * t0[p]
                        gs[i] = jnp.exp2(t[p] * dn[i]) * g
                    pb = jnp.concatenate(pb, axis=0)
                    if j > 0:
                        pb = pb + r.x_s[rows, lane(n)].astype(F32)
                        pc = pc + r.x_s[rows, lane(N + n)].astype(F32)
                    r.x_s[rows, lane(n)] = pb.astype(r.x_s.dtype)
                    r.x_s[rows, lane(N + n)] = pc.astype(r.x_s.dtype)
                gu, gt = jnp.concatenate(gu, axis=0), jnp.concatenate(gt, axis=0)
                if n0 > 0:
                    gu = gu + r.gsc[rows, lane(j)]
                    gt = gt + r.y_s[rows, lane(j)]
                r.gsc[rows, lane(j)] = gu
                r.y_s[rows, lane(j)] = gt
                return tuple(gs), tuple(gd)

            zero = tuple(jnp.zeros((V, LN), F32) for _ in range(half))
            first = tuple(r.start[1, row_n(n), lane(j)] for n in range(n0, n0 + half))
            _, gd = lax.fori_loop(0, Q // 2, behind, (first, zero))
            for i in range(half):
                dec = r.dec[n0 + i : n0 + i + 1, lane(j)] * (1.0 / LOG2E)
                r.rowsum[8 + n0 + i : 9 + n0 + i, lane(j)] = (
                    jnp.sum(gd[i], axis=0, keepdims=True) * dec
                )

    def gating(j):
        def body(i, sk):
            rows = pl.ds(pl.multiple_of(i * 64, 64), 64)
            x = r.inp[rows, lane(j)].astype(F32)
            mixed = r.y_s[rows, lane(j)] + r.cp[6:7, lane(j)] * x
            g = r.gate[rows, lane(j)]
            s = sigmoid(g)
            r.gated[rows, lane(j)] = (mixed * (g * s)).astype(BF16)
            r.ggate[rows, lane(j)] = (
                r.gg[rows, lane(j)] * mixed * s * (1.0 + g * (1.0 - s))
            ).astype(BF16)
            p = r.gy[rows, lane(j)] * x
            return sk + jnp.sum(p.reshape(8, V, LN), axis=0)

        sk = lax.fori_loop(0, T // 64, body, jnp.zeros((V, LN), F32))
        r.rowsum[6:7, lane(j)] = jnp.sum(sk, axis=0, keepdims=True)

    def put(dst, first, res):
        n = dst.shape[1]
        for t in range(res.shape[0] // n):
            dst[first // n + t] = res[t * n : (t + 1) * n].astype(dst.dtype)

    def put_split(dst, first, res):
        n = dst.shape[2]
        for t in range(res.shape[0] // n):
            s, f = divmod(first // n + t, F)
            dst[s, f] = res[t * n : (t + 1) * n].astype(dst.dtype)

    levels = list(range(S.bit_length() - 1))
    orders = (levels, [1, 0] + levels[2:])

    def start_sum(name, out, t, spread):
        parts = getattr(r, name + t), getattr(r, name + t + "n"), getattr(r, out + t)
        return Scatter(net, *parts, orders["ab".index(t)], spread)

    def sum_pair(name, out, spread):
        return [start_sum(name, out, t, spread) for t in "ab"]

    def both_halves(putter, name, first, res):
        n = getattr(r, name + "a").shape[-1]
        putter(getattr(r, name + "a"), first, res[:, :n])
        putter(getattr(r, name + "b"), first, res[:, n:])

    def step(sums, count=S - 2):
        for _ in range(count):
            for one in sums:
                one.step(1)

    back0 = from_scan(d, 0)
    cut = r.giwga.shape[-1]

    def gate_grads(t, cols):
        r.gatn[:, cols] = dot(back0, r.ggate[0:T, cols]).astype(BF16)
        for c in range(0, D, 256):
            res = dot(r.normed[0:T, c : c + 256], r.gatn[:, cols], 0, 0)
            put_split(getattr(r, "giwg" + t), c, res)
        return start_sum("giwg", "o_wg", t, True)

    r.rowsum[...] = jnp.zeros_like(r.rowsum)
    state_sems = [net.pair() for _ in range(NB)]
    states = [
        net.remote(r.eget.at[j], r.eget.at[j], *state_sems[j], *net.at(0, 1)) for j in range(NB)
    ]
    for j in range(NB):
        state_scan(j)
        piece_ends(j, 0)
    for c in [own[3], w_beside[1]] + wg_near:
        c.wait()
    for c in range(0, CL, 256):
        r.gate[:, c : c + 256] = dot(r.big[HG * V :, :], r.w[1, :, c : c + 256])

    def gys(i, _):
        rows = pl.ds(pl.multiple_of(i * 64, 64), 64)
        for j in range(NB):
            g = r.gate[rows, lane(j)]
            r.gy[rows, lane(j)] = r.gg[rows, lane(j)] * (g * sigmoid(g))
        return 0

    lax.fori_loop(0, T // 64, gys, 0)
    for j in range(NB):
        adjoint_scan(j)
        piece_ends(j, 1)
    tots.wait()
    for j in range(NB):
        begin(j, states[j])
        forward(j)
        gating(j)
        if (j + 1) * LN == cut:
            sum_g = [gate_grads("a", slice(0, cut))]
    level = S // 2

    sum_g.append(gate_grads("b", slice(cut, CL)))
    for c in range(0, CL, 256):
        both_halves(put, "gow", c, dot(r.gated[0:T, c : c + 256], r.cot[...], 0, 0))
    r.gated[0:T, :] = dot(back0, r.gated[0:T, :]).astype(BF16)
    for c in range(0, D, 256):
        r.cot[:, c : c + 256] = dot(r.gated[0:T, :], r.ow[:, c : c + 256]).astype(BF16)
    outs = Rows(net, core, r.cot, r.hid, r.outr)
    for j in range(NB):
        backward(j)
        if j == 0:
            outs.cross()
            sum_o = sum_pair("gow", "o_out", False)
        if j == 1:
            step(sum_g, level)
    step(sum_g, S - 2 - level)
    step(sum_o, level)
    def finish(i, acc):
        rows = pl.ds(pl.multiple_of(i * 64, 64), 64)
        out = []
        for j in range(NB):
            x = r.inp[rows, lane(j)].astype(F32)
            z = r.dtpre[rows, lane(j)]
            gu = r.gsc[rows, lane(j)]
            gt = r.y_s[rows, lane(j)] * (1.0 / LOG2E) + gu * x
            e = jnp.exp(-jnp.abs(z))
            dt = jnp.maximum(z, 0.0) + jnp.log1p(e)
            gz = gt * (jnp.where(z >= 0.0, 1.0, e) / (1.0 + e))
            r.ggate[rows, lane(j)] = gz.astype(BF16)
            r.gsc[rows, lane(j)] = gu * dt + r.gy[rows, lane(j)] * r.cp[6:7, lane(j)]
            out.append(acc[j] + jnp.sum(gz.reshape(8, V, LN), axis=0))
        return tuple(out)

    db = lax.fori_loop(0, T // 64, finish, tuple(jnp.zeros((V, LN), F32) for _ in range(NB)))
    for j in range(NB):
        r.rowsum[5:6, lane(j)] = jnp.sum(db[j], axis=0, keepdims=True)
    gx_near = []
    for band in bands:
        r.gx[band, 0 : d.R] = dot(r.ggate[band, :], r.wdt[...], 1, 1).astype(BF16)
        acc = jnp.zeros((T // 2, 2 * N), F32)
        for n in range(0, 2 * N, 4):
            row = lax.div(lax.broadcasted_iota(jnp.int32, (4 * LN, 2 * N), 0), LN) + n
            col = lax.broadcasted_iota(jnp.int32, (4 * LN, 2 * N), 1)
            pick = jnp.where(row == col, 1.0, 0.0).astype(BF16)
            acc = acc + dot(r.x_s[band, n * LN : (n + 4) * LN].astype(BF16), pick)
        r.gx[band, d.R : W] = acc.astype(BF16)
        gx_near.append(beside(r.gx, r.gxn, band))
    gx_far = [chips(r.gx, c, r.gxn, r.gxr, band) for c, band in zip(gx_near, bands)]
    gwdt = dot(r.ggate[0:T, :], r.xd[:, 0 : d.R], 0, 0)

    gxd = chips_total(r.gx, gx_far, r.gxr).astype(BF16)
    step(sum_o, S - 2 - level)
    pad = HG * V
    r.gg[0:pad, :] = jnp.zeros((pad, CL), F32)
    r.gg[pad + T :, :] = jnp.zeros((pad, CL), F32)
    for c in range(0, CL, 256):
        r.gg[pad : pad + T, c : c + 256] = r.gsc[:, c : c + 256] + dot(gxd, r.xp[:, c : c + 256])

    def act(i, acc):
        r0 = pl.multiple_of(i * 64, 64)
        rows = pl.ds(r0, 64)
        shift = pl.ds(pl.multiple_of(r0 + pad, V), 64)
        age = r.rel[shift, :]
        out = []
        for j in range(NB):
            p = r.pre[rows, lane(j)]
            q = sigmoid(p)
            g = r.gg[shift, lane(j)] * q * (1.0 + p * (1.0 - q))
            r.gg[shift, lane(j)] = g
            a = list(acc[j])
            a[4] = a[4] + jnp.sum(g.reshape(8, V, LN), axis=0)
            for k in range(d.K):
                back = d.K - 1 - k
                xs = r.xb[pl.ds(pl.multiple_of(r0 + (HG - back) * V, V), 64), lane(j)]
                t = jnp.where(age >= back, g * xs, 0.0)
                a[k] = a[k] + jnp.sum(t.reshape(8, V, LN), axis=0)
            out.append(tuple(a))
        return tuple(out)

    zero = tuple(tuple(jnp.zeros((V, LN), F32) for _ in range(5)) for _ in range(NB))
    acc = lax.fori_loop(0, T // 64, act, zero)
    for j in range(NB):
        for k in range(5):
            r.rowsum[k : k + 1, lane(j)] = jnp.sum(acc[j][k], axis=0, keepdims=True)

    def gather_taps(i, _):
        r0 = pl.multiple_of(i * 32, 32)
        for j in range(NB):
            acc = jnp.zeros((32, LN), F32)
            for k in range(d.K):
                back = d.K - 1 - k
                src = pl.ds(pl.multiple_of(r0 + back * V, V), 32)
                acc = acc + jnp.where(
                    r.rel[src, :] >= back, r.gg[src, lane(j)] * r.cp[k : k + 1, lane(j)], 0.0
                )
            r.gated[pl.ds(r0, 32), lane(j)] = acc.astype(BF16)
        return 0

    lax.fori_loop(0, d.TE // 32, gather_taps, 0)
    r.ggate[...] = dot(from_scan(d, HG), r.gated[...]).astype(BF16)
    sum_x, first = [], 0
    for t in "ab":
        part = getattr(r, "giwx" + t)
        cols = slice(first, first + part.shape[-1])
        first = cols.stop
        for c in range(0, D, 256):
            put_split(part, c, dot(r.normed[:, c : c + 256], r.ggate[:, cols], 0, 0))
        sum_x.append(start_sum("giwx", "o_wx", t, True))
    r.y_s[0:CL, 0:LN] = r.rowsum[...].T
    r.y_s[0:CL, LN : LN + W] = dot(r.inp[...], gxd, 0, 0)
    r.y_s[0:CL, LN + W : 2 * LN] = jnp.zeros((CL, LN - W), F32)
    r.y_s[0:CL, 32 : 32 + d.R] = gwdt
    put(r.small, 0, r.y_s[0:CL, 0 : 2 * LN])
    sum_s = Scatter(net, r.small, r.small_n, r.o_small, orders[1], False)
    for c in range(0, D, 256):
        g = dot(r.ggate[...], r.w[0, c : c + 256, :], 1, 1)
        r.hid[0:T, c : c + 256] = (
            g[0:T] + dot(r.gatn[...], r.w[1, c : c + 256, :], 1, 1)
        ).astype(BF16)
        r.hid[T:, c : c + 256] = g[T:].astype(BF16)
    def gains(i, acc):
        rows = pl.ds(pl.multiple_of(i * 64, 64), 64)
        t = r.hid[rows, :].astype(F32) * r.normed[rows, :].astype(F32)
        return acc + jnp.sum(t.reshape(8, V, D), axis=0)

    gtot = lax.fori_loop(0, d.NAT // 64, gains, jnp.zeros((V, D), F32)) / r.gain[...]
    gtot = jnp.sum(gtot, axis=0, keepdims=True)
    n = D // S
    for s in range(S):
        r.gg8[s] = gtot[:, s * n : (s + 1) * n]
    gns = Rows(net, core, r.hid, r.m_s.at[0, :, pl.ds(0, D)], r.o_gn)
    halo_rows = lambda f: r.hid.at[pl.ds(T + f * TAIL, TAIL)]
    halo_near = net.batch(
        [
            (halo_rows(lax.rem(core + 2 * k, F)), r.halo_n.at[k], ms, core)
            for k in range(F // 2)
        ],
        r.halo_n,
    )

    def halo_cross():
        halo_near.wait()
        out = []
        for k in range(F // 2):
            f = lax.rem(mf + 2 * k, F)
            here = halo_rows(f)
            here[...] = (here[...].astype(F32) + r.halo_n[k].astype(F32)).astype(BF16)
            out.append((here, r.o_gnh.at[k], lax.rem(ms + S - 1, S), f))
        net.batch(out, r.o_gnh)

    step(sum_x, 2)
    gns.cross()
    halo_cross()
    step([sum_s], 2)

    i, j = net.pair()

    def gain_copy(k):
        ps, pf = lax.rem(ms + lax.div(k, F), S), lax.rem(mf + lax.rem(k, F), F)
        return net.remote(r.gg8.at[ps], r.o_gain.at[k], i, j, ps, pf)

    def gain_send(k, _):
        gain_copy(k).start()
        return 0

    lax.fori_loop(1, S * F, gain_send, 0)
    net.local(r.gg8.at[ms], r.o_gain.at[0])
    others = r.o_gain.at[pl.ds(1, S * F - 1)]
    gain_all = net.remote(others, others, i, j, *net.at(0, 1))
    step(sum_x + [sum_s])
    gain_all.wait_send()
    gain_all.wait_recv()
    net.drain()
    assert (net.s_used, net.r_used) == semaphores(d), (net.s_used, net.r_used)


def close(d, gn, gnh, outr, hid, cot, gain, wxa, wxb, wga, wgb, outa, outb, small, ggain,
          o_out, o_hid, o_gain, o_in, o_conv, o_cb, o_db, o_sk, o_xp, o_dt, o_al, o_gout):
    F, T, tok, D = d.F, d.T, d.tok, d.D
    W = d.R + 2 * d.N

    def rows_(i, _):
        rows = pl.ds(pl.multiple_of(i * 16, 16), 16)
        h = hid[rows, :].astype(F32)
        g, o = jnp.zeros((16, D), F32), jnp.zeros((16, D), F32)
        for k in range(gn.shape[0]):
            g = g + gn[k, rows, :].astype(F32)
            o = o + outr[k, rows, :].astype(F32)
        late = jnp.zeros((TAIL, D), F32)
        for k in range(gnh.shape[0]):
            late = late + gnh[k].astype(F32)
        g = g + jnp.where(i == tok // 16 - 1, late, 0.0)
        inv = lax.rsqrt(jnp.mean(h * h, axis=-1, keepdims=True) + EPS)
        g2 = g * gain[...]
        mean = jnp.mean(g2 * h, axis=-1, keepdims=True)
        o_hid[0, rows, :] = cot[rows, :].astype(F32) + inv * g2 - h * (inv * inv * inv) * mean
        o_out[0, rows, :] = (h + o).astype(BF16)
        return 0

    lax.fori_loop(0, tok // 16, rows_, 0)
    for f in range(F):
        at = f * d.CL
        for part in (wxa, wxb, wga, wgb):
            n = part.shape[-1]
            at = d.DI + f * d.CL if part is wga else at
            o_in[:, at : at + n] = part[0, f].astype(F32) + part[1, f].astype(F32)
            at += n
    o_gout[:, : D // 2] = outa[0].astype(F32) + outa[1].astype(F32)
    o_gout[:, D // 2 :] = outb[0].astype(F32) + outb[1].astype(F32)
    sm = jnp.sum(small[...].astype(F32), axis=0)
    first = sm[:, 0:LN].T
    for i, o_row in enumerate((o_cb, o_db, o_sk)):
        o_row[...] = first[4 + i : 5 + i, :]
    o_conv[...] = first[0 : d.K, :]
    o_al[...] = first[V : V + d.N, :]
    o_dt[...] = sm[:, 32 : 32 + d.R]
    o_xp[...] = sm[:, LN : LN + W]
    tot = jnp.sum(ggain[...], axis=0)
    n, k = D // d.S, D // d.S // F
    row = lax.broadcasted_iota(jnp.int32, (n, k), 0) - lax.axis_index("fsdp") * k
    pick = jnp.where(row == lax.broadcasted_iota(jnp.int32, (n, k), 1), 1.0, 0.0)
    one = lax.dot_general(
        tot + jnp.zeros((V, n), F32), pick, (((1,), (0,)), ((), ())),
        precision=lax.Precision.HIGHEST, preferred_element_type=F32,
    )
    o_gain[...] = one[0:1, :]


def semaphores(d):
    far = d.F // 2 - 1
    one = (d.F - 1) + 2 * (2 * far + 1) + d.F + 2 * (2 * far) + 2 + 2 * (6 * far) + 2 * (2 * far + 1) + 2
    one += 2 * 4 + 1 + d.NB + 1
    return one + 7 * d.S, one + 7 * (d.S - 1) + 17


def vm(*shape, dtype=F32):
    return pltpu.VMEM(shape, dtype)


def per_device(
    d, hidden, cluster_lengths, norm_gain, in_weight, conv_weight, conv_bias, xproj_weight,
    dt_weight, dt_bias, a_log, skip, out_weight, cotangent,
):
    S, F, T, D, CL, N, NB, R = d.S, d.F, d.T, d.D, d.CL, d.N, d.NB, d.R
    ins = dict(
        hidden=hidden[0], lens=cluster_lengths, norm_gain=norm_gain, conv_bias=conv_bias,
        dt_bias=dt_bias, skip=skip, in_weight=in_weight, conv_weight=conv_weight.T,
        xproj_weight=xproj_weight.T, dt_weight=dt_weight.T, a_log=a_log.T, out_weight=out_weight,
        cotangent=cotangent[0],
    )
    DS, CS, W, W2 = D // S, CL // S, R + 2 * N, 2 * LN
    TP = T + 2 * HG * V
    rt = BF16 if CS >= 16 else F32
    half, most = CL // 2, CL // LN * 3 // 4 * LN or CL // 2
    two = lambda name, shape, t: {name + k: (shape, t) for k in "ab"}
    outs = dict(
        o_gn=((F // 2 + 1, d.tok, D), BF16), o_gnh=((F // 2, TAIL, D), BF16),
        outr=((F // 2 + 1, d.tok, D), BF16), gain=((1, D), F32),
        o_wxa=((2, F, DS // F, most), BF16), o_wxb=((2, F, DS // F, CL - most), BF16),
        **two("o_wg", (2, F, DS // F, half), BF16),
        **two("o_out", (2, CS, D // 2), rt), o_small=((2, CS, W2), rt), o_gain=((S * F, 1, DS), F32),
    )
    small_t = T <= 512
    EP = N // d.H * V
    scratch = dict(
        hid=((d.NAT, D), BF16), normed=((d.NAT, D), BF16), big=((d.TE, D), BF16),
        cot=((T, D), BF16), w=((2, D, CL), BF16), ow=((CL, D), BF16),
        xp=((W, CL), BF16), wdt=((R, CL), BF16), cw=((d.K, CL), BF16), al=((N, CL), BF16),
        row_cb=((CL,), BF16), row_db=((CL,), BF16), row_sk=((CL,), BF16), row_g=((D // F,), BF16),
        row_l=((1, d.clusters), jnp.int32), pg=((F, V, D // F), F32), pg_own=((V, D // F), F32), cp=((V, CL), F32), dec=((N, CL), F32), rel=((TP, LN), F32),
        xb=((d.TE, CL), F32), gate=((T, CL), F32), pre=((T, CL), F32), inp=((T, CL), BF16),
        xd=((T, LN), BF16), xdn=((T, LN), BF16), xdr=((F // 2 - 1, T, LN), BF16),
        dtpre=((T, CL), F32), dtd=((T, CL), F32), u=((T, CL), F32), gg=((TP, CL), F32),
        gy=((T, CL), F32), bcb=((T, 2 * N * LN), F32 if small_t else BF16),
        sd=((V, CL), F32), tot=((V, CL), F32), totr=((S - 1, V, CL), F32),
        ends=((2, N * V, CL), F32), epack=((2, NB, EP, LN), BF16), eget=((NB, S - 1, EP, LN), BF16),
        start=((2, N * V, CL), F32), m_s=((NB, T, N * LN), BF16), y_s=((T, CL), F32),
        gsc=((T, CL), F32), x_s=((T, 2 * N * LN), F32 if small_t else BF16),
        gated=((d.TE, CL), BF16), ggate=((d.NAT, CL), BF16), gatn=((T, CL), BF16),
        gx=((T, LN), BF16), gxn=((T, LN), BF16), gxr=((F // 2 - 1, T, LN), BF16), rowsum=((LN, CL), F32), halo_n=((F // 2, TAIL, D), BF16),

        small=((S, CS, W2), rt), small_n=((S - 2, CS, W2), rt),
        gg8=((S, 1, DS), F32),
    )
    for name, wide in (("giwg", half), ("giwx", most)):
        for t, n in (("a", wide), ("b", CL - wide)):
            scratch[name + t] = ((S, F, DS // F, n), BF16)
            scratch[name + t + "n"] = ((S - 2, F, DS // F, n), BF16)
    for t in "ab":
        scratch["gow" + t] = ((S, CS, D // 2), rt)
        scratch["gow" + t + "n"] = ((S - 2, CS, D // 2), rt)
    names = list(ins) + list(outs) + list(scratch) + ["ssem", "rsem"]
    sends, gets = semaphores(d)
    res = pl.pallas_call(
        functools.partial(layer, d, names),
        out_shape=[jax.ShapeDtypeStruct(*o) for o in outs.values()],
        in_specs=[pl.BlockSpec(memory_space=pl.ANY)] * len(ins),
        out_specs=[
            pl.BlockSpec(memory_space=pltpu.VMEM if k == "gain" else pl.ANY) for k in outs
        ],
        scratch_shapes=[vm(*s, dtype=t) for s, t in scratch.values()]
        + [pltpu.SemaphoreType.DMA((sends,)), pltpu.SemaphoreType.DMA((gets,))],
        compiler_params=pltpu.CompilerParams(
            collective_id=0, has_side_effects=True, vmem_limit_bytes=65250 * 1024
        ),
    )(*ins.values())
    o = dict(zip(outs, res))
    fin = kernel(
        functools.partial(close, d),
        (o["o_gn"], o["o_gnh"], o["outr"], hidden[0], cotangent[0], o["gain"])
        + tuple(o[k] for k in ("o_wxa", "o_wxb", "o_wga", "o_wgb", "o_outa", "o_outb", "o_small", "o_gain")),
        [((1, d.tok, D), BF16), ((1, d.tok, D), F32), ((1, DS // F), F32), ((DS // F, 2 * d.DI), F32),
         ((d.K, CS), F32), ((1, CS), F32), ((1, CS), F32), ((1, CS), F32), ((CS, W), F32), ((CS, R), F32),
         ((N, CS), F32), ((CS, D), F32)],
    )
    out, g_hid, g_gain, g_in, g_conv, g_cb, g_db, g_sk, g_xp, g_dt, g_al, g_out = fin
    return (
        out, g_hid, g_gain[0], g_in, g_conv.T, g_cb[0], g_xp, g_dt, g_db[0], g_al.T, g_sk[0], g_out,
    )


def solution(mesh):
    S, F = mesh.shape["seq"], mesh.shape["fsdp"]

    def run(*args):
        tok, D = args[0].shape[1] // S, args[0].shape[2]
        d = Dims(
            S, F, tok, D, args[11].shape[0], args[9].shape[1], args[7].shape[1], args[4].shape[1],
            args[1].shape[1],
        )
        return jax.shard_map(
            functools.partial(per_device, d),
            mesh=mesh,
            in_specs=(
                P("fsdp", "seq", None), P("fsdp", None), P("fsdp"), P("fsdp", None),
                P("fsdp", None), P("fsdp"), P("fsdp", None), P("fsdp", None), P("fsdp"),
                P("fsdp", None), P("fsdp"), P("fsdp", None), P("fsdp", "seq", None),
            ),
            out_specs=(
                P("fsdp", "seq", None), P("fsdp", "seq", None), P(("seq", "fsdp")),
                P(("seq", "fsdp"), None), P(("seq", "fsdp"), None), P(("seq", "fsdp")),
                P(("seq", "fsdp"), None), P(("seq", "fsdp"), None), P(("seq", "fsdp")),
                P(("seq", "fsdp"), None), P(("seq", "fsdp")), P(("seq", "fsdp"), None),
            ),
            check_vma=False,
        )(*args)

    return run
```
